128 devices in a mesh: set: 2 (over z_lo), tx: 16 (over x, y), ty: 4 (over z_hi, core).
Axes of the slice: x: 4, y: 4, z: 4 (z_hi: 2, z_lo: 2; z = z_hi * 2 + z_lo), core: 2. Of those that a mesh axis runs over, the one named last changes fastest.
Arguments:
- tracers: float32 [32, 16, 64, 4096], P('set', None, 'ty', 'tx'), may hold values from 0 to 2
- thickness: float32 [16, 64, 4096], P('set', 'ty', 'tx'), may hold values from 0.6 to 1.4
- velocity: float32 [2, 16, 64, 4096], P(None, 'set', 'ty', 'tx'), may hold values from -0.5 to 0.5
- diffusivity: float32 [16, 64, 4096], P(None, 'ty', 'tx'), may hold values from 0.05 to 5
- reaction: float32 [4, 8, 8], P('set'), may hold values from -2 to 2
- land_mask: int32 [64, 4096], P('ty', 'tx'), may hold values 0 or 1
- level_count: int32 [64, 4096], P('ty', 'tx'), may hold values from 1 to 16
Outputs:
- tracers_out: float32 [32, 16, 64, 4096], P('set', None, 'ty', 'tx')
- thickness_out: float32 [16, 64, 4096], P('set', 'ty', 'tx')
- velocity_out: float32 [2, 16, 64, 4096], P(None, 'set', 'ty', 'tx')
The draws below stay inside these ranges and needn't reach their ends.
All inputs are finite; a program needn't handle non-finite values. No bound on the sum of `land_mask` on one device may be relied on, other than what follows from the above.
Results may differ from the reference program's by a relative error of at most 0.00025.
Values sent between devices are 32-bit elements; how exact they have to be, the bound alone decides.
No kernel may reach another device: no remote copies, remote signals or barrier semaphores. Data moves between devices by JAX's collectives and lax.ppermute only.
A program may use at most 128 MiB of HBM per device.

```python
import math
import jax
import jax.numpy as jnp
from jax import lax

SETS = 4
TPS = 8
NTR = 32
NZ = 16
ITERS = 4
NY = 64
NX = 4096


def plant(entries, own_key, least, top_value):
    shape = entries.shape
    place = [jax.random.randint(jax.random.fold_in(own_key, axis), (), 0, shape[axis]) for axis in range(len(shape))]
    entries = entries.at[tuple(place)].set(least)
    longest = shape.index(max(shape))
    place[longest] = (place[longest] + 1) % shape[longest]
    return entries.at[tuple(place)].set(top_value)


def block_scale(own_key, extent, split, smallest, high):
    factor_of = 1.0
    for position, blocks in split:
        draws = jax.random.uniform(jax.random.fold_in(jax.random.fold_in(own_key, 6), position), (blocks,), jnp.float32, smallest / len(split), high / len(split))
        factor_of = factor_of * jnp.repeat(jnp.exp(draws), extent[position] // blocks).reshape((-1,) + (1,) * (len(extent) - 1 - position))
    return factor_of


def scatter_about(key, dims, scale, most, shards=(), kind=jnp.bfloat16):
    gain = block_scale(key, dims, shards, -0.22, 0.18) if shards else 1.0
    values = jax.random.normal(key, dims, jnp.float32) * scale * gain
    return jnp.minimum(jnp.maximum(values, -most), most).astype(kind)


def setup_inputs(seed: int = 0) -> dict:
    key_list = jax.random.split(jax.random.key(seed), 8)
    return {
        "tracers": jnp.clip(2.0 * jax.random.uniform(key_list[0], (NTR, NZ, NY, NX), jnp.float32) ** block_scale(key_list[0], (NTR, NZ, NY, NX), ((0, 2), (2, 4), (3, 16)), -0.2, 0.2), 0.0, 2.0),
        "thickness": jnp.clip(0.6 + 0.79999995 * jax.random.uniform(key_list[1], (NZ, NY, NX), jnp.float32) ** block_scale(key_list[1], (NZ, NY, NX), ((0, 2), (1, 4), (2, 16)), -0.2, 0.2), 0.6, 1.4),
        "velocity": scatter_about(key_list[2], (2, NZ, NY, NX), 0.2, 0.5, ((1, 2), (2, 4), (3, 16)), jnp.float32),
        "diffusivity": jnp.clip(jnp.exp(math.log(5.0) - 4.6051702 * jax.random.uniform(key_list[3], (NZ, NY, NX), jnp.float32) ** block_scale(key_list[3], (NZ, NY, NX), ((1, 4), (2, 16)), -0.2, 0.2)), 0.05, 5.0),
        "reaction": scatter_about(key_list[4], (SETS, TPS, TPS), 0.5, 2.0, ((0, 2),), jnp.float32),
        "land_mask": plant((jax.random.randint(key_list[5], (NY, NX), 0, 5) < 4).astype(jnp.int32), jax.random.fold_in(key_list[5], 1), 0, 1),
        "level_count": plant(jax.random.randint(key_list[6], (NY, NX), 1, NZ + 1), jax.random.fold_in(key_list[6], 1), 1, NZ).astype(jnp.int32),
    }


TIME_STEP = 0.2
GRAVITY = 1.0
ROTATION = 0.5


def padded_field(field):
    wrapped = jnp.concatenate([field[..., -1:], field, field[..., :1]], axis=-1)
    border = jnp.zeros_like(wrapped[..., :1, :])
    return jnp.concatenate([border, wrapped, border], axis=-2)


def divergence(flux_pad):
    zonal = flux_pad[0, :, 1:-1, 1:-1] - flux_pad[0, :, 1:-1, :-2]
    meridional = flux_pad[1, :, 1:-1, 1:-1] - flux_pad[1, :, :-2, 1:-1]
    return zonal + meridional


def momentum_fluxes(thick_pad, velocity, mask_pad, coriolis):
    center = thick_pad[:, 1:-1, 1:-1]
    east_side = thick_pad[:, 1:-1, 2:]
    north_side = thick_pad[:, 2:, 1:-1]
    wet_here = mask_pad[:, 1:-1, 1:-1]
    east_wet = wet_here * mask_pad[:, 1:-1, 2:]
    north_wet = wet_here * mask_pad[:, 2:, 1:-1]
    eastward = east_wet * (velocity[0] + TIME_STEP * (coriolis * velocity[1] - GRAVITY * (east_side - center)))
    northward = north_wet * (velocity[1] - TIME_STEP * (coriolis * velocity[0] + GRAVITY * (north_side - center)))
    fluxes = jnp.stack([eastward * 0.5 * (center + east_side), northward * 0.5 * (center + north_side)])
    return jnp.stack([eastward, northward]), fluxes


def column_mix(content, thick_new, link):
    levels = content.shape[1]
    upper_link = jnp.zeros_like(link[0])
    prev_ratio = jnp.zeros_like(link[0])
    prev_solved = jnp.zeros_like(content[:, 0])
    ratios = []
    solved = []
    for level in range(levels):
        below = link[level]
        recip = 1.0 / (thick_new[level] + upper_link + below - upper_link * prev_ratio)
        prev_ratio = below * recip
        prev_solved = (content[:, level] + upper_link * prev_solved) * recip
        ratios.append(prev_ratio)
        solved.append(prev_solved)
        upper_link = below
    result = [None] * levels
    result[levels - 1] = solved[levels - 1]
    for level in range(levels - 2, -1, -1):
        result[level] = solved[level] + ratios[level] * result[level + 1]
    return jnp.stack(result, axis=1)


def tracer_update(conc_pad, flux_pad, thickness, mask_pad, diffusivity, reaction):
    east_flux = flux_pad[0, :, 1:-1, 1:-1]
    west_flux = flux_pad[0, :, 1:-1, :-2]
    north_flux = flux_pad[1, :, 1:-1, 1:-1]
    south_flux = flux_pad[1, :, :-2, 1:-1]
    center = conc_pad[..., 1:-1, 1:-1]
    east_conc = conc_pad[..., 1:-1, 2:]
    west_conc = conc_pad[..., 1:-1, :-2]
    north_conc = conc_pad[..., 2:, 1:-1]
    south_conc = conc_pad[..., :-2, 1:-1]
    flux_east = jnp.maximum(east_flux, 0.0) * center + jnp.minimum(east_flux, 0.0) * east_conc
    flux_west = jnp.maximum(west_flux, 0.0) * west_conc + jnp.minimum(west_flux, 0.0) * center
    flux_north = jnp.maximum(north_flux, 0.0) * center + jnp.minimum(north_flux, 0.0) * north_conc
    flux_south = jnp.maximum(south_flux, 0.0) * south_conc + jnp.minimum(south_flux, 0.0) * center
    thick_new = thickness - TIME_STEP * divergence(flux_pad)
    content = thickness * center - TIME_STEP * ((flux_east - flux_west) + (flux_north - flux_south))
    wet_here = mask_pad[:, 1:-1, 1:-1]
    wet_below = jnp.concatenate([wet_here[1:], jnp.zeros_like(wet_here[:1])], axis=0)
    link = TIME_STEP * diffusivity * wet_here * wet_below
    mixed = column_mix(content, thick_new, link)
    groups = reaction.shape[0]
    per_group = reaction.shape[1]
    shaped = mixed.reshape((groups, per_group) + mixed.shape[1:])
    reacted = shaped + TIME_STEP * jnp.einsum("sab,sbzyx->sazyx", reaction, shaped, precision=lax.Precision.HIGHEST)
    return reacted.reshape(mixed.shape) * wet_here


def reference(tracers, thickness, velocity, diffusivity, reaction, land_mask, level_count):
    level_index = jnp.arange(NZ, dtype=jnp.int32)[:, None, None]
    wet_cells = ((level_index < level_count[None]) & (land_mask[None] == 1)).astype(jnp.float32)
    mask_pad = padded_field(wet_cells)
    row_index = jnp.arange(NY, dtype=jnp.int32)
    coriolis = (ROTATION * (2.0 * (row_index.astype(jnp.float32) + 0.5) / NY - 1.0))[:, None]
    concentration = tracers
    thick_now = thickness
    veloc_now = velocity
    for iteration in range(ITERS):
        thick_pad = padded_field(thick_now)
        veloc_next, fluxes = momentum_fluxes(thick_pad, veloc_now, mask_pad, coriolis)
        flux_pad = padded_field(fluxes)
        concentration = tracer_update(padded_field(concentration), flux_pad, thick_now, mask_pad, diffusivity, reaction)
        thick_now = thick_now - TIME_STEP * divergence(flux_pad)
        veloc_now = veloc_next
    return concentration, thick_now, veloc_now
```

```python
import jax
import jax.numpy as jnp
from jax import lax
from jax.experimental import pallas as pl
from jax.experimental.pallas import tpu as pltpu
from jax.sharding import PartitionSpec as P

ITERS = 4
DT = 0.2
G = 1.0
ROTATION = 0.5
LV = 16
NT = 16
PER = 8
VMEM_LIMIT = 60 * 1024 * 1024
F32 = jnp.float32
ANY = pl.BlockSpec(memory_space=pl.ANY)
SMEM = pl.BlockSpec(memory_space=pltpu.SMEM)
VMEM = pl.BlockSpec(memory_space=pltpu.VMEM)


def sub_iota(rows=8):
    return lax.broadcasted_iota(jnp.int32, (rows, 128), 0)


def lane_iota(rows=8):
    return lax.broadcasted_iota(jnp.int32, (rows, 128), 1)


def from_east(tiles):
    rolled = [pltpu.roll(x, 127, 1) for x in tiles]
    lane = lane_iota(tiles[0].shape[0])
    last = len(tiles) - 1
    return [rolled[i] if i == last else jnp.where(lane == 127, rolled[i + 1], rolled[i]) for i in range(last + 1)]


def from_west(tiles):
    rolled = [pltpu.roll(x, 1, 1) for x in tiles]
    lane = lane_iota(tiles[0].shape[0])
    return [rolled[i] if i == 0 else jnp.where(lane == 0, rolled[i - 1], rolled[i]) for i in range(len(tiles))]


def coriolis_of(row, rows_total):
    return ROTATION * (2.0 * (row.astype(F32) + 0.5) / rows_total - 1.0)


def level_step(k, h_s, h_c, h_n, u_s, u_c, v_s, v_c, deep, cor_c, cor_s, diff, up, prev):
    d_c, d_e, d_n, d_s = deep
    h_e = from_east(h_c)
    count = len(h_c)
    u_new, v_new, u_flux, v_flux, s_flux = [], [], [], [], []
    for j in range(count):
        un = jnp.where(k < d_e[j], u_c[j] + DT * (cor_c * v_c[j] - G * (h_e[j] - h_c[j])), 0.0)
        vn = jnp.where(k < d_n[j], v_c[j] - DT * (cor_c * u_c[j] + G * (h_n[j] - h_c[j])), 0.0)
        vs = jnp.where(k < d_s[j], v_s[j] - DT * (cor_s * u_s[j] + G * (h_c[j] - h_s[j])), 0.0)
        u_new.append(un)
        v_new.append(vn)
        u_flux.append(un * 0.5 * (h_c[j] + h_e[j]))
        v_flux.append(vn * 0.5 * (h_c[j] + h_n[j]))
        s_flux.append(vs * 0.5 * (h_s[j] + h_c[j]))
    w_flux = from_west(u_flux)
    h_new, coefs, links, ratios = [], [], [], []
    for j in range(count):
        fe, fw, fn, fs = u_flux[j], w_flux[j], v_flux[j], s_flux[j]
        hn = h_c[j] - DT * ((fe - fw) + (fn - fs))
        link = jnp.where(k + 1 < d_c[j], DT * diff[j], 0.0)
        q = jnp.where(k < d_c[j], 1.0 / (hn + up[j] + link - up[j] * prev[j]), 0.0)
        r = link * q
        dq = DT * q
        ce = dq * jnp.maximum(-fe, 0.0)
        cw = dq * jnp.maximum(fw, 0.0)
        cn = dq * jnp.maximum(-fn, 0.0)
        cs = dq * jnp.maximum(fs, 0.0)
        out = (jnp.maximum(fe, 0.0) - jnp.minimum(fw, 0.0)) + (jnp.maximum(fn, 0.0) - jnp.minimum(fs, 0.0))
        ca = q * h_c[j] - dq * out
        h_new.append(hn)
        links.append(link)
        ratios.append(r)
        coefs.append((ca, ce, cw, cn, cs, up[j] * q, r))
    return h_new, u_new, v_new, coefs, links, ratios


def forward(k, coefs, cells, before):
    result = []
    for t, (c, s, n) in enumerate(cells):
        e = from_east(c)
        w = from_west(c)
        result.append([
            ((coefs[0][j] * c[j] + coefs[1][j] * e[j]) + (coefs[2][j] * w[j] + coefs[3][j] * n[j]))
            + (coefs[4][j] * s[j] + coefs[5][j] * before[t][j])
            for j in range(len(c))
        ])
    return result


def react(table, s, m):
    outs = []
    for a in range(PER):
        acc = None
        for b in range(PER):
            w = table[s * 64 + a * 8 + b]
            term = [w * x for x in m[b]]
            acc = term if acc is None else [p + q for p, q in zip(acc, term)]
        outs.append(acc)
    return outs


def fill_table(react_ref, table):
    for s in range(2):
        for a in range(PER):
            for b in range(PER):
                v = DT * react_ref[s, a, b] + (1.0 if a == b else 0.0)
                table[s * 64 + a * 8 + b] = jnp.full((8, 128), v, F32)


def zeros_like_tiles(rows, count):
    return [jnp.zeros((rows, 128), F32) for _ in range(count)]


def own_copies(tr, ho, hp, vo, vp, df, off, c_buf, h_buf, u_buf, v_buf, d_buf, sem):
    copies = []
    part = LV // 2
    other = part - off
    for j in range(2):
        lanes = pl.ds(128 * j, 128)
        rows = pl.ds(8, 16)
        copies.append(pltpu.make_async_copy(ho.at[:, :, lanes], h_buf.at[pl.ds(off, part), j, rows, :], sem.at[0 + j]))
        copies.append(pltpu.make_async_copy(hp.at[:, :, lanes], h_buf.at[pl.ds(other, part), j, rows, :], sem.at[2 + j]))
        copies.append(pltpu.make_async_copy(vo.at[0, :, :, lanes], u_buf.at[pl.ds(off, part), j, rows, :], sem.at[4 + j]))
        copies.append(pltpu.make_async_copy(vp.at[0, :, :, lanes], u_buf.at[pl.ds(other, part), j, rows, :], sem.at[6 + j]))
        copies.append(pltpu.make_async_copy(vo.at[1, :, :, lanes], v_buf.at[pl.ds(off, part), j, rows, :], sem.at[8 + j]))
        copies.append(pltpu.make_async_copy(vp.at[1, :, :, lanes], v_buf.at[pl.ds(other, part), j, rows, :], sem.at[10 + j]))
        copies.append(pltpu.make_async_copy(df.at[:, :, lanes], d_buf.at[:, j, rows, :], sem.at[12 + j]))
    tracer = []
    for s in range(2):
        for j in range(2):
            tracer.append(pltpu.make_async_copy(
                tr.at[pl.ds(8 * s, 8), :, :, pl.ds(128 * j, 128)],
                c_buf.at[pl.ds(8 * s, 8), :, j, pl.ds(8, 16), :], sem.at[14 + 2 * s + j]))
    return copies, tracer


OWN_SCRATCH = [
    pltpu.VMEM((NT, LV, 2, 32, 128), F32),
    pltpu.VMEM((LV, 2, 32, 128), F32),
    pltpu.VMEM((LV, 2, 32, 128), F32),
    pltpu.VMEM((LV, 2, 32, 128), F32),
    pltpu.VMEM((LV, 2, 32, 128), F32),
    pltpu.VMEM((2, 32, 128), jnp.int32),
    pltpu.SemaphoreType.DMA((18,)),
]


def fill_depth(land, level, p_buf):
    for j in range(2):
        lanes = slice(128 * j, 128 * j + 128)
        p_buf[j, 8:24, :] = jnp.where(land[:, lanes] == 1, level[:, lanes], 0)


def rows_kernel(scal, tr, ho, hp, vo, vp, df, land, level, y_up, y_dn, c_buf, h_buf, u_buf, v_buf, d_buf, p_buf, sem):
    off = scal[0] * (LV // 2)
    fields, tracer = own_copies(tr, ho, hp, vo, vp, df, off, c_buf, h_buf, u_buf, v_buf, d_buf, sem)
    for c in fields + tracer:
        c.start()
    fill_depth(land, level, p_buf)
    for c in fields + tracer:
        c.wait()
    low = sub_iota() < 4

    def put(index, j, first, second):
        y_up[index, j] = jnp.where(low, first(20), second(16))
        y_dn[index, j] = jnp.where(low, first(8), second(4))

    @pl.loop(0, LV)
    def _(k):
        for j in range(2):
            for t in range(PER):
                put(t * LV + k, j, lambda r: c_buf[t, k, j, r:r + 8, :], lambda r: c_buf[t + PER, k, j, r:r + 8, :])
            put(128 + k, j, lambda r: h_buf[k, j, r:r + 8, :], lambda r: u_buf[k, j, r:r + 8, :])
            put(144 + k, j, lambda r: v_buf[k, j, r:r + 8, :], lambda r: d_buf[k, j, r:r + 8, :])

    for j in range(2):
        get = lambda r: p_buf[j, r:r + 8, :].astype(F32)
        put(160, j, get, get)


def inner_kernel(rows_total, scal, tr, ho, hp, vo, vp, df, land, level, reaction, saved, saved_f, mid, mid_f,
                 c_buf, h_buf, u_buf, v_buf, d_buf, p_buf, sem, c_alt, solved, coef, table):
    off = scal[0] * (LV // 2)
    fields, tracer = own_copies(tr, ho, hp, vo, vp, df, off, c_buf, h_buf, u_buf, v_buf, d_buf, sem)
    for c in fields + tracer:
        c.start()
    fill_depth(land, level, p_buf)
    fill_table(reaction, table)
    six = sub_iota() < 6
    rows = lax.broadcasted_iota(jnp.int32, (16, 128), 0) + scal[1]
    cor_c = coriolis_of(rows, rows_total)
    cor_s = coriolis_of(rows - 1, rows_total)
    d_c = [p_buf[j, 8:24, :] for j in range(2)]
    d_e = [jnp.minimum(a, b) for a, b in zip(d_c, from_east(d_c))]
    d_n = [jnp.minimum(d_c[j], p_buf[j, 9:25, :]) for j in range(2)]
    d_s = [jnp.minimum(d_c[j], p_buf[j, 7:23, :]) for j in range(2)]
    for c in fields:
        c.wait()

    def keep(n, read):
        return jnp.where(six, read(4 + n), read(16 - n))

    def keep_fields(n):
        @pl.loop(0, LV)
        def _(k):
            for f, buf in enumerate((h_buf, u_buf, v_buf)):
                for j in range(2):
                    saved_f[n, f, k, j] = keep(n, lambda r: buf[k, j, r:r + 8, :])

    def keep_tracers(n, buf):
        @pl.loop(0, LV)
        def _(k):
            for t in range(NT):
                for j in range(2):
                    saved[n, t, k, j] = keep(n, lambda r: buf[t, k, j, r:r + 8, :])

    keep_fields(0)
    for c in tracer:
        c.wait()
    keep_tracers(0, c_buf)
    for n in range(1, ITERS + 1):
        src, dst = (c_buf, c_alt) if n % 2 else (c_alt, c_buf)

        def dynamics(k, carry):
            up, prev = carry
            read = lambda buf, r: [buf[k, j, r:r + 16, :] for j in range(2)]
            h_new, u_new, v_new, co, links, ratios = level_step(
                k, read(h_buf, 7), read(h_buf, 8), read(h_buf, 9), read(u_buf, 7), read(u_buf, 8),
                read(v_buf, 7), read(v_buf, 8), (d_c, d_e, d_n, d_s), cor_c, cor_s, read(d_buf, 8), up, prev)
            for j in range(2):
                h_buf[k, j, 8:24, :] = h_new[j]
                u_buf[k, j, 8:24, :] = u_new[j]
                v_buf[k, j, 8:24, :] = v_new[j]
                for c in range(7):
                    coef[c, k, j] = co[j][c]
            return links, ratios

        lax.fori_loop(0, LV, dynamics, (zeros_like_tiles(16, 2), zeros_like_tiles(16, 2)))
        if n < ITERS:
            keep_fields(n)
        else:
            @pl.loop(0, LV)
            def _(k):
                for f, buf in enumerate((h_buf, u_buf, v_buf)):
                    for j in range(2):
                        mid_f[f, k, j] = buf[k, j, 12:20, :]

        for r0 in ((8, 16) if n < ITERS else (12,)):
            @pl.loop(0, 2)
            def _(s):
                def down(k, before):
                    co = [[coef[c, k, j, r0 - 8:r0, :] for j in range(2)] for c in range(6)]
                    read = lambda t, r: [src[s * PER + t, k, j, r:r + 8, :] for j in range(2)]
                    now = forward(k, co, [(read(t, r0), read(t, r0 - 1), read(t, r0 + 1)) for t in range(PER)], before)
                    for t in range(PER):
                        for j in range(2):
                            solved[k, t, j] = now[t][j]
                    return now

                lax.fori_loop(0, LV, down, [zeros_like_tiles(8, 2) for _ in range(PER)])

                def upward(i, m):
                    k = LV - 1 - i
                    r = [coef[6, k, j, r0 - 8:r0, :] for j in range(2)]
                    m = [[solved[k, t, j] + r[j] * m[t][j] for j in range(2)] for t in range(PER)]
                    outs = react(table, s, m)
                    for t in range(PER):
                        for j in range(2):
                            if n < ITERS:
                                dst[s * PER + t, k, j, r0:r0 + 8, :] = outs[t][j]
                            else:
                                mid[s * PER + t, k, j] = outs[t][j]
                    return m

                lax.fori_loop(0, LV, upward, [zeros_like_tiles(8, 2) for _ in range(PER)])
        if n < ITERS:
            keep_tracers(n, dst)


def strip_pack_kernel(scal, tr, ho, hp, vo, vp, df, land, level, y_s, y_n, o_ref, x_r, x_l,
                      c_buf, h_buf, u_buf, v_buf, d_buf, p_buf, sem):
    off = scal[0] * (LV // 2)
    fields, tracer = own_copies(tr, ho, hp, vo, vp, df, off, c_buf, h_buf, u_buf, v_buf, d_buf, sem)
    for c in fields + tracer:
        c.start()
    fill_depth(land, level, p_buf)
    for c in fields + tracer:
        c.wait()
    low = sub_iota() < 4
    lane = lane_iota()
    place = lane & 31
    slot = lane >> 5

    def three(read, index, half, j):
        ys, yn = y_s[index, j], y_n[index, j]
        if half == 0:
            yn = pltpu.roll(yn, 4, 0)
        else:
            ys = pltpu.roll(ys, 4, 0)
        return [jnp.where(low, ys, read(4)), read(12), jnp.where(low, read(20), yn)]

    def pack(sources):
        acc = [None] * 3
        for q, (read, index, half) in enumerate(sources):
            left = three(lambda r: read(0, r), index, half, 0)
            right = three(lambda r: read(1, r), index, half, 1)
            for i in range(3):
                a = pltpu.roll(left[i], (4 + 32 * q) % 128, 1)
                b = pltpu.roll(right[i], (28 + 32 * q) % 128, 1)
                x = jnp.where(place < 16, a, b)
                acc[i] = x if acc[i] is None else jnp.where(slot == q, x, acc[i])
        return acc

    @pl.loop(0, LV)
    def _(k):
        def tracer_source(t):
            return (lambda j, r: c_buf[t, k, j, r:r + 8, :], (t % PER) * LV + k, t // PER)

        groups = [[tracer_source(4 * g + q) for q in range(4)] for g in range(4)]
        groups.append([
            (lambda j, r: h_buf[k, j, r:r + 8, :], 128 + k, 0), (lambda j, r: u_buf[k, j, r:r + 8, :], 128 + k, 1),
            (lambda j, r: v_buf[k, j, r:r + 8, :], 144 + k, 0), (lambda j, r: d_buf[k, j, r:r + 8, :], 144 + k, 1)])
        xr, xl = [jnp.zeros((8, 128), F32)] * 3, [jnp.zeros((8, 128), F32)] * 3
        for g in range(5):
            packed = pack(groups[g])
            here = (place >= 4 * g) & (place < 4 * g + 4)
            for i in range(3):
                o_ref[k, g, 8 * i:8 * i + 8, :] = packed[i]
                xr[i] = jnp.where(here, pltpu.roll(packed[i], (4 * g - 24) % 128, 1), xr[i])
                xl[i] = jnp.where(here, pltpu.roll(packed[i], (4 * g - 4) % 128, 1), xl[i])
        for i in range(3):
            x_r[k, 8 * i:8 * i + 8, :] = xr[i]
            x_l[k, 8 * i:8 * i + 8, :] = xl[i]

    packed = pack([(lambda j, r: p_buf[j, r:r + 8, :].astype(F32), 160, 0)] * 4)
    for i in range(3):
        for g in range(5):
            o_ref[LV, g, 8 * i:8 * i + 8, :] = packed[i]
        x_r[LV, 8 * i:8 * i + 8, :] = pltpu.roll(packed[i], (16 - 24) % 128, 1)
        x_l[LV, 8 * i:8 * i + 8, :] = pltpu.roll(packed[i], (16 - 4) % 128, 1)


def edge_kernel(rows_total, scal, saved, saved_f, y_s, y_n, df, land, level, reaction, out_c, out_f,
                c_buf, f_buf, d_buf, p_buf, solved, coef, table, sem):
    copies = []
    for n in range(ITERS):
        copies.append(pltpu.make_async_copy(saved_f.at[n], f_buf.at[n, :, :, :, pl.ds(0, 8), :], sem.at[n]))
    for j in range(2):
        copies.append(pltpu.make_async_copy(df.at[:, :, pl.ds(128 * j, 128)], d_buf.at[:, j, pl.ds(8, 16), :], sem.at[4 + j]))
    tracer = [pltpu.make_async_copy(saved.at[n], c_buf.at[n, :, :, :, pl.ds(0, 8), :], sem.at[6 + n]) for n in range(ITERS)]
    for c in copies + tracer:
        c.start()
    fill_table(reaction, table)
    fill_depth(land, level, p_buf)
    sub = sub_iota()
    low = sub < 4
    for c in copies:
        c.wait()
    tracer[0].wait()

    def put(ref, y, half, south):
        if half != (0 if south else 1):
            y = pltpu.roll(y, 4, 0)
        if south:
            pltpu.store(ref.at[pl.ds(0, 8), :], y, mask=low)
        else:
            pltpu.store(ref.at[pl.ds(4, 8), :], y, mask=jnp.logical_not(low))

    @pl.loop(0, LV)
    def _(k):
        for j in range(2):
            for t in range(PER):
                ys, yn = y_s[t * LV + k, j], y_n[t * LV + k, j]
                for half in range(2):
                    put(c_buf.at[0, t + PER * half, k, j], ys, half, True)
                    put(c_buf.at[0, t + PER * half, k, j], yn, half, False)
            for f, (index, half) in enumerate(((128, 0), (128, 1), (144, 0))):
                put(f_buf.at[0, f, k, j], y_s[index + k, j], half, True)
                put(f_buf.at[0, f, k, j], y_n[index + k, j], half, False)
            ys, yn = y_s[144 + k, j], y_n[144 + k, j]
            pltpu.store(d_buf.at[k, j, pl.ds(0, 8), :], ys, mask=jnp.logical_not(low))
            pltpu.store(d_buf.at[k, j, pl.ds(24, 8), :], pltpu.roll(yn, 4, 0), mask=low)

    for j in range(2):
        ys, yn = y_s[160, j].astype(jnp.int32), y_n[160, j].astype(jnp.int32)
        pltpu.store(p_buf.at[j, pl.ds(0, 8), :], ys, mask=jnp.logical_not(low))
        pltpu.store(p_buf.at[j, pl.ds(24, 8), :], yn, mask=low)

    def gather(read, shift):
        return jnp.where(low, read(shift), read(shift + 2))

    for n in range(1, ITERS + 1):
        if n < ITERS:
            tracer[n].wait()

        def at(buf, j, shift):
            return jnp.where(low, buf[j, 4 + n + shift:12 + n + shift, :], buf[j, 20 - n + shift:28 - n + shift, :])

        row = jnp.where(low, sub - 4 + n, sub + 12 - n) + scal[1]
        cor_c = coriolis_of(row, rows_total)
        cor_s = coriolis_of(row - 1, rows_total)
        d_c = [at(p_buf, j, 0) for j in range(2)]
        d_e = [jnp.minimum(a, b) for a, b in zip(d_c, from_east(d_c))]
        d_n = [jnp.minimum(d_c[j], at(p_buf, j, 1)) for j in range(2)]
        d_s = [jnp.minimum(d_c[j], at(p_buf, j, -1)) for j in range(2)]

        def dynamics(k, carry):
            up, prev = carry
            read = lambda f, shift: [gather(lambda r: f_buf[n - 1, f, k, j, r:r + 8, :], shift) for j in range(2)]
            diff = [at(d_buf.at[k], j, 0) for j in range(2)]
            h_new, u_new, v_new, co, links, ratios = level_step(
                k, read(0, 0), read(0, 1), read(0, 2), read(1, 0), read(1, 1), read(2, 0), read(2, 1),
                (d_c, d_e, d_n, d_s), cor_c, cor_s, diff, up, prev)
            for j in range(2):
                for f, x in enumerate((h_new[j], u_new[j], v_new[j])):
                    if n < ITERS:
                        pltpu.store(f_buf.at[n, f, k, j, pl.ds(0, 8), :], x, mask=low)
                        pltpu.store(f_buf.at[n, f, k, j, pl.ds(4, 8), :], x, mask=jnp.logical_not(low))
                    else:
                        out_f[f, k, j] = x
                for c in range(7):
                    coef[c, k, j] = co[j][c]
            return links, ratios

        lax.fori_loop(0, LV, dynamics, (zeros_like_tiles(8, 2), zeros_like_tiles(8, 2)))

        @pl.loop(0, 2)
        def _(s):
            def down(k, before):
                co = [[coef[c, k, j] for j in range(2)] for c in range(6)]

                def read(t, shift):
                    return [gather(lambda r: c_buf[n - 1, s * PER + t, k, j, r:r + 8, :], shift) for j in range(2)]

                now = forward(k, co, [(read(t, 1), read(t, 0), read(t, 2)) for t in range(PER)], before)
                for t in range(PER):
                    for j in range(2):
                        solved[k, t, j] = now[t][j]
                return now

            lax.fori_loop(0, LV, down, [zeros_like_tiles(8, 2) for _ in range(PER)])

            def upward(i, m):
                k = LV - 1 - i
                r = [coef[6, k, j] for j in range(2)]
                m = [[solved[k, t, j] + r[j] * m[t][j] for j in range(2)] for t in range(PER)]
                outs = react(table, s, m)
                for t in range(PER):
                    for j in range(2):
                        if n < ITERS:
                            pltpu.store(c_buf.at[n, s * PER + t, k, j, pl.ds(0, 8), :], outs[t][j], mask=low)
                            pltpu.store(c_buf.at[n, s * PER + t, k, j, pl.ds(4, 8), :], outs[t][j], mask=jnp.logical_not(low))
                        else:
                            out_c[s * PER + t, k, j] = outs[t][j]
                return m

            lax.fori_loop(0, LV, upward, [zeros_like_tiles(8, 2) for _ in range(PER)])


def strip_kernel(rows_total, scal, o_ref, x_r, x_l, reaction, mid, mid_f, edge, edge_f, out_c, out_h, out_v,
                 c_buf, c_alt, h_buf, u_buf, v_buf, d_buf, p_buf, solved, coef, table):
    lane = lane_iota()
    place = lane & 31
    slot = lane >> 5
    low = sub_iota() < 4
    for s in range(2):
        for go in range(2):
            for gi in range(2):
                for rho in range(4):
                    v = jnp.zeros((8, 128), F32)
                    for q in range(4):
                        a, b = 4 * go + q, 4 * gi + (q - rho) % 4
                        w = DT * reaction[s, a, b] + (1.0 if a == b else 0.0)
                        v = jnp.where(slot == q, jnp.full((8, 128), w, F32), v)
                    table[((s * 2 + go) * 2 + gi) * 4 + rho] = v

    def whole(k, g, i, xg):
        rows = slice(8 * i, 8 * i + 8)
        a = pltpu.roll(x_r[k, rows, :], (-4 * xg) % 128, 1)
        b = pltpu.roll(x_l[k, rows, :], (28 - 4 * xg) % 128, 1)
        return jnp.where(place < 4, a, jnp.where(place >= 28, b, o_ref[k, g, rows, :]))

    @pl.loop(0, LV)
    def _(k):
        for i in range(3):
            for g in range(4):
                c_buf[g, k, 8 + 8 * i:16 + 8 * i, :] = whole(k, g, i, g)
            x = whole(k, 4, i, 4)
            for f, buf in enumerate((h_buf, u_buf, v_buf, d_buf)):
                y = jnp.where(lane < 32, pltpu.roll(x, (-32 * f) % 128, 1), 0.0)
                y = y + pltpu.roll(y, 32, 1)
                y = y + pltpu.roll(y, 64, 1)
                buf[k, 8 + 8 * i:16 + 8 * i, :] = y

    for i in range(3):
        p_buf[8 + 8 * i:16 + 8 * i, :] = whole(LV, 4, i, 4).astype(jnp.int32)

    rows = lax.broadcasted_iota(jnp.int32, (24, 128), 0) - 4 + scal[1]
    cor_c = coriolis_of(rows, rows_total)
    cor_s = coriolis_of(rows - 1, rows_total)
    d_c = [p_buf[8:32, :]]
    d_e = [jnp.minimum(d_c[0], from_east(d_c)[0])]
    d_n = [jnp.minimum(d_c[0], p_buf[9:33, :])]
    d_s = [jnp.minimum(d_c[0], p_buf[7:31, :])]

    for n in range(1, ITERS + 1):
        src, dst = (c_buf, c_alt) if n % 2 else (c_alt, c_buf)

        def dynamics(k, carry):
            up, prev = carry
            read = lambda buf, r: [buf[k, r:r + 24, :]]
            h_new, u_new, v_new, co, links, ratios = level_step(
                k, read(h_buf, 7), read(h_buf, 8), read(h_buf, 9), read(u_buf, 7), read(u_buf, 8),
                read(v_buf, 7), read(v_buf, 8), (d_c, d_e, d_n, d_s), cor_c, cor_s, read(d_buf, 8), up, prev)
            h_buf[k, 8:32, :] = h_new[0]
            u_buf[k, 8:32, :] = u_new[0]
            v_buf[k, 8:32, :] = v_new[0]
            for c in range(7):
                coef[c, k] = co[0][c]
            return links, ratios

        lax.fori_loop(0, LV, dynamics, (zeros_like_tiles(24, 1), zeros_like_tiles(24, 1)))

        for r0 in ((8, 16, 24) if n < ITERS else (12, 20)):
            def down(k, before):
                co = [[coef[c, k, r0 - 8:r0, :]] for c in range(6)]
                read = lambda t, r: [src[t, k, r:r + 8, :]]
                now = forward(k, co, [(read(t, r0), read(t, r0 - 1), read(t, r0 + 1)) for t in range(4)], before)
                for t in range(4):
                    solved[k, t] = now[t][0]
                return now

            lax.fori_loop(0, LV, down, [zeros_like_tiles(8, 1) for _ in range(4)])

            def upward(i, m):
                k = LV - 1 - i
                r = coef[6, k, r0 - 8:r0, :]
                m = [solved[k, t] + r * m[t] for t in range(4)]
                turned = [[x] + [pltpu.roll(x, 32 * rho, 1) for rho in range(1, 4)] for x in m]
                for s in range(2):
                    for go in range(2):
                        acc = None
                        for gi in range(2):
                            for rho in range(4):
                                term = table[((s * 2 + go) * 2 + gi) * 4 + rho] * turned[2 * s + gi][rho]
                                acc = term if acc is None else acc + term
                        dst[2 * s + go, k, r0:r0 + 8, :] = acc
                return m

            lax.fori_loop(0, LV, upward, [jnp.zeros((8, 128), F32) for _ in range(4)])

    final = c_buf if ITERS % 2 == 0 else c_alt

    def merge(inner, outer, strip, q, j, i):
        turned = pltpu.roll(inner, 4, 0)
        body = jnp.where(low, outer, turned) if i == 0 else jnp.where(low, turned, outer)
        if j == 0:
            return jnp.where(lane < 4, pltpu.roll(strip, (-(32 * q + 4)) % 128, 1), body)
        return jnp.where(lane >= 124, pltpu.roll(strip, (100 - 32 * q) % 128, 1), body)

    @pl.loop(0, LV)
    def _(k):
        for t in range(NT):
            for i in range(2):
                strip = final[t // 4, k, 12 + 8 * i:20 + 8 * i, :]
                for j in range(2):
                    out_c[t, k, 8 * i:8 * i + 8, 128 * j:128 * j + 128] = merge(
                        mid[t, k, j], edge[t, k, j], strip, t % 4, j, i)

    off = scal[0] * (LV // 2)

    @pl.loop(0, LV // 2)
    def _(k):
        for f, buf in enumerate((h_buf, u_buf, v_buf)):
            for i in range(2):
                strip = buf[k + off, 12 + 8 * i:20 + 8 * i, :]
                for j in range(2):
                    x = merge(mid_f[f, k + off, j], edge_f[f, k + off, j], strip, 0, j, i)
                    if f == 0:
                        out_h[k, 8 * i:8 * i + 8, 128 * j:128 * j + 128] = x
                    else:
                        out_v[f - 1, k, 8 * i:8 * i + 8, 128 * j:128 * j + 128] = x


def sds(*shape):
    return jax.ShapeDtypeStruct(shape, F32)


def body(tracers, thickness, velocity, diffusivity, reaction, land_mask, level_count):
    rows_local = thickness.shape[1]
    rows_total = rows_local * lax.axis_size("ty")
    set_index = lax.axis_index("set").astype(jnp.int32)
    row_start = lax.axis_index("ty").astype(jnp.int32) * rows_local
    scal = jnp.stack([set_index, row_start])
    swap = [(0, 1), (1, 0)]
    h_pair = lax.ppermute(thickness, "set", swap)
    v_pair = lax.ppermute(velocity, "set", swap)
    own = (scal, tracers, thickness, h_pair, velocity, v_pair, diffusivity, land_mask, level_count)
    own_specs = [SMEM] + [ANY] * 6 + [VMEM] * 2
    params = pltpu.CompilerParams(vmem_limit_bytes=VMEM_LIMIT)
    y_up, y_dn = pl.pallas_call(
        rows_kernel, out_shape=[sds(161, 2, 8, 128)] * 2, in_specs=own_specs, out_specs=[VMEM] * 2,
        scratch_shapes=OWN_SCRATCH, compiler_params=params, name="edge_rows")(*own)
    ty = lax.axis_size("ty")
    north = [(i, i + 1) for i in range(ty - 1)]
    south = [(j, i) for i, j in north]
    y_s = lax.ppermute(y_up, "ty", north)
    y_n = lax.ppermute(y_dn, "ty", south)
    saved, saved_f, mid, mid_f = pl.pallas_call(
        lambda *a: inner_kernel(rows_total, *a),
        out_shape=[sds(ITERS, NT, LV, 2, 8, 128), sds(ITERS, 3, LV, 2, 8, 128), sds(NT, LV, 2, 8, 128), sds(3, LV, 2, 8, 128)],
        in_specs=own_specs + [SMEM], out_specs=[VMEM] * 4,
        scratch_shapes=OWN_SCRATCH + [
            pltpu.VMEM((NT, LV, 2, 32, 128), F32),
            pltpu.VMEM((LV, PER, 2, 8, 128), F32),
            pltpu.VMEM((7, LV, 2, 16, 128), F32),
            pltpu.VMEM((128, 8, 128), F32)],
        compiler_params=params, name="inner")(*own, reaction)
    o_ref, x_r, x_l = pl.pallas_call(
        strip_pack_kernel, out_shape=[sds(LV + 1, 5, 24, 128), sds(LV + 1, 24, 128), sds(LV + 1, 24, 128)],
        in_specs=own_specs + [VMEM] * 2, out_specs=[VMEM] * 3,
        scratch_shapes=OWN_SCRATCH, compiler_params=params, name="strip_pack")(*own, y_s, y_n)
    tx = lax.axis_size("tx")
    east = [(i, (i + 1) % tx) for i in range(tx)]
    west = [(j, i) for i, j in east]
    x_west = lax.ppermute(x_r, "tx", east)
    x_east = lax.ppermute(x_l, "tx", west)
    edge, edge_f = pl.pallas_call(
        lambda *a: edge_kernel(rows_total, *a),
        out_shape=[sds(NT, LV, 2, 8, 128), sds(3, LV, 2, 8, 128)],
        in_specs=[SMEM, ANY, ANY, VMEM, VMEM, ANY, VMEM, VMEM, SMEM], out_specs=[VMEM] * 2,
        scratch_shapes=[
            pltpu.VMEM((ITERS, NT, LV, 2, 16, 128), F32),
            pltpu.VMEM((ITERS, 3, LV, 2, 16, 128), F32),
            pltpu.VMEM((LV, 2, 32, 128), F32),
            pltpu.VMEM((2, 32, 128), jnp.int32),
            pltpu.VMEM((LV, PER, 2, 8, 128), F32),
            pltpu.VMEM((7, LV, 2, 8, 128), F32),
            pltpu.VMEM((128, 8, 128), F32),
            pltpu.SemaphoreType.DMA((10,))],
        compiler_params=params, name="edge")(scal, saved, saved_f, y_s, y_n, diffusivity, land_mask, level_count, reaction)
    return pl.pallas_call(
        lambda *a: strip_kernel(rows_total, *a),
        out_shape=[sds(*tracers.shape), sds(*thickness.shape), sds(*velocity.shape)],
        in_specs=[SMEM, VMEM, VMEM, VMEM, SMEM, VMEM, VMEM, VMEM, VMEM], out_specs=[VMEM] * 3,
        scratch_shapes=[
            pltpu.VMEM((4, LV, 40, 128), F32),
            pltpu.VMEM((4, LV, 40, 128), F32),
            pltpu.VMEM((LV, 40, 128), F32),
            pltpu.VMEM((LV, 40, 128), F32),
            pltpu.VMEM((LV, 40, 128), F32),
            pltpu.VMEM((LV, 40, 128), F32),
            pltpu.VMEM((40, 128), jnp.int32),
            pltpu.VMEM((LV, 4, 8, 128), F32),
            pltpu.VMEM((7, LV, 24, 128), F32),
            pltpu.VMEM((32, 8, 128), F32)],
        compiler_params=params, name="strips")(scal, o_ref, x_west, x_east, reaction, mid, mid_f, edge, edge_f)


def solution(mesh):
    placed = (
        P("set", None, "ty", "tx"),
        P("set", "ty", "tx"),
        P(None, "set", "ty", "tx"),
        P(None, "ty", "tx"),
        P("set", None, None),
        P("ty", "tx"),
        P("ty", "tx"),
    )

    def whole(*args):
        return tuple(body(*args))

    return jax.shard_map(
        whole,
        mesh=mesh,
        in_specs=placed,
        out_specs=(P("set", None, "ty", "tx"), P("set", "ty", "tx"), P(None, "set", "ty", "tx")),
        check_vma=False,
    )
```

```python
import jax
import jax.numpy as jnp
from jax import lax
from jax.experimental import pallas as pl
from jax.experimental.pallas import tpu as pltpu
from jax.sharding import PartitionSpec as P

ITERS = 4
DT = 0.2
G = 1.0
ROTATION = 0.5
LV = 16
NT = 16
PER = 8
VMEM_LIMIT = 60 * 1024 * 1024
F32 = jnp.float32
ANY = pl.BlockSpec(memory_space=pl.ANY)
SMEM = pl.BlockSpec(memory_space=pltpu.SMEM)
VMEM = pl.BlockSpec(memory_space=pltpu.VMEM)


def sub_iota(rows=8):
    return lax.broadcasted_iota(jnp.int32, (rows, 128), 0)


def lane_iota(rows=8):
    return lax.broadcasted_iota(jnp.int32, (rows, 128), 1)


def from_east(tiles, joined=True):
    rolled = [pltpu.roll(x, 127, 1) for x in tiles]
    lane = lane_iota(tiles[0].shape[0])
    last = len(tiles) - 1
    return [rolled[i] if i == last or not joined else jnp.where(lane == 127, rolled[i + 1], rolled[i]) for i in range(last + 1)]


def from_west(tiles, joined=True):
    rolled = [pltpu.roll(x, 1, 1) for x in tiles]
    lane = lane_iota(tiles[0].shape[0])
    return [rolled[i] if i == 0 or not joined else jnp.where(lane == 0, rolled[i - 1], rolled[i]) for i in range(len(tiles))]


def coriolis_of(row, rows_total):
    return ROTATION * (2.0 * (row.astype(F32) + 0.5) / rows_total - 1.0)


def level_step(k, h_s, h_c, h_n, u_s, u_c, v_s, v_c, deep, cor_c, cor_s, diff, up, prev):
    d_c, d_e, d_n, d_s = deep
    h_e = from_east(h_c)
    count = len(h_c)
    u_new, v_new, u_flux, v_flux, s_flux = [], [], [], [], []
    for j in range(count):
        un = jnp.where(k < d_e[j], u_c[j] + DT * (cor_c * v_c[j] - G * (h_e[j] - h_c[j])), 0.0)
        vn = jnp.where(k < d_n[j], v_c[j] - DT * (cor_c * u_c[j] + G * (h_n[j] - h_c[j])), 0.0)
        vs = jnp.where(k < d_s[j], v_s[j] - DT * (cor_s * u_s[j] + G * (h_c[j] - h_s[j])), 0.0)
        u_new.append(un)
        v_new.append(vn)
        u_flux.append(un * 0.5 * (h_c[j] + h_e[j]))
        v_flux.append(vn * 0.5 * (h_c[j] + h_n[j]))
        s_flux.append(vs * 0.5 * (h_s[j] + h_c[j]))
    w_flux = from_west(u_flux)
    h_new, coefs, links, ratios = [], [], [], []
    for j in range(count):
        fe, fw, fn, fs = u_flux[j], w_flux[j], v_flux[j], s_flux[j]
        hn = h_c[j] - DT * ((fe - fw) + (fn - fs))
        link = jnp.where(k + 1 < d_c[j], DT * diff[j], 0.0)
        q = jnp.where(k < d_c[j], 1.0 / (hn + up[j] + link - up[j] * prev[j]), 0.0)
        r = link * q
        dq = DT * q
        ce = dq * jnp.maximum(-fe, 0.0)
        cw = dq * jnp.maximum(fw, 0.0)
        cn = dq * jnp.maximum(-fn, 0.0)
        cs = dq * jnp.maximum(fs, 0.0)
        out = (jnp.maximum(fe, 0.0) - jnp.minimum(fw, 0.0)) + (jnp.maximum(fn, 0.0) - jnp.minimum(fs, 0.0))
        ca = q * h_c[j] - dq * out
        h_new.append(hn)
        links.append(link)
        ratios.append(r)
        coefs.append((ca, ce, cw, cn, cs, up[j] * q, r))
    return h_new, u_new, v_new, coefs, links, ratios


def forward(coefs, cells, before, joined=True):
    result = []
    for t, (c, s, n) in enumerate(cells):
        e = from_east(c, joined)
        w = from_west(c, joined)
        result.append([
            ((coefs[0][j] * c[j] + coefs[1][j] * e[j]) + (coefs[2][j] * w[j] + coefs[3][j] * n[j]))
            + (coefs[4][j] * s[j] + coefs[5][j] * before[t][j])
            for j in range(len(c))
        ])
    return result


def react(table, s, m):
    outs = []
    for a in range(PER):
        acc = None
        for b in range(PER):
            w = table[s * 64 + a * 8 + b]
            term = [w * x for x in m[b]]
            acc = term if acc is None else [p + q for p, q in zip(acc, term)]
        outs.append(acc)
    return outs


def fill_table(react_ref, table):
    for s in range(2):
        for a in range(PER):
            for b in range(PER):
                v = DT * react_ref[s, a, b] + (1.0 if a == b else 0.0)
                table[s * 64 + a * 8 + b] = jnp.full((8, 128), v, F32)


def zeros_like_tiles(rows, count):
    return [jnp.zeros((rows, 128), F32) for _ in range(count)]


def own_copies(tr, ho, hp, vo, vp, df, off, c_buf, h_buf, u_buf, v_buf, d_buf, sem):
    copies = []
    part = LV // 2
    other = part - off
    for j in range(2):
        lanes = pl.ds(128 * j, 128)
        rows = pl.ds(8, 16)
        copies.append(pltpu.make_async_copy(ho.at[:, :, lanes], h_buf.at[pl.ds(off, part), j, rows, :], sem.at[0 + j]))
        copies.append(pltpu.make_async_copy(hp.at[:, :, lanes], h_buf.at[pl.ds(other, part), j, rows, :], sem.at[2 + j]))
        copies.append(pltpu.make_async_copy(vo.at[0, :, :, lanes], u_buf.at[pl.ds(off, part), j, rows, :], sem.at[4 + j]))
        copies.append(pltpu.make_async_copy(vp.at[0, :, :, lanes], u_buf.at[pl.ds(other, part), j, rows, :], sem.at[6 + j]))
        copies.append(pltpu.make_async_copy(vo.at[1, :, :, lanes], v_buf.at[pl.ds(off, part), j, rows, :], sem.at[8 + j]))
        copies.append(pltpu.make_async_copy(vp.at[1, :, :, lanes], v_buf.at[pl.ds(other, part), j, rows, :], sem.at[10 + j]))
        copies.append(pltpu.make_async_copy(df.at[:, :, lanes], d_buf.at[:, j, rows, :], sem.at[12 + j]))
    tracer = []
    for s in range(2):
        for j in range(2):
            tracer.append(pltpu.make_async_copy(
                tr.at[pl.ds(8 * s, 8), :, :, pl.ds(128 * j, 128)],
                c_buf.at[pl.ds(8 * s, 8), :, j, pl.ds(8, 16), :], sem.at[14 + 2 * s + j]))
    return copies, tracer


OWN_SCRATCH = [
    pltpu.VMEM((NT, LV, 2, 32, 128), F32),
    pltpu.VMEM((LV, 2, 32, 128), F32),
    pltpu.VMEM((LV, 2, 32, 128), F32),
    pltpu.VMEM((LV, 2, 32, 128), F32),
    pltpu.VMEM((LV, 2, 32, 128), F32),
    pltpu.VMEM((2, 32, 128), jnp.int32),
    pltpu.SemaphoreType.DMA((18,)),
]


def fill_depth(land, level, p_buf):
    for j in range(2):
        lanes = slice(128 * j, 128 * j + 128)
        p_buf[j, 8:24, :] = jnp.where(land[:, lanes] == 1, level[:, lanes], 0)


def rows_kernel(scal, tr, ho, hp, vo, vp, df, land, level, y_up, y_dn, c_buf, h_buf, u_buf, v_buf, d_buf, p_buf, sem):
    off = scal[0] * (LV // 2)
    fields, tracer = own_copies(tr, ho, hp, vo, vp, df, off, c_buf, h_buf, u_buf, v_buf, d_buf, sem)
    for c in fields + tracer:
        c.start()
    fill_depth(land, level, p_buf)
    for c in fields + tracer:
        c.wait()
    low = sub_iota() < 4

    def put(index, j, first, second):
        y_up[index, j] = jnp.where(low, first(20), second(16))
        y_dn[index, j] = jnp.where(low, first(8), second(4))

    @pl.loop(0, LV, unroll=2)
    def _(k):
        for j in range(2):
            for t in range(PER):
                put(t * LV + k, j, lambda r: c_buf[t, k, j, r:r + 8, :], lambda r: c_buf[t + PER, k, j, r:r + 8, :])
            put(128 + k, j, lambda r: h_buf[k, j, r:r + 8, :], lambda r: u_buf[k, j, r:r + 8, :])
            put(144 + k, j, lambda r: v_buf[k, j, r:r + 8, :], lambda r: d_buf[k, j, r:r + 8, :])

    for j in range(2):
        get = lambda r: p_buf[j, r:r + 8, :].astype(F32)
        put(160, j, get, get)


def inner_kernel(rows_total, scal, tr, ho, hp, vo, vp, df, land, level, reaction, saved_out, saved_f, mid, mid_f,
                 c_buf, h_buf, u_buf, v_buf, d_buf, p_buf, sem, c_alt, solved, coef, table, saved, out_sem):
    off = scal[0] * (LV // 2)
    fields, tracer = own_copies(tr, ho, hp, vo, vp, df, off, c_buf, h_buf, u_buf, v_buf, d_buf, sem)
    for c in fields + tracer:
        c.start()
    fill_depth(land, level, p_buf)
    fill_table(reaction, table)
    six = sub_iota() < 6
    rows = lax.broadcasted_iota(jnp.int32, (16, 128), 0) + scal[1]
    cor_c = coriolis_of(rows, rows_total)
    cor_s = coriolis_of(rows - 1, rows_total)
    d_c = [p_buf[j, 8:24, :] for j in range(2)]
    d_e = [jnp.minimum(a, b) for a, b in zip(d_c, from_east(d_c))]
    d_n = [jnp.minimum(d_c[j], p_buf[j, 9:25, :]) for j in range(2)]
    d_s = [jnp.minimum(d_c[j], p_buf[j, 7:23, :]) for j in range(2)]
    for c in fields:
        c.wait()

    def keep(n, read):
        return jnp.where(six, read(4 + n), read(16 - n))

    def keep_fields(n):
        @pl.loop(0, LV)
        def _(k):
            for f, buf in enumerate((h_buf, u_buf, v_buf)):
                for j in range(2):
                    saved_f[n, f, k, j] = keep(n, lambda r: buf[k, j, r:r + 8, :])

    def keep_tracers(n, buf):
        @pl.loop(0, LV)
        def _(k):
            for t in range(NT):
                for j in range(2):
                    saved[n, t, k, j] = keep(n, lambda r: buf[t, k, j, r:r + 8, :])

    keep_fields(0)
    for c in tracer:
        c.wait()
    keep_tracers(0, c_buf)
    leaving = [pltpu.make_async_copy(saved.at[n], saved_out.at[n], out_sem.at[n]) for n in range(ITERS)]
    leaving[0].start()
    for n in range(1, ITERS + 1):
        src, dst = (c_buf, c_alt) if n % 2 else (c_alt, c_buf)

        def dynamics(k, carry):
            up, prev = carry
            read = lambda buf, r: [buf[k, j, r:r + 16, :] for j in range(2)]
            h_new, u_new, v_new, co, links, ratios = level_step(
                k, read(h_buf, 7), read(h_buf, 8), read(h_buf, 9), read(u_buf, 7), read(u_buf, 8),
                read(v_buf, 7), read(v_buf, 8), (d_c, d_e, d_n, d_s), cor_c, cor_s, read(d_buf, 8), up, prev)
            for j in range(2):
                h_buf[k, j, 8:24, :] = h_new[j]
                u_buf[k, j, 8:24, :] = u_new[j]
                v_buf[k, j, 8:24, :] = v_new[j]
                for c in range(7):
                    coef[c, k, j] = co[j][c]
            return links, ratios

        lax.fori_loop(0, LV, dynamics, (zeros_like_tiles(16, 2), zeros_like_tiles(16, 2)), unroll=4)
        if n < ITERS:
            keep_fields(n)
        else:
            @pl.loop(0, LV)
            def _(k):
                for f, buf in enumerate((h_buf, u_buf, v_buf)):
                    for j in range(2):
                        mid_f[f, k, j] = buf[k, j, 12:20, :]

        for r0 in ((8, 16) if n < ITERS else (12,)):
            @pl.loop(0, 2)
            def _(s):
                def down(k, before):
                    co = [[coef[c, k, j, r0 - 8:r0, :] for j in range(2)] for c in range(6)]
                    read = lambda t, r: [src[s * PER + t, k, j, r:r + 8, :] for j in range(2)]
                    now = forward(co, [(read(t, r0), read(t, r0 - 1), read(t, r0 + 1)) for t in range(PER)], before)
                    for t in range(PER):
                        for j in range(2):
                            solved[k, t, j] = now[t][j]
                    return now

                lax.fori_loop(0, LV, down, [zeros_like_tiles(8, 2) for _ in range(PER)], unroll=8)

                def upward(i, m):
                    k = LV - 1 - i
                    r = [coef[6, k, j, r0 - 8:r0, :] for j in range(2)]
                    m = [[solved[k, t, j] + r[j] * m[t][j] for j in range(2)] for t in range(PER)]
                    outs = react(table, s, m)
                    for t in range(PER):
                        for j in range(2):
                            if n < ITERS:
                                dst[s * PER + t, k, j, r0:r0 + 8, :] = outs[t][j]
                            else:
                                mid[s * PER + t, k, j] = outs[t][j]
                    return m

                lax.fori_loop(0, LV, upward, [zeros_like_tiles(8, 2) for _ in range(PER)], unroll=4)
        if n < ITERS:
            keep_tracers(n, dst)
            leaving[n].start()
    for c in leaving:
        c.wait()


def strip_pack_kernel(scal, tr, ho, hp, vo, vp, df, land, level, y_s, y_n, o_ref, x_r, x_l,
                      c_buf, h_buf, u_buf, v_buf, d_buf, p_buf, sem):
    off = scal[0] * (LV // 2)
    fields, tracer = own_copies(tr, ho, hp, vo, vp, df, off, c_buf, h_buf, u_buf, v_buf, d_buf, sem)
    for c in fields + tracer:
        c.start()
    fill_depth(land, level, p_buf)
    for c in fields + tracer:
        c.wait()
    low = sub_iota() < 4
    lane = lane_iota()
    place = lane & 31
    slot = lane >> 5

    def three(read, index, half, j):
        ys, yn = y_s[index, j], y_n[index, j]
        if half == 0:
            yn = pltpu.roll(yn, 4, 0)
        else:
            ys = pltpu.roll(ys, 4, 0)
        return [jnp.where(low, ys, read(4)), read(12), jnp.where(low, read(20), yn)]

    def pack(sources):
        acc = [None] * 3
        for q, (read, index, half) in enumerate(sources):
            left = three(lambda r: read(0, r), index, half, 0)
            right = three(lambda r: read(1, r), index, half, 1)
            for i in range(3):
                a = pltpu.roll(left[i], (4 + 32 * q) % 128, 1)
                b = pltpu.roll(right[i], (28 + 32 * q) % 128, 1)
                x = jnp.where(place < 16, a, b)
                acc[i] = x if acc[i] is None else jnp.where(slot == q, x, acc[i])
        return acc

    @pl.loop(0, LV, unroll=2)
    def _(k):
        def tracer_source(t):
            return (lambda j, r: c_buf[t, k, j, r:r + 8, :], (t % PER) * LV + k, t // PER)

        groups = [[tracer_source(4 * g + q) for q in range(4)] for g in range(4)]
        groups.append([
            (lambda j, r: h_buf[k, j, r:r + 8, :], 128 + k, 0), (lambda j, r: u_buf[k, j, r:r + 8, :], 128 + k, 1),
            (lambda j, r: v_buf[k, j, r:r + 8, :], 144 + k, 0), (lambda j, r: d_buf[k, j, r:r + 8, :], 144 + k, 1)])
        xr, xl = [jnp.zeros((8, 128), F32)] * 3, [jnp.zeros((8, 128), F32)] * 3
        for g in range(5):
            packed = pack(groups[g])
            here = (place >= 4 * g) & (place < 4 * g + 4)
            for i in range(3):
                o_ref[k, g, 8 * i:8 * i + 8, :] = packed[i]
                xr[i] = jnp.where(here, pltpu.roll(packed[i], (4 * g - 24) % 128, 1), xr[i])
                xl[i] = jnp.where(here, pltpu.roll(packed[i], (4 * g - 4) % 128, 1), xl[i])
        for i in range(3):
            x_r[k, 8 * i:8 * i + 8, :] = xr[i]
            x_l[k, 8 * i:8 * i + 8, :] = xl[i]

    packed = pack([(lambda j, r: p_buf[j, r:r + 8, :].astype(F32), 160, 0)] * 4)
    for i in range(3):
        for g in range(5):
            o_ref[LV, g, 8 * i:8 * i + 8, :] = packed[i]
        x_r[LV, 8 * i:8 * i + 8, :] = pltpu.roll(packed[i], (16 - 24) % 128, 1)
        x_l[LV, 8 * i:8 * i + 8, :] = pltpu.roll(packed[i], (16 - 4) % 128, 1)


def edge_kernel(rows_total, scal, saved, saved_f, y_s, y_n, df, land, level, reaction, out_c, out_f,
                c_buf, f_buf, d_buf, p_buf, solved, coef, table, sem):
    copies = []
    for n in range(ITERS):
        copies.append(pltpu.make_async_copy(saved_f.at[n], f_buf.at[n, :, :, :, pl.ds(0, 8), :], sem.at[n]))
    for j in range(2):
        copies.append(pltpu.make_async_copy(df.at[:, :, pl.ds(128 * j, 128)], d_buf.at[:, j, pl.ds(8, 16), :], sem.at[4 + j]))
    tracer = [pltpu.make_async_copy(saved.at[n], c_buf.at[n, :, :, :, pl.ds(0, 8), :], sem.at[6 + n]) for n in range(ITERS)]
    for c in copies + tracer:
        c.start()
    fill_table(reaction, table)
    fill_depth(land, level, p_buf)
    sub = sub_iota()
    low = sub < 4
    for c in copies:
        c.wait()
    tracer[0].wait()

    def put(ref, y, half, south):
        if half != (0 if south else 1):
            y = pltpu.roll(y, 4, 0)
        if south:
            pltpu.store(ref.at[pl.ds(0, 8), :], y, mask=low)
        else:
            pltpu.store(ref.at[pl.ds(4, 8), :], y, mask=jnp.logical_not(low))

    @pl.loop(0, LV, unroll=2)
    def _(k):
        for j in range(2):
            for t in range(PER):
                ys, yn = y_s[t * LV + k, j], y_n[t * LV + k, j]
                for half in range(2):
                    put(c_buf.at[0, t + PER * half, k, j], ys, half, True)
                    put(c_buf.at[0, t + PER * half, k, j], yn, half, False)
            for f, (index, half) in enumerate(((128, 0), (128, 1), (144, 0))):
                put(f_buf.at[0, f, k, j], y_s[index + k, j], half, True)
                put(f_buf.at[0, f, k, j], y_n[index + k, j], half, False)
            ys, yn = y_s[144 + k, j], y_n[144 + k, j]
            pltpu.store(d_buf.at[k, j, pl.ds(0, 8), :], ys, mask=jnp.logical_not(low))
            pltpu.store(d_buf.at[k, j, pl.ds(24, 8), :], pltpu.roll(yn, 4, 0), mask=low)

    for j in range(2):
        ys, yn = y_s[160, j].astype(jnp.int32), y_n[160, j].astype(jnp.int32)
        pltpu.store(p_buf.at[j, pl.ds(0, 8), :], ys, mask=jnp.logical_not(low))
        pltpu.store(p_buf.at[j, pl.ds(24, 8), :], yn, mask=low)

    def gather(read, shift):
        return jnp.where(low, read(shift), read(shift + 2))

    for n in range(1, ITERS + 1):
        if n < ITERS:
            tracer[n].wait()

        def at(buf, j, shift):
            return jnp.where(low, buf[j, 4 + n + shift:12 + n + shift, :], buf[j, 20 - n + shift:28 - n + shift, :])

        row = jnp.where(low, sub - 4 + n, sub + 12 - n) + scal[1]
        cor_c = coriolis_of(row, rows_total)
        cor_s = coriolis_of(row - 1, rows_total)
        d_c = [at(p_buf, j, 0) for j in range(2)]
        d_e = [jnp.minimum(a, b) for a, b in zip(d_c, from_east(d_c))]
        d_n = [jnp.minimum(d_c[j], at(p_buf, j, 1)) for j in range(2)]
        d_s = [jnp.minimum(d_c[j], at(p_buf, j, -1)) for j in range(2)]

        def dynamics(k, carry):
            up, prev = carry
            read = lambda f, shift: [gather(lambda r: f_buf[n - 1, f, k, j, r:r + 8, :], shift) for j in range(2)]
            diff = [at(d_buf.at[k], j, 0) for j in range(2)]
            h_new, u_new, v_new, co, links, ratios = level_step(
                k, read(0, 0), read(0, 1), read(0, 2), read(1, 0), read(1, 1), read(2, 0), read(2, 1),
                (d_c, d_e, d_n, d_s), cor_c, cor_s, diff, up, prev)
            for j in range(2):
                for f, x in enumerate((h_new[j], u_new[j], v_new[j])):
                    if n < ITERS:
                        pltpu.store(f_buf.at[n, f, k, j, pl.ds(0, 8), :], x, mask=low)
                        pltpu.store(f_buf.at[n, f, k, j, pl.ds(4, 8), :], x, mask=jnp.logical_not(low))
                    else:
                        out_f[f, k, j] = x
                for c in range(7):
                    coef[c, k, j] = co[j][c]
            return links, ratios

        lax.fori_loop(0, LV, dynamics, (zeros_like_tiles(8, 2), zeros_like_tiles(8, 2)), unroll=8)

        @pl.loop(0, 2)
        def _(s):
            def down(k, before):
                co = [[coef[c, k, j] for j in range(2)] for c in range(6)]

                def read(t, shift):
                    return [gather(lambda r: c_buf[n - 1, s * PER + t, k, j, r:r + 8, :], shift) for j in range(2)]

                now = forward(co, [(read(t, 1), read(t, 0), read(t, 2)) for t in range(PER)], before)
                for t in range(PER):
                    for j in range(2):
                        solved[k, t, j] = now[t][j]
                return now

            lax.fori_loop(0, LV, down, [zeros_like_tiles(8, 2) for _ in range(PER)], unroll=8)

            def upward(i, m):
                k = LV - 1 - i
                r = [coef[6, k, j] for j in range(2)]
                m = [[solved[k, t, j] + r[j] * m[t][j] for j in range(2)] for t in range(PER)]
                outs = react(table, s, m)
                for t in range(PER):
                    for j in range(2):
                        if n < ITERS:
                            pltpu.store(c_buf.at[n, s * PER + t, k, j, pl.ds(0, 8), :], outs[t][j], mask=low)
                            pltpu.store(c_buf.at[n, s * PER + t, k, j, pl.ds(4, 8), :], outs[t][j], mask=jnp.logical_not(low))
                        else:
                            out_c[s * PER + t, k, j] = outs[t][j]
                return m

            lax.fori_loop(0, LV, upward, [zeros_like_tiles(8, 2) for _ in range(PER)], unroll=4)


def strip_kernel(rows_total, scal, o_ref, x_r, x_l, reaction, mid, mid_f, edge, edge_f, out_c, out_h, out_v,
                 c_buf, c_alt, h_buf, u_buf, v_buf, d_buf, p_buf, solved, coef, table):
    lane = lane_iota()
    place = lane & 31
    slot = lane >> 5
    low = sub_iota() < 4
    for s in range(2):
        for go in range(2):
            for gi in range(2):
                for rho in range(4):
                    v = jnp.zeros((8, 128), F32)
                    for q in range(4):
                        a, b = 4 * go + q, 4 * gi + (q - rho) % 4
                        w = DT * reaction[s, a, b] + (1.0 if a == b else 0.0)
                        v = jnp.where(slot == q, jnp.full((8, 128), w, F32), v)
                    table[((s * 2 + go) * 2 + gi) * 4 + rho] = v

    def whole(k, g, i, xg):
        rows = slice(8 * i, 8 * i + 8)
        a = pltpu.roll(x_r[k, rows, :], (-4 * xg) % 128, 1)
        b = pltpu.roll(x_l[k, rows, :], (28 - 4 * xg) % 128, 1)
        return jnp.where(place < 4, a, jnp.where(place >= 28, b, o_ref[k, g, rows, :]))

    @pl.loop(0, LV, unroll=4)
    def _(k):
        for i in range(3):
            for g in range(4):
                c_buf[g, k, 8 + 8 * i:16 + 8 * i, :] = whole(k, g, i, g)
            x = whole(k, 4, i, 4)
            for f, buf in enumerate((h_buf, u_buf, v_buf, d_buf)):
                y = jnp.where(lane < 32, pltpu.roll(x, (-32 * f) % 128, 1), 0.0)
                y = y + pltpu.roll(y, 32, 1)
                y = y + pltpu.roll(y, 64, 1)
                buf[k, 8 + 8 * i:16 + 8 * i, :] = y

    for i in range(3):
        p_buf[8 + 8 * i:16 + 8 * i, :] = whole(LV, 4, i, 4).astype(jnp.int32)

    rows = lax.broadcasted_iota(jnp.int32, (24, 128), 0) - 4 + scal[1]
    cor_c = coriolis_of(rows, rows_total)
    cor_s = coriolis_of(rows - 1, rows_total)
    d_c = [p_buf[8:32, :]]
    d_e = [jnp.minimum(d_c[0], from_east(d_c)[0])]
    d_n = [jnp.minimum(d_c[0], p_buf[9:33, :])]
    d_s = [jnp.minimum(d_c[0], p_buf[7:31, :])]

    for n in range(1, ITERS + 1):
        src, dst = (c_buf, c_alt) if n % 2 else (c_alt, c_buf)

        def dynamics(k, carry):
            up, prev = carry
            read = lambda buf, r: [buf[k, r:r + 24, :]]
            h_new, u_new, v_new, co, links, ratios = level_step(
                k, read(h_buf, 7), read(h_buf, 8), read(h_buf, 9), read(u_buf, 7), read(u_buf, 8),
                read(v_buf, 7), read(v_buf, 8), (d_c, d_e, d_n, d_s), cor_c, cor_s, read(d_buf, 8), up, prev)
            h_buf[k, 8:32, :] = h_new[0]
            u_buf[k, 8:32, :] = u_new[0]
            v_buf[k, 8:32, :] = v_new[0]
            for c in range(7):
                coef[c, k] = co[0][c]
            return links, ratios

        lax.fori_loop(0, LV, dynamics, (zeros_like_tiles(24, 1), zeros_like_tiles(24, 1)), unroll=8)

        starts = (8, 16, 24) if n < ITERS else (12, 20)
        tiles = len(starts)

        def down(k, before):
            co = [[coef[c, k, r0 - 8:r0, :] for r0 in starts] for c in range(6)]
            read = lambda t, shift: [src[t, k, r0 + shift:r0 + shift + 8, :] for r0 in starts]
            now = forward(co, [(read(t, 0), read(t, -1), read(t, 1)) for t in range(4)], before, joined=False)
            for t in range(4):
                for i in range(tiles):
                    solved[k, t, i] = now[t][i]
            return now

        lax.fori_loop(0, LV, down, [zeros_like_tiles(8, tiles) for _ in range(4)], unroll=4)

        def upward(i, m):
            k = LV - 1 - i
            r = [coef[6, k, r0 - 8:r0, :] for r0 in starts]
            m = [[solved[k, t, i] + r[i] * m[t][i] for i in range(tiles)] for t in range(4)]
            for i, r0 in enumerate(starts):
                turned = [[m[t][i]] + [pltpu.roll(m[t][i], 32 * rho, 1) for rho in range(1, 4)] for t in range(4)]
                for s in range(2):
                    for go in range(2):
                        acc = None
                        for gi in range(2):
                            for rho in range(4):
                                term = table[((s * 2 + go) * 2 + gi) * 4 + rho] * turned[2 * s + gi][rho]
                                acc = term if acc is None else acc + term
                        dst[2 * s + go, k, r0:r0 + 8, :] = acc
            return m

        lax.fori_loop(0, LV, upward, [zeros_like_tiles(8, tiles) for _ in range(4)], unroll=4)

    final = c_buf if ITERS % 2 == 0 else c_alt

    def merge(inner, outer, strip, q, j, i):
        turned = pltpu.roll(inner, 4, 0)
        body = jnp.where(low, outer, turned) if i == 0 else jnp.where(low, turned, outer)
        if j == 0:
            return jnp.where(lane < 4, pltpu.roll(strip, (-(32 * q + 4)) % 128, 1), body)
        return jnp.where(lane >= 124, pltpu.roll(strip, (100 - 32 * q) % 128, 1), body)

    @pl.loop(0, LV, unroll=2)
    def _(k):
        for t in range(NT):
            for i in range(2):
                strip = final[t // 4, k, 12 + 8 * i:20 + 8 * i, :]
                for j in range(2):
                    out_c[t, k, 8 * i:8 * i + 8, 128 * j:128 * j + 128] = merge(
                        mid[t, k, j], edge[t, k, j], strip, t % 4, j, i)

    off = scal[0] * (LV // 2)

    @pl.loop(0, LV // 2, unroll=4)
    def _(k):
        for f, buf in enumerate((h_buf, u_buf, v_buf)):
            for i in range(2):
                strip = buf[k + off, 12 + 8 * i:20 + 8 * i, :]
                for j in range(2):
                    x = merge(mid_f[f, k + off, j], edge_f[f, k + off, j], strip, 0, j, i)
                    if f == 0:
                        out_h[k, 8 * i:8 * i + 8, 128 * j:128 * j + 128] = x
                    else:
                        out_v[f - 1, k, 8 * i:8 * i + 8, 128 * j:128 * j + 128] = x


def sds(*shape):
    return jax.ShapeDtypeStruct(shape, F32)


def body(tracers, thickness, velocity, diffusivity, reaction, land_mask, level_count):
    rows_local = thickness.shape[1]
    rows_total = rows_local * lax.axis_size("ty")
    set_index = lax.axis_index("set").astype(jnp.int32)
    row_start = lax.axis_index("ty").astype(jnp.int32) * rows_local
    scal = jnp.stack([set_index, row_start])
    swap = [(0, 1), (1, 0)]
    h_pair = lax.ppermute(thickness, "set", swap)
    v_pair = lax.ppermute(velocity, "set", swap)
    own = (scal, tracers, thickness, h_pair, velocity, v_pair, diffusivity, land_mask, level_count)
    own_specs = [SMEM] + [ANY] * 6 + [VMEM] * 2
    params = pltpu.CompilerParams(vmem_limit_bytes=VMEM_LIMIT)
    y_up, y_dn = pl.pallas_call(
        rows_kernel, out_shape=[sds(161, 2, 8, 128)] * 2, in_specs=own_specs, out_specs=[VMEM] * 2,
        scratch_shapes=OWN_SCRATCH, compiler_params=params, name="edge_rows")(*own)
    ty = lax.axis_size("ty")
    north = [(i, i + 1) for i in range(ty - 1)]
    south = [(j, i) for i, j in north]
    y_s = lax.ppermute(y_up, "ty", north)
    y_n = lax.ppermute(y_dn, "ty", south)
    saved, saved_f, mid, mid_f = pl.pallas_call(
        lambda *a: inner_kernel(rows_total, *a),
        out_shape=[sds(ITERS, NT, LV, 2, 8, 128), sds(ITERS, 3, LV, 2, 8, 128), sds(NT, LV, 2, 8, 128), sds(3, LV, 2, 8, 128)],
        in_specs=own_specs + [SMEM], out_specs=[ANY] + [VMEM] * 3,
        scratch_shapes=OWN_SCRATCH + [
            pltpu.VMEM((NT, LV, 2, 32, 128), F32),
            pltpu.VMEM((LV, PER, 2, 8, 128), F32),
            pltpu.VMEM((7, LV, 2, 16, 128), F32),
            pltpu.VMEM((128, 8, 128), F32),
            pltpu.VMEM((ITERS, NT, LV, 2, 8, 128), F32),
            pltpu.SemaphoreType.DMA((ITERS,))],
        compiler_params=params, name="inner")(*own, reaction)
    y_s, y_n, mid_f = lax.optimization_barrier((y_s, y_n, mid_f))
    o_ref, x_r, x_l = pl.pallas_call(
        strip_pack_kernel, out_shape=[sds(LV + 1, 5, 24, 128), sds(LV + 1, 24, 128), sds(LV + 1, 24, 128)],
        in_specs=own_specs + [VMEM] * 2, out_specs=[VMEM] * 3,
        scratch_shapes=OWN_SCRATCH, compiler_params=params, name="strip_pack")(*own, y_s, y_n)
    tx = lax.axis_size("tx")
    east = [(i, (i + 1) % tx) for i in range(tx)]
    west = [(j, i) for i, j in east]
    x_west = lax.ppermute(x_r, "tx", east)
    x_east = lax.ppermute(x_l, "tx", west)
    edge, edge_f = pl.pallas_call(
        lambda *a: edge_kernel(rows_total, *a),
        out_shape=[sds(NT, LV, 2, 8, 128), sds(3, LV, 2, 8, 128)],
        in_specs=[SMEM, ANY, ANY, VMEM, VMEM, ANY, VMEM, VMEM, SMEM], out_specs=[VMEM] * 2,
        scratch_shapes=[
            pltpu.VMEM((ITERS, NT, LV, 2, 16, 128), F32),
            pltpu.VMEM((ITERS, 3, LV, 2, 16, 128), F32),
            pltpu.VMEM((LV, 2, 32, 128), F32),
            pltpu.VMEM((2, 32, 128), jnp.int32),
            pltpu.VMEM((LV, PER, 2, 8, 128), F32),
            pltpu.VMEM((7, LV, 2, 8, 128), F32),
            pltpu.VMEM((128, 8, 128), F32),
            pltpu.SemaphoreType.DMA((10,))],
        compiler_params=params, name="edge")(scal, saved, saved_f, y_s, y_n, diffusivity, land_mask, level_count, reaction)
    return pl.pallas_call(
        lambda *a: strip_kernel(rows_total, *a),
        out_shape=[sds(*tracers.shape), sds(*thickness.shape), sds(*velocity.shape)],
        in_specs=[SMEM, VMEM, VMEM, VMEM, SMEM, VMEM, VMEM, VMEM, VMEM], out_specs=[VMEM] * 3,
        scratch_shapes=[
            pltpu.VMEM((4, LV, 40, 128), F32),
            pltpu.VMEM((4, LV, 40, 128), F32),
            pltpu.VMEM((LV, 40, 128), F32),
            pltpu.VMEM((LV, 40, 128), F32),
            pltpu.VMEM((LV, 40, 128), F32),
            pltpu.VMEM((LV, 40, 128), F32),
            pltpu.VMEM((40, 128), jnp.int32),
            pltpu.VMEM((LV, 4, 3, 8, 128), F32),
            pltpu.VMEM((7, LV, 24, 128), F32),
            pltpu.VMEM((32, 8, 128), F32)],
        compiler_params=params, name="strips")(scal, o_ref, x_west, x_east, reaction, mid, mid_f, edge, edge_f)


def solution(mesh):
    placed = (
        P("set", None, "ty", "tx"),
        P("set", "ty", "tx"),
        P(None, "set", "ty", "tx"),
        P(None, "ty", "tx"),
        P("set", None, None),
        P("ty", "tx"),
        P("ty", "tx"),
    )

    def whole(*args):
        return tuple(body(*args))

    return jax.shard_map(
        whole,
        mesh=mesh,
        in_specs=placed,
        out_specs=(P("set", None, "ty", "tx"), P("set", "ty", "tx"), P(None, "set", "ty", "tx")),
        check_vma=False,
    )
```

```python
import jax
import jax.numpy as jnp
from jax import lax
from jax.experimental import pallas as pl
from jax.experimental.pallas import tpu as pltpu
from jax.sharding import PartitionSpec as P

ITERS = 4
DT = 0.2
G = 1.0
ROTATION = 0.5
LV = 16
NT = 16
PER = 8
VMEM_LIMIT = 60 * 1024 * 1024
F32 = jnp.float32
ANY = pl.BlockSpec(memory_space=pl.ANY)
SMEM = pl.BlockSpec(memory_space=pltpu.SMEM)
VMEM = pl.BlockSpec(memory_space=pltpu.VMEM)


def sub_iota(rows=8):
    return lax.broadcasted_iota(jnp.int32, (rows, 128), 0)


def lane_iota(rows=8):
    return lax.broadcasted_iota(jnp.int32, (rows, 128), 1)


def from_east(tiles, joined=True):
    rolled = [pltpu.roll(x, 127, 1) for x in tiles]
    lane = lane_iota(tiles[0].shape[0])
    last = len(tiles) - 1
    return [rolled[i] if i == last or not joined else jnp.where(lane == 127, rolled[i + 1], rolled[i]) for i in range(last + 1)]


def from_west(tiles, joined=True):
    rolled = [pltpu.roll(x, 1, 1) for x in tiles]
    lane = lane_iota(tiles[0].shape[0])
    return [rolled[i] if i == 0 or not joined else jnp.where(lane == 0, rolled[i - 1], rolled[i]) for i in range(len(tiles))]


def coriolis_of(row, rows_total):
    return ROTATION * (2.0 * (row.astype(F32) + 0.5) / rows_total - 1.0)


def level_step(k, h_s, h_c, h_n, u_s, u_c, v_s, v_c, deep, cor_c, cor_s, diff, up, prev):
    d_c, d_e, d_n, d_s = deep
    h_e = from_east(h_c)
    count = len(h_c)
    u_new, v_new, u_flux, v_flux, s_flux = [], [], [], [], []
    for j in range(count):
        un = jnp.where(k < d_e[j], u_c[j] + DT * (cor_c * v_c[j] - G * (h_e[j] - h_c[j])), 0.0)
        vn = jnp.where(k < d_n[j], v_c[j] - DT * (cor_c * u_c[j] + G * (h_n[j] - h_c[j])), 0.0)
        vs = jnp.where(k < d_s[j], v_s[j] - DT * (cor_s * u_s[j] + G * (h_c[j] - h_s[j])), 0.0)
        u_new.append(un)
        v_new.append(vn)
        u_flux.append(un * 0.5 * (h_c[j] + h_e[j]))
        v_flux.append(vn * 0.5 * (h_c[j] + h_n[j]))
        s_flux.append(vs * 0.5 * (h_s[j] + h_c[j]))
    w_flux = from_west(u_flux)
    h_new, coefs, links, ratios = [], [], [], []
    for j in range(count):
        fe, fw, fn, fs = u_flux[j], w_flux[j], v_flux[j], s_flux[j]
        hn = h_c[j] - DT * ((fe - fw) + (fn - fs))
        link = jnp.where(k + 1 < d_c[j], DT * diff[j], 0.0)
        q = jnp.where(k < d_c[j], 1.0 / (hn + up[j] + link - up[j] * prev[j]), 0.0)
        r = link * q
        dq = DT * q
        ce = dq * jnp.maximum(-fe, 0.0)
        cw = dq * jnp.maximum(fw, 0.0)
        cn = dq * jnp.maximum(-fn, 0.0)
        cs = dq * jnp.maximum(fs, 0.0)
        out = (jnp.maximum(fe, 0.0) - jnp.minimum(fw, 0.0)) + (jnp.maximum(fn, 0.0) - jnp.minimum(fs, 0.0))
        ca = q * h_c[j] - dq * out
        h_new.append(hn)
        links.append(link)
        ratios.append(r)
        coefs.append((ca, ce, cw, cn, cs, up[j] * q, r))
    return h_new, u_new, v_new, coefs, links, ratios


def forward(coefs, cells, before, joined=True):
    result = []
    for t, (c, s, n) in enumerate(cells):
        e = from_east(c, joined)
        w = from_west(c, joined)
        result.append([
            ((coefs[0][j] * c[j] + coefs[1][j] * e[j]) + (coefs[2][j] * w[j] + coefs[3][j] * n[j]))
            + (coefs[4][j] * s[j] + coefs[5][j] * before[t][j])
            for j in range(len(c))
        ])
    return result


def react(table, s, m):
    outs = []
    for a in range(PER):
        acc = None
        for b in range(PER):
            w = table[s * 64 + a * 8 + b]
            term = [w * x for x in m[b]]
            acc = term if acc is None else [p + q for p, q in zip(acc, term)]
        outs.append(acc)
    return outs


def fill_table(react_ref, table):
    for s in range(2):
        for a in range(PER):
            for b in range(PER):
                v = DT * react_ref[s, a, b] + (1.0 if a == b else 0.0)
                table[s * 64 + a * 8 + b] = jnp.full((8, 128), v, F32)


def zeros_like_tiles(rows, count):
    return [jnp.zeros((rows, 128), F32) for _ in range(count)]


def field_copies(ho, hp, vo, vp, df, off, h_buf, u_buf, v_buf, d_buf, sem):
    copies = []
    part = LV // 2
    other = part - off
    rows = pl.ds(8, 16)
    for j in range(2):
        lanes = pl.ds(128 * j, 128)
        copies.append(pltpu.make_async_copy(ho.at[:, :, lanes], h_buf.at[pl.ds(off, part), j, rows, :], sem.at[0 + j]))
        copies.append(pltpu.make_async_copy(hp.at[:, :, lanes], h_buf.at[pl.ds(other, part), j, rows, :], sem.at[2 + j]))
        copies.append(pltpu.make_async_copy(vo.at[0, :, :, lanes], u_buf.at[pl.ds(off, part), j, rows, :], sem.at[4 + j]))
        copies.append(pltpu.make_async_copy(vp.at[0, :, :, lanes], u_buf.at[pl.ds(other, part), j, rows, :], sem.at[6 + j]))
        copies.append(pltpu.make_async_copy(vo.at[1, :, :, lanes], v_buf.at[pl.ds(off, part), j, rows, :], sem.at[8 + j]))
        copies.append(pltpu.make_async_copy(vp.at[1, :, :, lanes], v_buf.at[pl.ds(other, part), j, rows, :], sem.at[10 + j]))
        copies.append(pltpu.make_async_copy(df.at[:, :, lanes], d_buf.at[:, j, rows, :], sem.at[12 + j]))
    return copies


def tracer_copies(tr, c_buf, sem):
    return [[pltpu.make_async_copy(
        tr.at[pl.ds(8 * s, 8), :, :, pl.ds(128 * j, 128)],
        c_buf.at[pl.ds(8 * s, 8), :, j, pl.ds(8, 16), :], sem.at[2 * s + j]) for j in range(2)] for s in range(2)]


def depth_copies(land, level, l_buf, sem):
    return [pltpu.make_async_copy(x.at[:, pl.ds(128 * j, 128)], l_buf.at[i, j], sem.at[2 * i + j])
            for i, x in enumerate((land, level)) for j in range(2)]


def fill_depth(l_buf, p_buf):
    for j in range(2):
        p_buf[j, 8:24, :] = jnp.where(l_buf[0, j] == 1, l_buf[1, j], 0)


FIELD_SCRATCH = [
    pltpu.VMEM((LV, 2, 32, 128), F32),
    pltpu.VMEM((LV, 2, 32, 128), F32),
    pltpu.VMEM((LV, 2, 32, 128), F32),
    pltpu.VMEM((LV, 2, 32, 128), F32),
    pltpu.SemaphoreType.DMA((14,)),
]
DEPTH_SCRATCH = [
    pltpu.VMEM((2, 2, 16, 128), jnp.int32),
    pltpu.VMEM((2, 32, 128), jnp.int32),
    pltpu.SemaphoreType.DMA((4,)),
]
TRACER_SCRATCH = [
    pltpu.VMEM((NT, LV, 2, 32, 128), F32),
    pltpu.SemaphoreType.DMA((4,)),
]


def pack_lanes(sources):
    lane = lane_iota()
    place, slot = lane & 31, lane >> 5
    acc = None
    for q, (left, right) in enumerate(sources):
        a = pltpu.roll(left, (4 + 32 * q) % 128, 1)
        b = pltpu.roll(right, (28 + 32 * q) % 128, 1)
        x = jnp.where(place < 16, a, b)
        acc = x if acc is None else jnp.where(slot == q, x, acc)
    return acc


def to_east(packed, g):
    return pltpu.roll(packed, (4 * g - 24) % 128, 1)


def to_west(packed, g):
    return pltpu.roll(packed, (4 * g - 4) % 128, 1)


def tracer_pack_kernel(tr, y_up, y_dn, own, x_r, x_l, c_buf, c_sem):
    copies = tracer_copies(tr, c_buf, c_sem)
    for c in copies[0] + copies[1]:
        c.start()
    low = sub_iota() < 4
    place = lane_iota() & 31
    for c in copies[0] + copies[1]:
        c.wait()

    @pl.loop(0, LV, unroll=2)
    def _(k):
        for j in range(2):
            for t in range(PER):
                read = lambda b, r: c_buf[t + b, k, j, r:r + 8, :]
                y_up[t * LV + k, j] = jnp.where(low, read(0, 20), read(PER, 16))
                y_dn[t * LV + k, j] = jnp.where(low, read(0, 8), read(PER, 4))
        for i in range(2):
            rows = slice(8 * i, 8 * i + 8)
            xr, xl = None, None
            for g in range(4):
                packed = pack_lanes([[c_buf[4 * g + q, k, j, 8 + 8 * i:16 + 8 * i, :] for j in range(2)] for q in range(4)])
                own[k, g, rows, :] = packed
                here = place >= 4 * g
                xr = to_east(packed, g) if g == 0 else jnp.where(here, to_east(packed, g), xr)
                xl = to_west(packed, g) if g == 0 else jnp.where(here, to_west(packed, g), xl)
            x_r[k, rows, :] = xr
            x_l[k, rows, :] = xl


def field_pack_kernel(scal, ho, hp, vo, vp, df, land, level, up_in, dn_in, y_up, y_dn, own,
                      h_buf, u_buf, v_buf, d_buf, sem, l_buf, p_buf, l_sem, f_up, f_dn, out_sem):
    off = scal[0] * (LV // 2)
    copies = field_copies(ho, hp, vo, vp, df, off, h_buf, u_buf, v_buf, d_buf, sem) + depth_copies(land, level, l_buf, l_sem)
    for c in copies:
        c.start()
    low = sub_iota() < 4
    for c in copies:
        c.wait()
    fill_depth(l_buf, p_buf)

    def put(index, j, first, second):
        f_up[index, j] = jnp.where(low, first(20), second(16))
        f_dn[index, j] = jnp.where(low, first(8), second(4))

    @pl.loop(0, LV, unroll=4)
    def _(k):
        for j in range(2):
            put(k, j, lambda r: h_buf[k, j, r:r + 8, :], lambda r: u_buf[k, j, r:r + 8, :])
            put(16 + k, j, lambda r: v_buf[k, j, r:r + 8, :], lambda r: d_buf[k, j, r:r + 8, :])

    for j in range(2):
        get = lambda r: p_buf[j, r:r + 8, :].astype(F32)
        put(32, j, get, get)
    leaving = [pltpu.make_async_copy(f, y.at[pl.ds(128, 33)], out_sem.at[i]) for i, (f, y) in enumerate(((f_up, y_up), (f_dn, y_dn)))]
    for c in leaving:
        c.start()

    @pl.loop(0, LV, unroll=4)
    def _(k):
        for i in range(2):
            rows = slice(8 + 8 * i, 16 + 8 * i)
            own[k, 8 * i:8 * i + 8, :] = pack_lanes([[buf[k, j, rows, :] for j in range(2)] for buf in (h_buf, u_buf, v_buf, d_buf)])

    for i in range(2):
        own[LV, 8 * i:8 * i + 8, :] = pack_lanes([[p_buf[j, 8 + 8 * i:16 + 8 * i, :].astype(F32) for j in range(2)]] * 4)
    for c in leaving:
        c.wait()


def inner_kernel(rows_total, scal, tr, ho, hp, vo, vp, df, land, level, reaction, saved_out, saved_f, mid, mid_f,
                 h_buf, u_buf, v_buf, d_buf, sem, l_buf, p_buf, l_sem, c_buf, c_sem, c_alt, solved, coef, table, saved, out_sem):
    off = scal[0] * (LV // 2)
    fields = field_copies(ho, hp, vo, vp, df, off, h_buf, u_buf, v_buf, d_buf, sem)
    depths = depth_copies(land, level, l_buf, l_sem)
    tracer = tracer_copies(tr, c_buf, c_sem)
    for c in depths + fields + tracer[0] + tracer[1]:
        c.start()
    fill_table(reaction, table)
    for c in depths:
        c.wait()
    fill_depth(l_buf, p_buf)
    six = sub_iota() < 6
    rows = lax.broadcasted_iota(jnp.int32, (16, 128), 0) + scal[1]
    cor_c = coriolis_of(rows, rows_total)
    cor_s = coriolis_of(rows - 1, rows_total)
    d_c = [p_buf[j, 8:24, :] for j in range(2)]
    d_e = [jnp.minimum(a, b) for a, b in zip(d_c, from_east(d_c))]
    d_n = [jnp.minimum(d_c[j], p_buf[j, 9:25, :]) for j in range(2)]
    d_s = [jnp.minimum(d_c[j], p_buf[j, 7:23, :]) for j in range(2)]
    for c in fields:
        c.wait()

    def keep(n, read):
        return jnp.where(six, read(4 + n), read(16 - n))

    def keep_fields(n):
        @pl.loop(0, LV)
        def _(k):
            for f, buf in enumerate((h_buf, u_buf, v_buf)):
                for j in range(2):
                    saved_f[n, f, k, j] = keep(n, lambda r: buf[k, j, r:r + 8, :])

    def keep_tracers(n, buf):
        @pl.loop(0, LV)
        def _(k):
            for t in range(NT):
                for j in range(2):
                    saved[n, t, k, j] = keep(n, lambda r: buf[t, k, j, r:r + 8, :])

    keep_fields(0)
    for c in tracer[0] + tracer[1]:
        c.wait()
    keep_tracers(0, c_buf)
    leaving = [pltpu.make_async_copy(saved.at[n], saved_out.at[n], out_sem.at[n]) for n in range(ITERS)]
    leaving[0].start()
    for n in range(1, ITERS + 1):
        src, dst = (c_buf, c_alt) if n % 2 else (c_alt, c_buf)

        def dynamics(k, carry):
            up, prev = carry
            read = lambda buf, r: [buf[k, j, r:r + 16, :] for j in range(2)]
            h_new, u_new, v_new, co, links, ratios = level_step(
                k, read(h_buf, 7), read(h_buf, 8), read(h_buf, 9), read(u_buf, 7), read(u_buf, 8),
                read(v_buf, 7), read(v_buf, 8), (d_c, d_e, d_n, d_s), cor_c, cor_s, read(d_buf, 8), up, prev)
            for j in range(2):
                h_buf[k, j, 8:24, :] = h_new[j]
                u_buf[k, j, 8:24, :] = u_new[j]
                v_buf[k, j, 8:24, :] = v_new[j]
                for c in range(7):
                    coef[c, k, j] = co[j][c]
            return links, ratios

        lax.fori_loop(0, LV, dynamics, (zeros_like_tiles(16, 2), zeros_like_tiles(16, 2)), unroll=4)
        if n < ITERS:
            keep_fields(n)
        else:
            @pl.loop(0, LV)
            def _(k):
                for f, buf in enumerate((h_buf, u_buf, v_buf)):
                    for j in range(2):
                        mid_f[f, k, j] = buf[k, j, 12:20, :]

        for r0 in ((8, 16) if n < ITERS else (12,)):
            @pl.loop(0, 2)
            def _(s):
                def down(k, before):
                    co = [[coef[c, k, j, r0 - 8:r0, :] for j in range(2)] for c in range(6)]
                    read = lambda t, r: [src[s * PER + t, k, j, r:r + 8, :] for j in range(2)]
                    now = forward(co, [(read(t, r0), read(t, r0 - 1), read(t, r0 + 1)) for t in range(PER)], before)
                    for t in range(PER):
                        for j in range(2):
                            solved[k, t, j] = now[t][j]
                    return now

                lax.fori_loop(0, LV, down, [zeros_like_tiles(8, 2) for _ in range(PER)], unroll=8)

                def upward(i, m):
                    k = LV - 1 - i
                    r = [coef[6, k, j, r0 - 8:r0, :] for j in range(2)]
                    m = [[solved[k, t, j] + r[j] * m[t][j] for j in range(2)] for t in range(PER)]
                    outs = react(table, s, m)
                    for t in range(PER):
                        for j in range(2):
                            if n < ITERS:
                                dst[s * PER + t, k, j, r0:r0 + 8, :] = outs[t][j]
                            else:
                                mid[s * PER + t, k, j] = outs[t][j]
                    return m

                lax.fori_loop(0, LV, upward, [zeros_like_tiles(8, 2) for _ in range(PER)], unroll=4)
        if n < ITERS:
            keep_tracers(n, dst)
            leaving[n].start()
    for c in leaving:
        c.wait()


def halo_pack_kernel(y_s, y_n, own_f, r_own, l_own, halo, x_r, x_l, s_buf, n_buf, sem):
    copies = [pltpu.make_async_copy(y_s, s_buf, sem.at[0]), pltpu.make_async_copy(y_n, n_buf, sem.at[1])]
    for c in copies:
        c.start()
    low = sub_iota() < 4
    place = lane_iota() & 31
    for i in range(2):
        rows = slice(8 * i, 8 * i + 8)
        x_r[LV, rows, :] = to_east(own_f[LV, rows, :], 4)
        x_l[LV, rows, :] = to_west(own_f[LV, rows, :], 4)

    @pl.loop(0, LV, unroll=4)
    def _(k):
        for i in range(2):
            rows = slice(8 * i, 8 * i + 8)
            x_r[k, rows, :] = jnp.where(place >= 16, to_east(own_f[k, rows, :], 4), r_own[k, rows, :])
            x_l[k, rows, :] = jnp.where(place >= 16, to_west(own_f[k, rows, :], 4), l_own[k, rows, :])

    for c in copies:
        c.wait()

    def pair(index, j):
        ys, yn = s_buf[index, j], n_buf[index, j]
        return jnp.where(low, ys, pltpu.roll(yn, 4, 0)), jnp.where(low, pltpu.roll(ys, 4, 0), yn)

    @pl.loop(0, LV, unroll=2)
    def _(k):
        pairs = [[pair(t * LV + k, j) for j in range(2)] for t in range(PER)]
        hu = [pair(128 + k, j) for j in range(2)]
        vd = [pair(144 + k, j) for j in range(2)]
        groups = [[[pairs[4 * (g % 2) + q][j][g // 2] for j in range(2)] for q in range(4)] for g in range(4)]
        groups.append([[x[j][w] for j in range(2)] for x in (hu, vd) for w in range(2)])
        xr, xl = None, None
        for g in range(5):
            packed = pack_lanes(groups[g])
            halo[k, g] = packed
            here = place >= 4 * g
            xr = to_east(packed, g) if g == 0 else jnp.where(here, to_east(packed, g), xr)
            xl = to_west(packed, g) if g == 0 else jnp.where(here, to_west(packed, g), xl)
        x_r[k, 16:24, :] = xr
        x_l[k, 16:24, :] = xl

    packed = pack_lanes([[pair(160, j)[0] for j in range(2)]] * 4)
    for g in range(5):
        halo[LV, g] = packed
    x_r[LV, 16:24, :] = to_east(packed, 4)
    x_l[LV, 16:24, :] = to_west(packed, 4)


def edge_kernel(rows_total, scal, saved, saved_f, south, north, df, land, level, reaction, out_c, out_f,
                c_buf, f_buf, d_buf, l_buf, p_buf, l_sem, solved, coef, table, y_s, y_n, sem):
    copies = [pltpu.make_async_copy(south, y_s, sem.at[10]), pltpu.make_async_copy(north, y_n, sem.at[11])]
    copies += depth_copies(land, level, l_buf, l_sem)
    for n in range(ITERS):
        copies.append(pltpu.make_async_copy(saved_f.at[n], f_buf.at[n, :, :, :, pl.ds(0, 8), :], sem.at[n]))
    for j in range(2):
        copies.append(pltpu.make_async_copy(df.at[:, :, pl.ds(128 * j, 128)], d_buf.at[:, j, pl.ds(8, 16), :], sem.at[4 + j]))
    tracer = [pltpu.make_async_copy(saved.at[n], c_buf.at[n, :, :, :, pl.ds(0, 8), :], sem.at[6 + n]) for n in range(ITERS)]
    for c in copies + tracer:
        c.start()
    fill_table(reaction, table)
    sub = sub_iota()
    low = sub < 4
    for c in copies:
        c.wait()
    fill_depth(l_buf, p_buf)
    tracer[0].wait()

    def put(ref, y, half, south):
        if half != (0 if south else 1):
            y = pltpu.roll(y, 4, 0)
        if south:
            pltpu.store(ref.at[pl.ds(0, 8), :], y, mask=low)
        else:
            pltpu.store(ref.at[pl.ds(4, 8), :], y, mask=jnp.logical_not(low))

    @pl.loop(0, LV, unroll=2)
    def _(k):
        for j in range(2):
            for t in range(PER):
                ys, yn = y_s[t * LV + k, j], y_n[t * LV + k, j]
                for half in range(2):
                    put(c_buf.at[0, t + PER * half, k, j], ys, half, True)
                    put(c_buf.at[0, t + PER * half, k, j], yn, half, False)
            for f, (index, half) in enumerate(((128, 0), (128, 1), (144, 0))):
                put(f_buf.at[0, f, k, j], y_s[index + k, j], half, True)
                put(f_buf.at[0, f, k, j], y_n[index + k, j], half, False)
            ys, yn = y_s[144 + k, j], y_n[144 + k, j]
            pltpu.store(d_buf.at[k, j, pl.ds(0, 8), :], ys, mask=jnp.logical_not(low))
            pltpu.store(d_buf.at[k, j, pl.ds(24, 8), :], pltpu.roll(yn, 4, 0), mask=low)

    for j in range(2):
        ys, yn = y_s[160, j].astype(jnp.int32), y_n[160, j].astype(jnp.int32)
        pltpu.store(p_buf.at[j, pl.ds(0, 8), :], ys, mask=jnp.logical_not(low))
        pltpu.store(p_buf.at[j, pl.ds(24, 8), :], yn, mask=low)

    def gather(read, shift):
        return jnp.where(low, read(shift), read(shift + 2))

    for n in range(1, ITERS + 1):
        if n < ITERS:
            tracer[n].wait()

        def at(buf, j, shift):
            return jnp.where(low, buf[j, 4 + n + shift:12 + n + shift, :], buf[j, 20 - n + shift:28 - n + shift, :])

        row = jnp.where(low, sub - 4 + n, sub + 12 - n) + scal[1]
        cor_c = coriolis_of(row, rows_total)
        cor_s = coriolis_of(row - 1, rows_total)
        d_c = [at(p_buf, j, 0) for j in range(2)]
        d_e = [jnp.minimum(a, b) for a, b in zip(d_c, from_east(d_c))]
        d_n = [jnp.minimum(d_c[j], at(p_buf, j, 1)) for j in range(2)]
        d_s = [jnp.minimum(d_c[j], at(p_buf, j, -1)) for j in range(2)]

        def dynamics(k, carry):
            up, prev = carry
            read = lambda f, shift: [gather(lambda r: f_buf[n - 1, f, k, j, r:r + 8, :], shift) for j in range(2)]
            diff = [at(d_buf.at[k], j, 0) for j in range(2)]
            h_new, u_new, v_new, co, links, ratios = level_step(
                k, read(0, 0), read(0, 1), read(0, 2), read(1, 0), read(1, 1), read(2, 0), read(2, 1),
                (d_c, d_e, d_n, d_s), cor_c, cor_s, diff, up, prev)
            for j in range(2):
                for f, x in enumerate((h_new[j], u_new[j], v_new[j])):
                    if n < ITERS:
                        pltpu.store(f_buf.at[n, f, k, j, pl.ds(0, 8), :], x, mask=low)
                        pltpu.store(f_buf.at[n, f, k, j, pl.ds(4, 8), :], x, mask=jnp.logical_not(low))
                    else:
                        out_f[f, k, j] = x
                for c in range(7):
                    coef[c, k, j] = co[j][c]
            return links, ratios

        lax.fori_loop(0, LV, dynamics, (zeros_like_tiles(8, 2), zeros_like_tiles(8, 2)), unroll=8)

        @pl.loop(0, 2)
        def _(s):
            def down(k, before):
                co = [[coef[c, k, j] for j in range(2)] for c in range(6)]

                def read(t, shift):
                    return [gather(lambda r: c_buf[n - 1, s * PER + t, k, j, r:r + 8, :], shift) for j in range(2)]

                now = forward(co, [(read(t, 1), read(t, 0), read(t, 2)) for t in range(PER)], before)
                for t in range(PER):
                    for j in range(2):
                        solved[k, t, j] = now[t][j]
                return now

            lax.fori_loop(0, LV, down, [zeros_like_tiles(8, 2) for _ in range(PER)], unroll=8)

            def upward(i, m):
                k = LV - 1 - i
                r = [coef[6, k, j] for j in range(2)]
                m = [[solved[k, t, j] + r[j] * m[t][j] for j in range(2)] for t in range(PER)]
                outs = react(table, s, m)
                for t in range(PER):
                    for j in range(2):
                        if n < ITERS:
                            pltpu.store(c_buf.at[n, s * PER + t, k, j, pl.ds(0, 8), :], outs[t][j], mask=low)
                            pltpu.store(c_buf.at[n, s * PER + t, k, j, pl.ds(4, 8), :], outs[t][j], mask=jnp.logical_not(low))
                        else:
                            out_c[s * PER + t, k, j] = outs[t][j]
                return m

            lax.fori_loop(0, LV, upward, [zeros_like_tiles(8, 2) for _ in range(PER)], unroll=4)


def strip_kernel(rows_total, scal, own, own_f, halo, x_w, x_e, reaction, mid_in, mid_f, edge_in, edge_f, out, out_h, out_v,
                 c_buf, c_alt, h_buf, u_buf, v_buf, d_buf, p_buf, solved, coef, table, mid, edge, out_c, sem):
    arriving = [pltpu.make_async_copy(mid_in, mid, sem.at[0]), pltpu.make_async_copy(edge_in, edge, sem.at[1])]
    for c in arriving:
        c.start()
    lane = lane_iota()
    place = lane & 31
    slot = lane >> 5
    low = sub_iota() < 4
    for s in range(2):
        for go in range(2):
            for gi in range(2):
                for rho in range(4):
                    v = jnp.zeros((8, 128), F32)
                    for q in range(4):
                        a, b = 4 * go + q, 4 * gi + (q - rho) % 4
                        w = DT * reaction[s, a, b] + (1.0 if a == b else 0.0)
                        v = jnp.where(slot == q, jnp.full((8, 128), w, F32), v)
                    table[((s * 2 + go) * 2 + gi) * 4 + rho] = v

    def whole(k, g, i, xg):
        rows = slice(8 * i, 8 * i + 8)
        a = pltpu.roll(x_w[k, rows, :], (-4 * xg) % 128, 1)
        b = pltpu.roll(x_e[k, rows, :], (28 - 4 * xg) % 128, 1)
        if i == 2:
            body = halo[k, g]
        elif g == 4:
            body = own_f[k, rows, :]
        else:
            body = own[k, g, rows, :]
        return jnp.where(place < 4, a, jnp.where(place >= 28, b, body))

    def put(ref, i, x):
        if i < 2:
            ref[12 + 8 * i:20 + 8 * i, :] = x
        else:
            pltpu.store(ref.at[pl.ds(8, 8), :], x, mask=low)
            pltpu.store(ref.at[pl.ds(24, 8), :], x, mask=jnp.logical_not(low))

    @pl.loop(0, LV, unroll=4)
    def _(k):
        for i in range(3):
            for g in range(4):
                put(c_buf.at[g, k], i, whole(k, g, i, g))
            x = whole(k, 4, i, 4)
            for f, buf in enumerate((h_buf, u_buf, v_buf, d_buf)):
                y = jnp.where(lane < 32, pltpu.roll(x, (-32 * f) % 128, 1), 0.0)
                y = y + pltpu.roll(y, 32, 1)
                y = y + pltpu.roll(y, 64, 1)
                put(buf.at[k], i, y)

    for i in range(3):
        put(p_buf, i, whole(LV, 4, i, 4).astype(jnp.int32))

    rows = lax.broadcasted_iota(jnp.int32, (24, 128), 0) - 4 + scal[1]
    cor_c = coriolis_of(rows, rows_total)
    cor_s = coriolis_of(rows - 1, rows_total)
    d_c = [p_buf[8:32, :]]
    d_e = [jnp.minimum(d_c[0], from_east(d_c)[0])]
    d_n = [jnp.minimum(d_c[0], p_buf[9:33, :])]
    d_s = [jnp.minimum(d_c[0], p_buf[7:31, :])]

    for n in range(1, ITERS + 1):
        src, dst = (c_buf, c_alt) if n % 2 else (c_alt, c_buf)

        def dynamics(k, carry):
            up, prev = carry
            read = lambda buf, r: [buf[k, r:r + 24, :]]
            h_new, u_new, v_new, co, links, ratios = level_step(
                k, read(h_buf, 7), read(h_buf, 8), read(h_buf, 9), read(u_buf, 7), read(u_buf, 8),
                read(v_buf, 7), read(v_buf, 8), (d_c, d_e, d_n, d_s), cor_c, cor_s, read(d_buf, 8), up, prev)
            h_buf[k, 8:32, :] = h_new[0]
            u_buf[k, 8:32, :] = u_new[0]
            v_buf[k, 8:32, :] = v_new[0]
            for c in range(7):
                coef[c, k] = co[0][c]
            return links, ratios

        lax.fori_loop(0, LV, dynamics, (zeros_like_tiles(24, 1), zeros_like_tiles(24, 1)), unroll=8)

        starts = (8, 16, 24) if n < ITERS else (12, 20)
        tiles = len(starts)

        def down(k, before):
            co = [[coef[c, k, r0 - 8:r0, :] for r0 in starts] for c in range(6)]
            read = lambda t, shift: [src[t, k, r0 + shift:r0 + shift + 8, :] for r0 in starts]
            now = forward(co, [(read(t, 0), read(t, -1), read(t, 1)) for t in range(4)], before, joined=False)
            for t in range(4):
                for i in range(tiles):
                    solved[k, t, i] = now[t][i]
            return now

        lax.fori_loop(0, LV, down, [zeros_like_tiles(8, tiles) for _ in range(4)], unroll=4)

        def upward(i, m):
            k = LV - 1 - i
            r = [coef[6, k, r0 - 8:r0, :] for r0 in starts]
            m = [[solved[k, t, i] + r[i] * m[t][i] for i in range(tiles)] for t in range(4)]
            for i, r0 in enumerate(starts):
                turned = [[m[t][i]] + [pltpu.roll(m[t][i], 32 * rho, 1) for rho in range(1, 4)] for t in range(4)]
                for s in range(2):
                    for go in range(2):
                        acc = None
                        for gi in range(2):
                            for rho in range(4):
                                term = table[((s * 2 + go) * 2 + gi) * 4 + rho] * turned[2 * s + gi][rho]
                                acc = term if acc is None else acc + term
                        dst[2 * s + go, k, r0:r0 + 8, :] = acc
            return m

        lax.fori_loop(0, LV, upward, [zeros_like_tiles(8, tiles) for _ in range(4)], unroll=4)

    final = c_buf if ITERS % 2 == 0 else c_alt

    def merge(inner, outer, strip, q, j, i):
        turned = pltpu.roll(inner, 4, 0)
        body = jnp.where(low, outer, turned) if i == 0 else jnp.where(low, turned, outer)
        if j == 0:
            return jnp.where(lane < 4, pltpu.roll(strip, (-(32 * q + 4)) % 128, 1), body)
        return jnp.where(lane >= 124, pltpu.roll(strip, (100 - 32 * q) % 128, 1), body)

    for c in arriving:
        c.wait()
    leaving = []
    for part in range(4):
        @pl.loop(4 * part, 4 * part + 4, unroll=2)
        def _(k):
            for t in range(NT):
                for i in range(2):
                    strip = final[t // 4, k, 12 + 8 * i:20 + 8 * i, :]
                    for j in range(2):
                        out_c[t, k, 8 * i:8 * i + 8, 128 * j:128 * j + 128] = merge(
                            mid[t, k, j], edge[t, k, j], strip, t % 4, j, i)
        levels = pl.ds(4 * part, 4)
        leaving.append(pltpu.make_async_copy(out_c.at[:, levels], out.at[:, levels], sem.at[2 + part]))
        leaving[part].start()

    off = scal[0] * (LV // 2)

    @pl.loop(0, LV // 2, unroll=4)
    def _(k):
        for f, buf in enumerate((h_buf, u_buf, v_buf)):
            for i in range(2):
                strip = buf[k + off, 12 + 8 * i:20 + 8 * i, :]
                for j in range(2):
                    x = merge(mid_f[f, k + off, j], edge_f[f, k + off, j], strip, 0, j, i)
                    if f == 0:
                        out_h[k, 8 * i:8 * i + 8, 128 * j:128 * j + 128] = x
                    else:
                        out_v[f - 1, k, 8 * i:8 * i + 8, 128 * j:128 * j + 128] = x
    for c in leaving:
        c.wait()


def sds(*shape):
    return jax.ShapeDtypeStruct(shape, F32)


def body(tracers, thickness, velocity, diffusivity, reaction, land_mask, level_count):
    rows_local = thickness.shape[1]
    rows_total = rows_local * lax.axis_size("ty")
    set_index = lax.axis_index("set").astype(jnp.int32)
    row_start = lax.axis_index("ty").astype(jnp.int32) * rows_local
    scal = jnp.stack([set_index, row_start])
    params = pltpu.CompilerParams(vmem_limit_bytes=VMEM_LIMIT)
    swap = [(0, 1), (1, 0)]
    h_pair = lax.ppermute(thickness, "set", swap)
    v_pair = lax.ppermute(velocity, "set", swap)
    up_part, dn_part, own, r_own, l_own = pl.pallas_call(
        tracer_pack_kernel,
        out_shape=[sds(161, 2, 8, 128), sds(161, 2, 8, 128), sds(LV, 4, 16, 128), sds(LV, 16, 128), sds(LV, 16, 128)],
        in_specs=[ANY], out_specs=[VMEM] * 5, scratch_shapes=TRACER_SCRATCH,
        compiler_params=params, name="tracer_pack")(tracers)
    h_pair, v_pair, up_part, dn_part = lax.optimization_barrier((h_pair, v_pair, up_part, dn_part))
    fields = (thickness, h_pair, velocity, v_pair, diffusivity, land_mask, level_count)
    y_up, y_dn, own_f = pl.pallas_call(
        field_pack_kernel, out_shape=[sds(161, 2, 8, 128), sds(161, 2, 8, 128), sds(LV + 1, 16, 128)],
        in_specs=[SMEM] + [ANY] * 9, out_specs=[ANY, ANY, VMEM], input_output_aliases={8: 0, 9: 1},
        scratch_shapes=FIELD_SCRATCH + DEPTH_SCRATCH + [
            pltpu.VMEM((33, 2, 8, 128), F32), pltpu.VMEM((33, 2, 8, 128), F32), pltpu.SemaphoreType.DMA((2,))],
        compiler_params=params, name="field_pack")(scal, *fields, up_part, dn_part)
    ty = lax.axis_size("ty")
    north = [(i, i + 1) for i in range(ty - 1)]
    south = [(j, i) for i, j in north]
    y_s = lax.ppermute(y_up, "ty", north)
    y_n = lax.ppermute(y_dn, "ty", south)
    saved, saved_f, mid, mid_f = pl.pallas_call(
        lambda *a: inner_kernel(rows_total, *a),
        out_shape=[sds(ITERS, NT, LV, 2, 8, 128), sds(ITERS, 3, LV, 2, 8, 128), sds(NT, LV, 2, 8, 128), sds(3, LV, 2, 8, 128)],
        in_specs=[SMEM] + [ANY] * 8 + [SMEM], out_specs=[ANY] + [VMEM] * 3,
        scratch_shapes=FIELD_SCRATCH + DEPTH_SCRATCH + TRACER_SCRATCH + [
            pltpu.VMEM((NT, LV, 2, 32, 128), F32),
            pltpu.VMEM((LV, PER, 2, 8, 128), F32),
            pltpu.VMEM((7, LV, 2, 16, 128), F32),
            pltpu.VMEM((128, 8, 128), F32),
            pltpu.VMEM((ITERS, NT, LV, 2, 8, 128), F32),
            pltpu.SemaphoreType.DMA((ITERS,))],
        compiler_params=params, name="inner")(scal, tracers, *fields, reaction)
    y_s, y_n, mid_f = lax.optimization_barrier((y_s, y_n, mid_f))
    halo, x_r, x_l = pl.pallas_call(
        halo_pack_kernel, out_shape=[sds(LV + 1, 5, 8, 128), sds(LV + 1, 24, 128), sds(LV + 1, 24, 128)],
        in_specs=[ANY, ANY] + [VMEM] * 3, out_specs=[VMEM] * 3,
        scratch_shapes=[pltpu.VMEM((161, 2, 8, 128), F32), pltpu.VMEM((161, 2, 8, 128), F32), pltpu.SemaphoreType.DMA((2,))],
        compiler_params=params, name="halo_pack")(y_s, y_n, own_f, r_own, l_own)
    tx = lax.axis_size("tx")
    east = [(i, (i + 1) % tx) for i in range(tx)]
    west = [(j, i) for i, j in east]
    x_w = lax.ppermute(x_r, "tx", east)
    x_e = lax.ppermute(x_l, "tx", west)
    edge, edge_f = pl.pallas_call(
        lambda *a: edge_kernel(rows_total, *a),
        out_shape=[sds(NT, LV, 2, 8, 128), sds(3, LV, 2, 8, 128)],
        in_specs=[SMEM] + [ANY] * 7 + [SMEM], out_specs=[VMEM] * 2,
        scratch_shapes=[
            pltpu.VMEM((ITERS, NT, LV, 2, 16, 128), F32),
            pltpu.VMEM((ITERS, 3, LV, 2, 16, 128), F32),
            pltpu.VMEM((LV, 2, 32, 128), F32)] + DEPTH_SCRATCH + [
            pltpu.VMEM((LV, PER, 2, 8, 128), F32),
            pltpu.VMEM((7, LV, 2, 8, 128), F32),
            pltpu.VMEM((128, 8, 128), F32),
            pltpu.VMEM((161, 2, 8, 128), F32),
            pltpu.VMEM((161, 2, 8, 128), F32),
            pltpu.SemaphoreType.DMA((12,))],
        compiler_params=params, name="edge")(scal, saved, saved_f, y_s, y_n, diffusivity, land_mask, level_count, reaction)
    return pl.pallas_call(
        lambda *a: strip_kernel(rows_total, *a),
        out_shape=[sds(*tracers.shape), sds(*thickness.shape), sds(*velocity.shape)],
        in_specs=[SMEM] + [VMEM] * 5 + [SMEM, ANY, VMEM, ANY, VMEM], out_specs=[ANY, VMEM, VMEM],
        scratch_shapes=[
            pltpu.VMEM((4, LV, 40, 128), F32),
            pltpu.VMEM((4, LV, 40, 128), F32),
            pltpu.VMEM((LV, 40, 128), F32),
            pltpu.VMEM((LV, 40, 128), F32),
            pltpu.VMEM((LV, 40, 128), F32),
            pltpu.VMEM((LV, 40, 128), F32),
            pltpu.VMEM((40, 128), jnp.int32),
            pltpu.VMEM((LV, 4, 3, 8, 128), F32),
            pltpu.VMEM((7, LV, 24, 128), F32),
            pltpu.VMEM((32, 8, 128), F32),
            pltpu.VMEM((NT, LV, 2, 8, 128), F32),
            pltpu.VMEM((NT, LV, 2, 8, 128), F32),
            pltpu.VMEM((NT, LV, 16, 256), F32),
            pltpu.SemaphoreType.DMA((6,))],
        compiler_params=params, name="strips")(scal, own, own_f, halo, x_w, x_e, reaction, mid, mid_f, edge, edge_f)


def solution(mesh):
    placed = (
        P("set", None, "ty", "tx"),
        P("set", "ty", "tx"),
        P(None, "set", "ty", "tx"),
        P(None, "ty", "tx"),
        P("set", None, None),
        P("ty", "tx"),
        P("ty", "tx"),
    )

    def whole(*args):
        return tuple(body(*args))

    return jax.shard_map(
        whole,
        mesh=mesh,
        in_specs=placed,
        out_specs=(P("set", None, "ty", "tx"), P("set", "ty", "tx"), P(None, "set", "ty", "tx")),
        check_vma=False,
    )
```

```python
import jax
import jax.numpy as jnp
from jax import lax
from jax.experimental import pallas as pl
from jax.experimental.pallas import tpu as pltpu
from jax.sharding import PartitionSpec as P

ITERS = 4
DT = 0.2
G = 1.0
ROTATION = 0.5
LV = 16
NT = 16
PER = 8
F32 = jnp.float32
ANY = pl.BlockSpec(memory_space=pl.ANY)
SMEM = pl.BlockSpec(memory_space=pltpu.SMEM)
VMEM = pl.BlockSpec(memory_space=pltpu.VMEM)


def sub_iota(rows=8):
    return lax.broadcasted_iota(jnp.int32, (rows, 128), 0)


def lane_iota(rows=8):
    return lax.broadcasted_iota(jnp.int32, (rows, 128), 1)


def from_east(tiles, joined=True):
    rolled = [pltpu.roll(x, 127, 1) for x in tiles]
    lane = lane_iota(tiles[0].shape[0])
    last = len(tiles) - 1
    return [rolled[i] if i == last or not joined else jnp.where(lane == 127, rolled[i + 1], rolled[i]) for i in range(last + 1)]


def from_west(tiles, joined=True):
    rolled = [pltpu.roll(x, 1, 1) for x in tiles]
    lane = lane_iota(tiles[0].shape[0])
    return [rolled[i] if i == 0 or not joined else jnp.where(lane == 0, rolled[i - 1], rolled[i]) for i in range(len(tiles))]


def coriolis_of(row, rows_total):
    return ROTATION * (2.0 * (row.astype(F32) + 0.5) / rows_total - 1.0)


def level_step(k, h_s, h_c, h_n, u_s, u_c, v_s, v_c, deep, cor_c, cor_s, diff, up, prev):
    d_c, d_e, d_n, d_s = deep
    h_e = from_east(h_c)
    count = len(h_c)
    u_new, v_new, u_flux, v_flux, s_flux = [], [], [], [], []
    for j in range(count):
        un = jnp.where(k < d_e[j], u_c[j] + DT * (cor_c * v_c[j] - G * (h_e[j] - h_c[j])), 0.0)
        vn = jnp.where(k < d_n[j], v_c[j] - DT * (cor_c * u_c[j] + G * (h_n[j] - h_c[j])), 0.0)
        vs = jnp.where(k < d_s[j], v_s[j] - DT * (cor_s * u_s[j] + G * (h_c[j] - h_s[j])), 0.0)
        u_new.append(un)
        v_new.append(vn)
        u_flux.append(un * 0.5 * (h_c[j] + h_e[j]))
        v_flux.append(vn * 0.5 * (h_c[j] + h_n[j]))
        s_flux.append(vs * 0.5 * (h_s[j] + h_c[j]))
    w_flux = from_west(u_flux)
    h_new, coefs, links, ratios = [], [], [], []
    for j in range(count):
        fe, fw, fn, fs = u_flux[j], w_flux[j], v_flux[j], s_flux[j]
        hn = h_c[j] - DT * ((fe - fw) + (fn - fs))
        link = jnp.where(k + 1 < d_c[j], DT * diff[j], 0.0)
        q = jnp.where(k < d_c[j], 1.0 / (hn + up[j] + link - up[j] * prev[j]), 0.0)
        r = link * q
        dq = DT * q
        ce = dq * jnp.maximum(-fe, 0.0)
        cw = dq * jnp.maximum(fw, 0.0)
        cn = dq * jnp.maximum(-fn, 0.0)
        cs = dq * jnp.maximum(fs, 0.0)
        out = (jnp.maximum(fe, 0.0) - jnp.minimum(fw, 0.0)) + (jnp.maximum(fn, 0.0) - jnp.minimum(fs, 0.0))
        ca = q * h_c[j] - dq * out
        h_new.append(hn)
        links.append(link)
        ratios.append(r)
        coefs.append((ca, ce, cw, cn, cs, up[j] * q, r))
    return h_new, u_new, v_new, coefs, links, ratios


def forward(coefs, cells, before, joined=True):
    result = []
    for t, (c, s, n) in enumerate(cells):
        e = from_east(c, joined)
        w = from_west(c, joined)
        result.append([
            ((coefs[0][j] * c[j] + coefs[1][j] * e[j]) + (coefs[2][j] * w[j] + coefs[3][j] * n[j]))
            + (coefs[4][j] * s[j] + coefs[5][j] * before[t][j])
            for j in range(len(c))
        ])
    return result


def react(table, s, m):
    outs = []
    for a in range(PER):
        acc = None
        for b in range(PER):
            w = table[s * 64 + a * 8 + b]
            term = [w * x for x in m[b]]
            acc = term if acc is None else [p + q for p, q in zip(acc, term)]
        outs.append(acc)
    return outs


def zeros_like_tiles(rows, count):
    return [jnp.zeros((rows, 128), F32) for _ in range(count)]


def pack_lanes(sources):
    lane = lane_iota()
    place, slot = lane & 31, lane >> 5
    acc = None
    for q, (left, right) in enumerate(sources):
        a = pltpu.roll(left, (4 + 32 * q) % 128, 1)
        b = pltpu.roll(right, (28 + 32 * q) % 128, 1)
        x = jnp.where(place < 16, a, b)
        acc = x if acc is None else jnp.where(slot == q, x, acc)
    return acc


def to_east(packed, g):
    return pltpu.roll(packed, (4 * g - 24) % 128, 1)


def to_west(packed, g):
    return pltpu.roll(packed, (4 * g - 4) % 128, 1)


def tracer_pack_kernel(tr, reaction, y_up, y_dn, own, x_r, x_l, c_buf, kept, table, s_table, sem):
    copies = [pltpu.make_async_copy(
        tr.at[pl.ds(8 * s, 8), :, :, pl.ds(128 * j, 128)],
        c_buf.at[pl.ds(8 * s, 8), :, j, pl.ds(8, 16), :], sem.at[2 * s + j]) for s in range(2) for j in range(2)]
    for c in copies:
        c.start()
    low = sub_iota() < 4
    place = lane_iota() & 31
    slot = lane_iota() >> 5
    for s in range(2):
        for a in range(PER):
            for b in range(PER):
                v = DT * reaction[s, a, b] + (1.0 if a == b else 0.0)
                table[s * 64 + a * 8 + b] = jnp.full((8, 128), v, F32)
    for s in range(2):
        for go in range(2):
            for gi in range(2):
                for rho in range(4):
                    v = jnp.zeros((8, 128), F32)
                    for q in range(4):
                        a, b = 4 * go + q, 4 * gi + (q - rho) % 4
                        w = DT * reaction[s, a, b] + (1.0 if a == b else 0.0)
                        v = jnp.where(slot == q, jnp.full((8, 128), w, F32), v)
                    s_table[((s * 2 + go) * 2 + gi) * 4 + rho] = v
    for c in copies:
        c.wait()

    @pl.loop(0, LV, unroll=2)
    def _(k):
        for j in range(2):
            for t in range(PER):
                read = lambda b, r: c_buf[t + b, k, j, r:r + 8, :]
                y_up[t * LV + k, j] = jnp.where(low, read(0, 20), read(PER, 16))
                y_dn[t * LV + k, j] = jnp.where(low, read(0, 8), read(PER, 4))
            for t in range(NT):
                kept[t, k, j] = keep_rows(0, lambda r: c_buf[t, k, j, r:r + 8, :])
        for i in range(2):
            rows = slice(8 * i, 8 * i + 8)
            xr, xl = None, None
            for g in range(4):
                packed = pack_lanes([[c_buf[4 * g + q, k, j, 8 + 8 * i:16 + 8 * i, :] for j in range(2)] for q in range(4)])
                own[k, g, rows, :] = packed
                here = place >= 4 * g
                xr = to_east(packed, g) if g == 0 else jnp.where(here, to_east(packed, g), xr)
                xl = to_west(packed, g) if g == 0 else jnp.where(here, to_west(packed, g), xl)
            x_r[k, rows, :] = xr
            x_l[k, rows, :] = xl


def keep_rows(n, read):
    return jnp.where(sub_iota() < 6, read(4 + n), read(16 - n))


def field_pack_kernel(scal, ho, hp, vo, vp, df, land, level, up_in, dn_in, y_up, y_dn, own, h_buf, u_buf, v_buf, d_buf, p_buf,
                      f_up, f_dn, l_buf, sem, out_sem):
    off = scal[0] * (LV // 2)
    part = LV // 2
    rows = pl.ds(8, 16)
    copies = []
    for j in range(2):
        lanes = pl.ds(128 * j, 128)
        for i, (h, v, at) in enumerate(((ho, vo, off), (hp, vp, part - off))):
            levels = pl.ds(at, part)
            copies.append(pltpu.make_async_copy(h.at[:, :, lanes], h_buf.at[levels, j, rows, :], sem.at[6 * j + 3 * i]))
            copies.append(pltpu.make_async_copy(v.at[0, :, :, lanes], u_buf.at[levels, j, rows, :], sem.at[6 * j + 3 * i + 1]))
            copies.append(pltpu.make_async_copy(v.at[1, :, :, lanes], v_buf.at[levels, j, rows, :], sem.at[6 * j + 3 * i + 2]))
        copies.append(pltpu.make_async_copy(df.at[:, :, lanes], d_buf.at[:, j, rows, :], sem.at[12 + j]))
        copies.append(pltpu.make_async_copy(land.at[:, lanes], l_buf.at[0, j], sem.at[14 + j]))
        copies.append(pltpu.make_async_copy(level.at[:, lanes], l_buf.at[1, j], sem.at[16 + j]))
    for c in copies:
        c.start()
    low = sub_iota() < 4
    for c in copies:
        c.wait()

    for j in range(2):
        p_buf[j, 8:24, :] = jnp.where(l_buf[0, j] == 1, l_buf[1, j], 0)

    def put(index, j, first, second):
        f_up[index, j] = jnp.where(low, first(20), second(16))
        f_dn[index, j] = jnp.where(low, first(8), second(4))

    @pl.loop(0, LV, unroll=4)
    def _(k):
        for j in range(2):
            put(k, j, lambda r: h_buf[k, j, r:r + 8, :], lambda r: u_buf[k, j, r:r + 8, :])
            put(16 + k, j, lambda r: v_buf[k, j, r:r + 8, :], lambda r: d_buf[k, j, r:r + 8, :])

    for j in range(2):
        get = lambda r: p_buf[j, r:r + 8, :].astype(F32)
        put(32, j, get, get)
    leaving = [pltpu.make_async_copy(f, y.at[pl.ds(128, 33)], out_sem.at[i]) for i, (f, y) in enumerate(((f_up, y_up), (f_dn, y_dn)))]
    for c in leaving:
        c.start()

    @pl.loop(0, LV, unroll=4)
    def _(k):
        for i in range(2):
            own[k, 8 * i:8 * i + 8, :] = pack_lanes(
                [[buf[k, j, 8 + 8 * i:16 + 8 * i, :] for j in range(2)] for buf in (h_buf, u_buf, v_buf, d_buf)])

    for i in range(2):
        own[LV, 8 * i:8 * i + 8, :] = pack_lanes([[p_buf[j, 8 + 8 * i:16 + 8 * i, :].astype(F32) for j in range(2)]] * 4)
    for c in leaving:
        c.wait()


def inner_kernel(rows_total, scal, c_first, h_first, u_first, v_first, d_buf, p_buf, table, saved, saved_f, mid, mid_f,
                 h_buf, u_buf, v_buf, c_one, c_two, solved, coef):
    rows = lax.broadcasted_iota(jnp.int32, (16, 128), 0) + scal[1]
    cor_c = coriolis_of(rows, rows_total)
    cor_s = coriolis_of(rows - 1, rows_total)
    d_c = [p_buf[j, 8:24, :] for j in range(2)]
    d_e = [jnp.minimum(a, b) for a, b in zip(d_c, from_east(d_c))]
    d_n = [jnp.minimum(d_c[j], p_buf[j, 9:25, :]) for j in range(2)]
    d_s = [jnp.minimum(d_c[j], p_buf[j, 7:23, :]) for j in range(2)]
    buffers = (c_first, c_one, c_two, c_one, None)
    for n in range(1, ITERS + 1):
        src, dst = buffers[n - 1], buffers[n]
        old = (h_first, u_first, v_first) if n == 1 else (h_buf, u_buf, v_buf)

        def dynamics(k, carry):
            up, prev = carry
            read = lambda buf, r: [buf[k, j, r:r + 16, :] for j in range(2)]
            h_new, u_new, v_new, co, links, ratios = level_step(
                k, read(old[0], 7), read(old[0], 8), read(old[0], 9), read(old[1], 7), read(old[1], 8),
                read(old[2], 7), read(old[2], 8), (d_c, d_e, d_n, d_s), cor_c, cor_s, read(d_buf, 8), up, prev)
            for j in range(2):
                h_buf[k, j, 8:24, :] = h_new[j]
                u_buf[k, j, 8:24, :] = u_new[j]
                v_buf[k, j, 8:24, :] = v_new[j]
                for c in range(7):
                    coef[c, k, j] = co[j][c]
            return links, ratios

        lax.fori_loop(0, LV, dynamics, (zeros_like_tiles(16, 2), zeros_like_tiles(16, 2)), unroll=4)

        @pl.loop(0, LV)
        def _(k):
            for f, buf in enumerate((h_buf, u_buf, v_buf)):
                for j in range(2):
                    if n < ITERS:
                        saved_f[n - 1, f, k, j] = keep_rows(n, lambda r: buf[k, j, r:r + 8, :])
                    else:
                        mid_f[f, k, j] = buf[k, j, 12:20, :]

        for r0 in ((8, 16) if n < ITERS else (12,)):
            @pl.loop(0, 2)
            def _(s):
                def down(k, before):
                    co = [[coef[c, k, j, r0 - 8:r0, :] for j in range(2)] for c in range(6)]
                    read = lambda t, r: [src[s * PER + t, k, j, r:r + 8, :] for j in range(2)]
                    now = forward(co, [(read(t, r0), read(t, r0 - 1), read(t, r0 + 1)) for t in range(PER)], before)
                    for t in range(PER):
                        for j in range(2):
                            solved[k, t, j] = now[t][j]
                    return now

                lax.fori_loop(0, LV, down, [zeros_like_tiles(8, 2) for _ in range(PER)], unroll=8)

                def upward(i, m):
                    k = LV - 1 - i
                    r = [coef[6, k, j, r0 - 8:r0, :] for j in range(2)]
                    m = [[solved[k, t, j] + r[j] * m[t][j] for j in range(2)] for t in range(PER)]
                    outs = react(table, s, m)
                    for t in range(PER):
                        for j in range(2):
                            if n < ITERS:
                                dst[s * PER + t, k, j, r0:r0 + 8, :] = outs[t][j]
                            else:
                                mid[s * PER + t, k, j] = outs[t][j]
                    return m

                lax.fori_loop(0, LV, upward, [zeros_like_tiles(8, 2) for _ in range(PER)], unroll=4)
        if n < ITERS:
            @pl.loop(0, LV)
            def _(k):
                for t in range(NT):
                    for j in range(2):
                        saved[n - 1, t, k, j] = keep_rows(n, lambda r: dst[t, k, j, r:r + 8, :])


def halo_pack_kernel(y_s, y_n, own_f, r_own, l_own, halo, x_r, x_l):
    low = sub_iota() < 4
    place = lane_iota() & 31
    for i in range(2):
        rows = slice(8 * i, 8 * i + 8)
        x_r[LV, rows, :] = to_east(own_f[LV, rows, :], 4)
        x_l[LV, rows, :] = to_west(own_f[LV, rows, :], 4)

    @pl.loop(0, LV, unroll=4)
    def _(k):
        for i in range(2):
            rows = slice(8 * i, 8 * i + 8)
            x_r[k, rows, :] = jnp.where(place >= 16, to_east(own_f[k, rows, :], 4), r_own[k, rows, :])
            x_l[k, rows, :] = jnp.where(place >= 16, to_west(own_f[k, rows, :], 4), l_own[k, rows, :])

    def pair(index, j):
        ys, yn = y_s[index, j], y_n[index, j]
        return jnp.where(low, ys, pltpu.roll(yn, 4, 0)), jnp.where(low, pltpu.roll(ys, 4, 0), yn)

    @pl.loop(0, LV, unroll=2)
    def _(k):
        pairs = [[pair(t * LV + k, j) for j in range(2)] for t in range(PER)]
        hu = [pair(128 + k, j) for j in range(2)]
        vd = [pair(144 + k, j) for j in range(2)]
        groups = [[[pairs[4 * (g % 2) + q][j][g // 2] for j in range(2)] for q in range(4)] for g in range(4)]
        groups.append([[x[j][w] for j in range(2)] for x in (hu, vd) for w in range(2)])
        xr, xl = None, None
        for g in range(5):
            packed = pack_lanes(groups[g])
            halo[k, g] = packed
            here = place >= 4 * g
            xr = to_east(packed, g) if g == 0 else jnp.where(here, to_east(packed, g), xr)
            xl = to_west(packed, g) if g == 0 else jnp.where(here, to_west(packed, g), xl)
        x_r[k, 16:24, :] = xr
        x_l[k, 16:24, :] = xl

    packed = pack_lanes([[pair(160, j)[0] for j in range(2)]] * 4)
    for g in range(5):
        halo[LV, g] = packed
    x_r[LV, 16:24, :] = to_east(packed, 4)
    x_l[LV, 16:24, :] = to_west(packed, 4)


def edge_kernel(rows_total, scal, kept, saved, saved_f, h_first, u_first, v_first, y_s, y_n, d_first, p_first, table,
                out_c, out_f, c_buf, f_buf, d_buf, p_buf, solved, coef, sem):
    tracer = [None] + [pltpu.make_async_copy(saved.at[n - 1], c_buf.at[n, :, :, :, pl.ds(0, 8), :], sem.at[n]) for n in range(1, ITERS)]
    fields = [None] + [pltpu.make_async_copy(saved_f.at[n - 1], f_buf.at[n, :, :, :, pl.ds(0, 8), :], sem.at[3 + n]) for n in range(1, ITERS)]
    for c in fields[1:] + tracer[1:]:
        c.start()
    sub = sub_iota()
    low = sub < 4
    high = jnp.logical_not(low)

    def put(ref, inside, ys, yn, half):
        south = ys if half == 0 else pltpu.roll(ys, 4, 0)
        north = yn if half == 1 else pltpu.roll(yn, 4, 0)
        ref[0:8, :] = jnp.where(low, south, inside)
        pltpu.store(ref.at[pl.ds(4, 8), :], north, mask=high)

    @pl.loop(0, LV, unroll=2)
    def _(k):
        for j in range(2):
            for t in range(PER):
                ys, yn = y_s[t * LV + k, j], y_n[t * LV + k, j]
                for half in range(2):
                    put(c_buf.at[0, t + PER * half, k, j], kept[t + PER * half, k, j], ys, yn, half)
            for f, (buf, index, half) in enumerate(((h_first, 128, 0), (u_first, 128, 1), (v_first, 144, 0))):
                inside = keep_rows(0, lambda r: buf[k, j, r:r + 8, :])
                put(f_buf.at[0, f, k, j], inside, y_s[index + k, j], y_n[index + k, j], half)
            ys, yn = y_s[144 + k, j], y_n[144 + k, j]
            d_buf[k, j, 0:8, :] = ys
            d_buf[k, j, 8:16, :] = d_first[k, j, 8:16, :]
            d_buf[k, j, 16:24, :] = d_first[k, j, 16:24, :]
            d_buf[k, j, 24:32, :] = pltpu.roll(yn, 4, 0)

    for j in range(2):
        p_buf[j, 0:8, :] = y_s[160, j].astype(jnp.int32)
        p_buf[j, 8:24, :] = p_first[j, 8:24, :]
        p_buf[j, 24:32, :] = y_n[160, j].astype(jnp.int32)

    def gather(read, shift):
        return jnp.where(low, read(shift), read(shift + 2))

    for n in range(1, ITERS + 1):
        if n < ITERS:
            fields[n].wait()
            tracer[n].wait()

        def at(buf, j, shift):
            return jnp.where(low, buf[j, 4 + n + shift:12 + n + shift, :], buf[j, 20 - n + shift:28 - n + shift, :])

        row = jnp.where(low, sub - 4 + n, sub + 12 - n) + scal[1]
        cor_c = coriolis_of(row, rows_total)
        cor_s = coriolis_of(row - 1, rows_total)
        d_c = [at(p_buf, j, 0) for j in range(2)]
        d_e = [jnp.minimum(a, b) for a, b in zip(d_c, from_east(d_c))]
        d_n = [jnp.minimum(d_c[j], at(p_buf, j, 1)) for j in range(2)]
        d_s = [jnp.minimum(d_c[j], at(p_buf, j, -1)) for j in range(2)]

        def dynamics(k, carry):
            up, prev = carry
            read = lambda f, shift: [gather(lambda r: f_buf[n - 1, f, k, j, r:r + 8, :], shift) for j in range(2)]
            diff = [at(d_buf.at[k], j, 0) for j in range(2)]
            h_new, u_new, v_new, co, links, ratios = level_step(
                k, read(0, 0), read(0, 1), read(0, 2), read(1, 0), read(1, 1), read(2, 0), read(2, 1),
                (d_c, d_e, d_n, d_s), cor_c, cor_s, diff, up, prev)
            for j in range(2):
                for f, x in enumerate((h_new[j], u_new[j], v_new[j])):
                    if n < ITERS:
                        pltpu.store(f_buf.at[n, f, k, j, pl.ds(0, 8), :], x, mask=low)
                        pltpu.store(f_buf.at[n, f, k, j, pl.ds(4, 8), :], x, mask=jnp.logical_not(low))
                    else:
                        out_f[f, k, j] = x
                for c in range(7):
                    coef[c, k, j] = co[j][c]
            return links, ratios

        lax.fori_loop(0, LV, dynamics, (zeros_like_tiles(8, 2), zeros_like_tiles(8, 2)), unroll=8)

        @pl.loop(0, 2)
        def _(s):
            def down(k, before):
                co = [[coef[c, k, j] for j in range(2)] for c in range(6)]

                def read(t, shift):
                    return [gather(lambda r: c_buf[n - 1, s * PER + t, k, j, r:r + 8, :], shift) for j in range(2)]

                now = forward(co, [(read(t, 1), read(t, 0), read(t, 2)) for t in range(PER)], before)
                for t in range(PER):
                    for j in range(2):
                        solved[k, t, j] = now[t][j]
                return now

            lax.fori_loop(0, LV, down, [zeros_like_tiles(8, 2) for _ in range(PER)], unroll=8)

            def upward(i, m):
                k = LV - 1 - i
                r = [coef[6, k, j] for j in range(2)]
                m = [[solved[k, t, j] + r[j] * m[t][j] for j in range(2)] for t in range(PER)]
                outs = react(table, s, m)
                for t in range(PER):
                    for j in range(2):
                        if n < ITERS:
                            pltpu.store(c_buf.at[n, s * PER + t, k, j, pl.ds(0, 8), :], outs[t][j], mask=low)
                            pltpu.store(c_buf.at[n, s * PER + t, k, j, pl.ds(4, 8), :], outs[t][j], mask=jnp.logical_not(low))
                        else:
                            out_c[s * PER + t, k, j] = outs[t][j]
                return m

            lax.fori_loop(0, LV, upward, [zeros_like_tiles(8, 2) for _ in range(PER)], unroll=4)


def strip_kernel(rows_total, scal, own, own_f, halo, x_w, x_e, table, mid, mid_f, edge, edge_f, out, out_h, out_v,
                 c_buf, c_alt, h_buf, u_buf, v_buf, d_buf, p_buf, solved, coef, out_c, sem):
    lane = lane_iota()
    place = lane & 31
    low = sub_iota() < 4

    def whole(k, g, i, xg):
        rows = slice(8 * i, 8 * i + 8)
        a = pltpu.roll(x_w[k, rows, :], (-4 * xg) % 128, 1)
        b = pltpu.roll(x_e[k, rows, :], (28 - 4 * xg) % 128, 1)
        if i == 2:
            body = halo[k, g]
        elif g == 4:
            body = own_f[k, rows, :]
        else:
            body = own[k, g, rows, :]
        return jnp.where(place < 4, a, jnp.where(place >= 28, b, body))

    def put(ref, i, x):
        if i < 2:
            ref[12 + 8 * i:20 + 8 * i, :] = x
        else:
            pltpu.store(ref.at[pl.ds(8, 8), :], x, mask=low)
            pltpu.store(ref.at[pl.ds(24, 8), :], x, mask=jnp.logical_not(low))

    @pl.loop(0, LV, unroll=4)
    def _(k):
        for i in range(3):
            for g in range(4):
                put(c_buf.at[g, k], i, whole(k, g, i, g))
            x = whole(k, 4, i, 4)
            for f, buf in enumerate((h_buf, u_buf, v_buf, d_buf)):
                y = jnp.where(lane < 32, pltpu.roll(x, (-32 * f) % 128, 1), 0.0)
                y = y + pltpu.roll(y, 32, 1)
                y = y + pltpu.roll(y, 64, 1)
                put(buf.at[k], i, y)

    for i in range(3):
        put(p_buf, i, whole(LV, 4, i, 4).astype(jnp.int32))

    rows = lax.broadcasted_iota(jnp.int32, (24, 128), 0) - 4 + scal[1]
    cor_c = coriolis_of(rows, rows_total)
    cor_s = coriolis_of(rows - 1, rows_total)
    d_c = [p_buf[8:32, :]]
    d_e = [jnp.minimum(d_c[0], from_east(d_c)[0])]
    d_n = [jnp.minimum(d_c[0], p_buf[9:33, :])]
    d_s = [jnp.minimum(d_c[0], p_buf[7:31, :])]

    for n in range(1, ITERS + 1):
        src, dst = (c_buf, c_alt) if n % 2 else (c_alt, c_buf)

        def dynamics(k, carry):
            up, prev = carry
            read = lambda buf, r: [buf[k, r:r + 24, :]]
            h_new, u_new, v_new, co, links, ratios = level_step(
                k, read(h_buf, 7), read(h_buf, 8), read(h_buf, 9), read(u_buf, 7), read(u_buf, 8),
                read(v_buf, 7), read(v_buf, 8), (d_c, d_e, d_n, d_s), cor_c, cor_s, read(d_buf, 8), up, prev)
            h_buf[k, 8:32, :] = h_new[0]
            u_buf[k, 8:32, :] = u_new[0]
            v_buf[k, 8:32, :] = v_new[0]
            for c in range(7):
                coef[c, k] = co[0][c]
            return links, ratios

        lax.fori_loop(0, LV, dynamics, (zeros_like_tiles(24, 1), zeros_like_tiles(24, 1)), unroll=8)

        starts = (8, 16, 24) if n < ITERS else (12, 20)
        tiles = len(starts)

        def down(k, before):
            co = [[coef[c, k, r0 - 8:r0, :] for r0 in starts] for c in range(6)]
            read = lambda t, shift: [src[t, k, r0 + shift:r0 + shift + 8, :] for r0 in starts]
            now = forward(co, [(read(t, 0), read(t, -1), read(t, 1)) for t in range(4)], before, joined=False)
            for t in range(4):
                for i in range(tiles):
                    solved[k, t, i] = now[t][i]
            return now

        lax.fori_loop(0, LV, down, [zeros_like_tiles(8, tiles) for _ in range(4)], unroll=4)

        def upward(i, m):
            k = LV - 1 - i
            r = [coef[6, k, r0 - 8:r0, :] for r0 in starts]
            m = [[solved[k, t, i] + r[i] * m[t][i] for i in range(tiles)] for t in range(4)]
            for i, r0 in enumerate(starts):
                turned = [[m[t][i]] + [pltpu.roll(m[t][i], 32 * rho, 1) for rho in range(1, 4)] for t in range(4)]
                for s in range(2):
                    for go in range(2):
                        acc = None
                        for gi in range(2):
                            for rho in range(4):
                                term = table[((s * 2 + go) * 2 + gi) * 4 + rho] * turned[2 * s + gi][rho]
                                acc = term if acc is None else acc + term
                        dst[2 * s + go, k, r0:r0 + 8, :] = acc
            return m

        lax.fori_loop(0, LV, upward, [zeros_like_tiles(8, tiles) for _ in range(4)], unroll=4)

    final = c_buf if ITERS % 2 == 0 else c_alt

    def merge(inner, outer, strip, q, j, i):
        turned = pltpu.roll(inner, 4, 0)
        body = jnp.where(low, outer, turned) if i == 0 else jnp.where(low, turned, outer)
        if j == 0:
            return jnp.where(lane < 4, pltpu.roll(strip, (-(32 * q + 4)) % 128, 1), body)
        return jnp.where(lane >= 124, pltpu.roll(strip, (100 - 32 * q) % 128, 1), body)

    leaving = []
    for part in range(4):
        @pl.loop(4 * part, 4 * part + 4, unroll=2)
        def _(k):
            for t in range(NT):
                for i in range(2):
                    strip = final[t // 4, k, 12 + 8 * i:20 + 8 * i, :]
                    for j in range(2):
                        out_c[t, k, 8 * i:8 * i + 8, 128 * j:128 * j + 128] = merge(
                            mid[t, k, j], edge[t, k, j], strip, t % 4, j, i)
        levels = pl.ds(4 * part, 4)
        leaving.append(pltpu.make_async_copy(out_c.at[:, levels], out.at[:, levels], sem.at[part]))
        leaving[part].start()

    off = scal[0] * (LV // 2)

    @pl.loop(0, LV // 2, unroll=4)
    def _(k):
        for f, buf in enumerate((h_buf, u_buf, v_buf)):
            for i in range(2):
                strip = buf[k + off, 12 + 8 * i:20 + 8 * i, :]
                for j in range(2):
                    x = merge(mid_f[f, k + off, j], edge_f[f, k + off, j], strip, 0, j, i)
                    if f == 0:
                        out_h[k, 8 * i:8 * i + 8, 128 * j:128 * j + 128] = x
                    else:
                        out_v[f - 1, k, 8 * i:8 * i + 8, 128 * j:128 * j + 128] = x
    for c in leaving:
        c.wait()


def room(mebibytes):
    return pltpu.CompilerParams(vmem_limit_bytes=mebibytes * 1024 * 1024)


def sds(*shape):
    return jax.ShapeDtypeStruct(shape, F32)


def body(tracers, thickness, velocity, diffusivity, reaction, land_mask, level_count):
    rows_local = thickness.shape[1]
    rows_total = rows_local * lax.axis_size("ty")
    set_index = lax.axis_index("set").astype(jnp.int32)
    row_start = lax.axis_index("ty").astype(jnp.int32) * rows_local
    scal = jnp.stack([set_index, row_start])
    swap = [(0, 1), (1, 0)]
    h_pair = lax.ppermute(thickness, "set", swap)
    v_pair = lax.ppermute(velocity, "set", swap)
    field = sds(LV, 2, 32, 128)
    y_shape = sds(161, 2, 8, 128)
    up_part, dn_part, own, r_own, l_own, c_first, kept, table, s_table = pl.pallas_call(
        tracer_pack_kernel,
        out_shape=[y_shape, y_shape, sds(LV, 4, 16, 128), sds(LV, 16, 128), sds(LV, 16, 128), sds(NT, LV, 2, 32, 128),
                   sds(NT, LV, 2, 8, 128), sds(128, 8, 128), sds(32, 8, 128)],
        in_specs=[ANY, SMEM], out_specs=[VMEM] * 9,
        scratch_shapes=[pltpu.SemaphoreType.DMA((4,))],
        compiler_params=room(4), name="tracer_pack")(tracers, reaction)
    h_pair, v_pair, up_part, dn_part = lax.optimization_barrier((h_pair, v_pair, up_part, dn_part))
    y_up, y_dn, own_f, h_first, u_first, v_first, d_first, p_first = pl.pallas_call(
        field_pack_kernel, out_shape=[y_shape, y_shape, sds(LV + 1, 16, 128)] + [field] * 4 + [jax.ShapeDtypeStruct((2, 32, 128), jnp.int32)],
        in_specs=[SMEM] + [ANY] * 9, out_specs=[ANY, ANY] + [VMEM] * 6,
        input_output_aliases={8: 0, 9: 1},
        scratch_shapes=[pltpu.VMEM((33, 2, 8, 128), F32), pltpu.VMEM((33, 2, 8, 128), F32),
                        pltpu.VMEM((2, 2, 16, 128), jnp.int32),
                        pltpu.SemaphoreType.DMA((18,)), pltpu.SemaphoreType.DMA((2,))],
        compiler_params=room(4), name="field_pack")(
            scal, thickness, h_pair, velocity, v_pair, diffusivity, land_mask, level_count, up_part, dn_part)
    ty = lax.axis_size("ty")
    north = [(i, i + 1) for i in range(ty - 1)]
    south = [(j, i) for i, j in north]
    y_s = lax.ppermute(y_up, "ty", north)
    y_n = lax.ppermute(y_dn, "ty", south)
    saved, saved_f, mid, mid_f = pl.pallas_call(
        lambda *a: inner_kernel(rows_total, *a),
        out_shape=[sds(ITERS - 1, NT, LV, 2, 8, 128), sds(ITERS - 1, 3, LV, 2, 8, 128), sds(NT, LV, 2, 8, 128), sds(3, LV, 2, 8, 128)],
        in_specs=[SMEM] + [VMEM] * 7, out_specs=[VMEM] * 4,
        scratch_shapes=[pltpu.VMEM((LV, 2, 32, 128), F32)] * 3 + [
            pltpu.VMEM((NT, LV, 2, 32, 128), F32),
            pltpu.VMEM((NT, LV, 2, 32, 128), F32),
            pltpu.VMEM((LV, PER, 2, 8, 128), F32),
            pltpu.VMEM((7, LV, 2, 16, 128), F32)],
        compiler_params=room(24), name="inner")(scal, c_first, h_first, u_first, v_first, d_first, p_first, table)
    y_s, y_n, mid_f = lax.optimization_barrier((y_s, y_n, mid_f))
    halo, x_r, x_l = pl.pallas_call(
        halo_pack_kernel, out_shape=[sds(LV + 1, 5, 8, 128), sds(LV + 1, 24, 128), sds(LV + 1, 24, 128)],
        in_specs=[VMEM] * 5, out_specs=[VMEM] * 3,
        compiler_params=room(4), name="halo_pack")(y_s, y_n, own_f, r_own, l_own)
    tx = lax.axis_size("tx")
    east = [(i, (i + 1) % tx) for i in range(tx)]
    west = [(j, i) for i, j in east]
    x_w = lax.ppermute(x_r, "tx", east)
    x_e = lax.ppermute(x_l, "tx", west)
    edge, edge_f = pl.pallas_call(
        lambda *a: edge_kernel(rows_total, *a),
        out_shape=[sds(NT, LV, 2, 8, 128), sds(3, LV, 2, 8, 128)],
        in_specs=[SMEM] + [VMEM] * 11, out_specs=[VMEM] * 2,
        scratch_shapes=[
            pltpu.VMEM((ITERS, NT, LV, 2, 16, 128), F32),
            pltpu.VMEM((ITERS, 3, LV, 2, 16, 128), F32),
            pltpu.VMEM((LV, 2, 32, 128), F32),
            pltpu.VMEM((2, 32, 128), jnp.int32),
            pltpu.VMEM((LV, PER, 2, 8, 128), F32),
            pltpu.VMEM((7, LV, 2, 8, 128), F32),
            pltpu.SemaphoreType.DMA((2 * ITERS,))],
        compiler_params=room(24), name="edge")(
            scal, kept, saved, saved_f, h_first, u_first, v_first, y_s, y_n, d_first, p_first, table)
    return pl.pallas_call(
        lambda *a: strip_kernel(rows_total, *a),
        out_shape=[sds(*tracers.shape), sds(*thickness.shape), sds(*velocity.shape)],
        in_specs=[SMEM] + [VMEM] * 10, out_specs=[ANY, VMEM, VMEM],
        scratch_shapes=[
            pltpu.VMEM((4, LV, 40, 128), F32),
            pltpu.VMEM((4, LV, 40, 128), F32),
            pltpu.VMEM((LV, 40, 128), F32),
            pltpu.VMEM((LV, 40, 128), F32),
            pltpu.VMEM((LV, 40, 128), F32),
            pltpu.VMEM((LV, 40, 128), F32),
            pltpu.VMEM((40, 128), jnp.int32),
            pltpu.VMEM((LV, 4, 3, 8, 128), F32),
            pltpu.VMEM((7, LV, 24, 128), F32),
            pltpu.VMEM((NT, LV, 16, 256), F32),
            pltpu.SemaphoreType.DMA((4,))],
        compiler_params=room(14), name="strips")(scal, own, own_f, halo, x_w, x_e, s_table, mid, mid_f, edge, edge_f)


def solution(mesh):
    placed = (
        P("set", None, "ty", "tx"),
        P("set", "ty", "tx"),
        P(None, "set", "ty", "tx"),
        P(None, "ty", "tx"),
        P("set", None, None),
        P("ty", "tx"),
        P("ty", "tx"),
    )

    def whole(*args):
        return tuple(body(*args))

    return jax.shard_map(
        whole,
        mesh=mesh,
        in_specs=placed,
        out_specs=(P("set", None, "ty", "tx"), P("set", "ty", "tx"), P(None, "set", "ty", "tx")),
        check_vma=False,
    )
```

```python
import jax
import jax.numpy as jnp
from jax import lax
from jax.experimental import pallas as pl
from jax.experimental.pallas import tpu as pltpu
from jax.sharding import PartitionSpec as P

ITERS = 4
DT = 0.2
G = 1.0
ROTATION = 0.5
LV = 16
NT = 16
PER = 8
F32 = jnp.float32
BF16 = jnp.bfloat16
ANY = pl.BlockSpec(memory_space=pl.ANY)
SMEM = pl.BlockSpec(memory_space=pltpu.SMEM)
VMEM = pl.BlockSpec(memory_space=pltpu.VMEM)


def sub_iota(rows=8):
    return lax.broadcasted_iota(jnp.int32, (rows, 128), 0)


def lane_iota(rows=8):
    return lax.broadcasted_iota(jnp.int32, (rows, 128), 1)


def from_east(tiles, joined=True):
    rolled = [pltpu.roll(x, 127, 1) for x in tiles]
    lane = lane_iota(tiles[0].shape[0])
    last = len(tiles) - 1
    return [rolled[i] if i == last or not joined else jnp.where(lane == 127, rolled[i + 1], rolled[i]) for i in range(last + 1)]


def from_west(tiles, joined=True):
    rolled = [pltpu.roll(x, 1, 1) for x in tiles]
    lane = lane_iota(tiles[0].shape[0])
    return [rolled[i] if i == 0 or not joined else jnp.where(lane == 0, rolled[i - 1], rolled[i]) for i in range(len(tiles))]


def coriolis_of(row, rows_total):
    return ROTATION * (2.0 * (row.astype(F32) + 0.5) / rows_total - 1.0)


def level_step(k, h_s, h_c, h_n, u_s, u_c, v_s, v_c, deep, cor_c, cor_s, diff, up, prev):
    d_c, d_e, d_n, d_s = deep
    h_e = from_east(h_c)
    count = len(h_c)
    u_new, v_new, u_flux, v_flux, s_flux = [], [], [], [], []
    for j in range(count):
        un = jnp.where(k < d_e[j], u_c[j] + DT * (cor_c * v_c[j] - G * (h_e[j] - h_c[j])), 0.0)
        vn = jnp.where(k < d_n[j], v_c[j] - DT * (cor_c * u_c[j] + G * (h_n[j] - h_c[j])), 0.0)
        vs = jnp.where(k < d_s[j], v_s[j] - DT * (cor_s * u_s[j] + G * (h_c[j] - h_s[j])), 0.0)
        u_new.append(un)
        v_new.append(vn)
        u_flux.append(un * 0.5 * (h_c[j] + h_e[j]))
        v_flux.append(vn * 0.5 * (h_c[j] + h_n[j]))
        s_flux.append(vs * 0.5 * (h_s[j] + h_c[j]))
    w_flux = from_west(u_flux)
    h_new, coefs, links, ratios = [], [], [], []
    for j in range(count):
        fe, fw, fn, fs = u_flux[j], w_flux[j], v_flux[j], s_flux[j]
        hn = h_c[j] - DT * ((fe - fw) + (fn - fs))
        link = jnp.where(k + 1 < d_c[j], DT * diff[j], 0.0)
        q = jnp.where(k < d_c[j], 1.0 / (hn + up[j] + link - up[j] * prev[j]), 0.0)
        r = link * q
        dq = DT * q
        ce = dq * jnp.maximum(-fe, 0.0)
        cw = dq * jnp.maximum(fw, 0.0)
        cn = dq * jnp.maximum(-fn, 0.0)
        cs = dq * jnp.maximum(fs, 0.0)
        out = (jnp.maximum(fe, 0.0) - jnp.minimum(fw, 0.0)) + (jnp.maximum(fn, 0.0) - jnp.minimum(fs, 0.0))
        ca = q * h_c[j] - dq * out
        h_new.append(hn)
        links.append(link)
        ratios.append(r)
        coefs.append((ca, ce, cw, cn, cs, up[j] * q, r))
    return h_new, u_new, v_new, coefs, links, ratios


def forward(coefs, cells, before, joined=True):
    result = []
    for t, (c, s, n) in enumerate(cells):
        e = from_east(c, joined)
        w = from_west(c, joined)
        result.append([
            ((coefs[0][j] * c[j] + coefs[1][j] * e[j]) + (coefs[2][j] * w[j] + coefs[3][j] * n[j]))
            + (coefs[4][j] * s[j] + coefs[5][j] * before[t][j])
            for j in range(len(c))
        ])
    return result


def react(weights, m):
    x = jnp.concatenate([jnp.concatenate([m[t][j] for t in range(PER)], axis=0) for j in range(2)], axis=1)
    high = x.astype(BF16)
    rest = (x - high.astype(F32)).astype(BF16)
    parts = jnp.concatenate([high, rest, high], axis=0)
    out = jnp.dot(weights[:, :192], parts, preferred_element_type=F32)
    return [[out[8 * t:8 * t + 8, 128 * j:128 * j + 128] for j in range(2)] for t in range(PER)]


def sweep(down, upward, unroll=8):
    def step(i, carry):
        before, m = carry
        if down is not None:
            before = down(i, before)
        if upward is not None:
            m = upward(LV - 1 - i, m)
        return before, m

    start = [zeros_like_tiles(8, 2) for _ in range(PER)]
    lax.fori_loop(0, LV, step, (start if down is not None else 0, start if upward is not None else 0), unroll=unroll)


def zeros_like_tiles(rows, count):
    return [jnp.zeros((rows, 128), F32) for _ in range(count)]


def pack_lanes(sources):
    lane = lane_iota()
    place, slot = lane & 31, lane >> 5
    acc = None
    for q, (left, right) in enumerate(sources):
        a = pltpu.roll(left, (4 + 32 * q) % 128, 1)
        b = pltpu.roll(right, (28 + 32 * q) % 128, 1)
        x = jnp.where(place < 16, a, b)
        acc = x if acc is None else jnp.where(slot == q, x, acc)
    return acc


def to_east(packed, g):
    return pltpu.roll(packed, (4 * g - 24) % 128, 1)


def to_west(packed, g):
    return pltpu.roll(packed, (4 * g - 4) % 128, 1)


def tracer_pack_kernel(tr, reaction, y_up, y_dn, own, x_r, x_l, c_buf, kept, table, s_table, sem):
    copies = [pltpu.make_async_copy(
        tr.at[pl.ds(8 * s, 8), :, :, pl.ds(128 * j, 128)],
        c_buf.at[pl.ds(8 * s, 8), :, j, pl.ds(8, 16), :], sem.at[2 * s + j]) for s in range(2) for j in range(2)]
    for c in copies:
        c.start()
    low = sub_iota() < 4
    place = lane_iota() & 31
    slot = lane_iota() >> 5
    same = (lane_iota() & 7) == sub_iota()
    column = (lane_iota() >> 3) & 7
    for s in range(2):
        blocks = []
        for a in range(PER):
            v = jnp.zeros((8, 128), F32)
            for b in range(PER):
                w = DT * reaction[s, a, b] + (1.0 if a == b else 0.0)
                v = jnp.where(same & (column == b), jnp.full((8, 128), w, F32), v)
            blocks.append(v)
        v = jnp.concatenate(blocks, axis=0)
        high = v.astype(BF16)
        table[s, :, 0:128] = high
        table[s, :, 128:256] = (v - high.astype(F32)).astype(BF16)
    for s in range(2):
        for go in range(2):
            for gi in range(2):
                for rho in range(4):
                    v = jnp.zeros((8, 128), F32)
                    for q in range(4):
                        a, b = 4 * go + q, 4 * gi + (q - rho) % 4
                        w = DT * reaction[s, a, b] + (1.0 if a == b else 0.0)
                        v = jnp.where(slot == q, jnp.full((8, 128), w, F32), v)
                    s_table[((s * 2 + go) * 2 + gi) * 4 + rho] = v
    for c in copies:
        c.wait()

    @pl.loop(0, LV, unroll=2)
    def _(k):
        for j in range(2):
            for t in range(PER):
                read = lambda b, r: c_buf[t + b, k, j, r:r + 8, :]
                y_up[t * LV + k, j] = jnp.where(low, read(0, 20), read(PER, 16))
                y_dn[t * LV + k, j] = jnp.where(low, read(0, 8), read(PER, 4))
            for t in range(NT):
                kept[t, k, j] = keep_rows(0, lambda r: c_buf[t, k, j, r:r + 8, :])
        for i in range(2):
            rows = slice(8 * i, 8 * i + 8)
            xr, xl = None, None
            for g in range(4):
                packed = pack_lanes([[c_buf[4 * g + q, k, j, 8 + 8 * i:16 + 8 * i, :] for j in range(2)] for q in range(4)])
                own[k, g, rows, :] = packed
                here = place >= 4 * g
                xr = to_east(packed, g) if g == 0 else jnp.where(here, to_east(packed, g), xr)
                xl = to_west(packed, g) if g == 0 else jnp.where(here, to_west(packed, g), xl)
            x_r[k, rows, :] = xr
            x_l[k, rows, :] = xl


def keep_rows(n, read):
    return jnp.where(sub_iota() < 6, read(4 + n), read(16 - n))


def field_pack_kernel(scal, ho, hp, vo, vp, df, land, level, up_in, dn_in, y_up, y_dn, own, h_buf, u_buf, v_buf, d_buf, p_buf,
                      f_up, f_dn, l_buf, sem, out_sem):
    off = scal[0] * (LV // 2)
    part = LV // 2
    rows = pl.ds(8, 16)
    copies = []
    for j in range(2):
        lanes = pl.ds(128 * j, 128)
        for i, (h, v, at) in enumerate(((ho, vo, off), (hp, vp, part - off))):
            levels = pl.ds(at, part)
            copies.append(pltpu.make_async_copy(h.at[:, :, lanes], h_buf.at[levels, j, rows, :], sem.at[6 * j + 3 * i]))
            copies.append(pltpu.make_async_copy(v.at[0, :, :, lanes], u_buf.at[levels, j, rows, :], sem.at[6 * j + 3 * i + 1]))
            copies.append(pltpu.make_async_copy(v.at[1, :, :, lanes], v_buf.at[levels, j, rows, :], sem.at[6 * j + 3 * i + 2]))
        copies.append(pltpu.make_async_copy(df.at[:, :, lanes], d_buf.at[:, j, rows, :], sem.at[12 + j]))
        copies.append(pltpu.make_async_copy(land.at[:, lanes], l_buf.at[0, j], sem.at[14 + j]))
        copies.append(pltpu.make_async_copy(level.at[:, lanes], l_buf.at[1, j], sem.at[16 + j]))
    for c in copies:
        c.start()
    low = sub_iota() < 4
    for c in copies:
        c.wait()

    for j in range(2):
        p_buf[j, 8:24, :] = jnp.where(l_buf[0, j] == 1, l_buf[1, j], 0)

    def put(index, j, first, second):
        f_up[index, j] = jnp.where(low, first(20), second(16))
        f_dn[index, j] = jnp.where(low, first(8), second(4))

    @pl.loop(0, LV, unroll=4)
    def _(k):
        for j in range(2):
            put(k, j, lambda r: h_buf[k, j, r:r + 8, :], lambda r: u_buf[k, j, r:r + 8, :])
            put(16 + k, j, lambda r: v_buf[k, j, r:r + 8, :], lambda r: d_buf[k, j, r:r + 8, :])

    for j in range(2):
        get = lambda r: p_buf[j, r:r + 8, :].astype(F32)
        put(32, j, get, get)
    leaving = [pltpu.make_async_copy(f, y.at[pl.ds(128, 33)], out_sem.at[i]) for i, (f, y) in enumerate(((f_up, y_up), (f_dn, y_dn)))]
    for c in leaving:
        c.start()

    @pl.loop(0, LV, unroll=4)
    def _(k):
        for i in range(2):
            own[k, 8 * i:8 * i + 8, :] = pack_lanes(
                [[buf[k, j, 8 + 8 * i:16 + 8 * i, :] for j in range(2)] for buf in (h_buf, u_buf, v_buf, d_buf)])

    for i in range(2):
        own[LV, 8 * i:8 * i + 8, :] = pack_lanes([[p_buf[j, 8 + 8 * i:16 + 8 * i, :].astype(F32) for j in range(2)]] * 4)
    for c in leaving:
        c.wait()


def inner_kernel(rows_total, scal, c_first, h_first, u_first, v_first, d_buf, p_buf, table, saved, saved_f, mid, mid_f,
                 h_buf, u_buf, v_buf, one_a, one_b, two_a, two_b, solved_a, solved_b, coef, ratio):
    rows = lax.broadcasted_iota(jnp.int32, (16, 128), 0) + scal[1]
    cor_c = coriolis_of(rows, rows_total)
    cor_s = coriolis_of(rows - 1, rows_total)
    d_c = [p_buf[j, 8:24, :] for j in range(2)]
    d_e = [jnp.minimum(a, b) for a, b in zip(d_c, from_east(d_c))]
    d_n = [jnp.minimum(d_c[j], p_buf[j, 9:25, :]) for j in range(2)]
    d_s = [jnp.minimum(d_c[j], p_buf[j, 7:23, :]) for j in range(2)]
    c_one, c_two = (one_a, one_b), (two_a, two_b)
    buffers = ((c_first.at[pl.ds(0, PER)], c_first.at[pl.ds(PER, PER)]), c_one, c_two, c_one, None)
    solved = (solved_a, solved_b)
    pending, keep, slot = None, None, 0
    for n in range(1, ITERS + 1):
        src, dst = buffers[n - 1], buffers[n]
        old = (h_first, u_first, v_first) if n == 1 else (h_buf, u_buf, v_buf)

        def dynamics(k, carry):
            up, prev = carry
            read = lambda buf, r: [buf[k, j, r:r + 16, :] for j in range(2)]
            h_new, u_new, v_new, co, links, ratios = level_step(
                k, read(old[0], 7), read(old[0], 8), read(old[0], 9), read(old[1], 7), read(old[1], 8),
                read(old[2], 7), read(old[2], 8), (d_c, d_e, d_n, d_s), cor_c, cor_s, read(d_buf, 8), up, prev)
            for j in range(2):
                h_buf[k, j, 8:24, :] = h_new[j]
                u_buf[k, j, 8:24, :] = u_new[j]
                v_buf[k, j, 8:24, :] = v_new[j]
                for c in range(6):
                    coef[c, k, j] = co[j][c]
                ratio[n % 2, k, j] = co[j][6]
            return links, ratios

        lax.fori_loop(0, LV, dynamics, (zeros_like_tiles(16, 2), zeros_like_tiles(16, 2)), unroll=4)

        @pl.loop(0, LV)
        def _(k):
            for f, buf in enumerate((h_buf, u_buf, v_buf)):
                for j in range(2):
                    if n < ITERS:
                        saved_f[n - 1, f, k, j] = keep_rows(n, lambda r: buf[k, j, r:r + 8, :])
                    else:
                        mid_f[f, k, j] = buf[k, j, 12:20, :]

        for s in range(2):
            for r0 in ((8, 16) if n < ITERS else (12,)):
                def down(k, before, s=s, r0=r0, src=src, slot=slot):
                    co = [[coef[c, k, j, r0 - 8:r0, :] for j in range(2)] for c in range(6)]
                    read = lambda t, r: [src[s][t, k, j, r:r + 8, :] for j in range(2)]
                    now = forward(co, [(read(t, r0), read(t, r0 - 1), read(t, r0 + 1)) for t in range(PER)], before)
                    for t in range(PER):
                        for j in range(2):
                            solved[slot][k, t, j] = now[t][j]
                    return now

                def upward(k, m, s=s, r0=r0, dst=dst, slot=slot, n=n):
                    r = [ratio[n % 2, k, j, r0 - 8:r0, :] for j in range(2)]
                    m = [[solved[slot][k, t, j] + r[j] * m[t][j] for j in range(2)] for t in range(PER)]
                    outs = react(table[s], m)
                    for t in range(PER):
                        for j in range(2):
                            if n < ITERS:
                                dst[s][t, k, j, r0:r0 + 8, :] = outs[t][j]
                            else:
                                mid[s * PER + t, k, j] = outs[t][j]
                    return m

                sweep(down, pending)
                pending = upward
                slot = 1 - slot
                if keep is not None:
                    keep()
                    keep = None

        def keep(n=n, dst=dst):
            @pl.loop(0, LV)
            def _(k):
                for t in range(NT):
                    for j in range(2):
                        saved[n - 1, t, k, j] = keep_rows(n, lambda r: dst[t // PER][t % PER, k, j, r:r + 8, :])

    sweep(None, pending)


def halo_pack_kernel(y_s, y_n, own_f, r_own, l_own, halo, x_r, x_l):
    low = sub_iota() < 4
    place = lane_iota() & 31
    for i in range(2):
        rows = slice(8 * i, 8 * i + 8)
        x_r[LV, rows, :] = to_east(own_f[LV, rows, :], 4)
        x_l[LV, rows, :] = to_west(own_f[LV, rows, :], 4)

    @pl.loop(0, LV, unroll=4)
    def _(k):
        for i in range(2):
            rows = slice(8 * i, 8 * i + 8)
            x_r[k, rows, :] = jnp.where(place >= 16, to_east(own_f[k, rows, :], 4), r_own[k, rows, :])
            x_l[k, rows, :] = jnp.where(place >= 16, to_west(own_f[k, rows, :], 4), l_own[k, rows, :])

    def pair(index, j):
        ys, yn = y_s[index, j], y_n[index, j]
        return jnp.where(low, ys, pltpu.roll(yn, 4, 0)), jnp.where(low, pltpu.roll(ys, 4, 0), yn)

    @pl.loop(0, LV, unroll=2)
    def _(k):
        pairs = [[pair(t * LV + k, j) for j in range(2)] for t in range(PER)]
        hu = [pair(128 + k, j) for j in range(2)]
        vd = [pair(144 + k, j) for j in range(2)]
        groups = [[[pairs[4 * (g % 2) + q][j][g // 2] for j in range(2)] for q in range(4)] for g in range(4)]
        groups.append([[x[j][w] for j in range(2)] for x in (hu, vd) for w in range(2)])
        xr, xl = None, None
        for g in range(5):
            packed = pack_lanes(groups[g])
            halo[k, g] = packed
            here = place >= 4 * g
            xr = to_east(packed, g) if g == 0 else jnp.where(here, to_east(packed, g), xr)
            xl = to_west(packed, g) if g == 0 else jnp.where(here, to_west(packed, g), xl)
        x_r[k, 16:24, :] = xr
        x_l[k, 16:24, :] = xl

    packed = pack_lanes([[pair(160, j)[0] for j in range(2)]] * 4)
    for g in range(5):
        halo[LV, g] = packed
    x_r[LV, 16:24, :] = to_east(packed, 4)
    x_l[LV, 16:24, :] = to_west(packed, 4)


def edge_kernel(rows_total, scal, kept, saved, saved_f, h_first, u_first, v_first, y_s, y_n, d_first, p_first, table,
                out_c, out_f, *scratch):
    c_buf = [scratch[2 * n:2 * n + 2] for n in range(ITERS)]
    f_buf, d_buf, p_buf, solved_a, solved_b, coef, ratio, sem = scratch[2 * ITERS:]
    solved = (solved_a, solved_b)
    tracer = [[pltpu.make_async_copy(saved.at[n - 1, pl.ds(PER * s, PER)], c_buf[n][s].at[:, :, :, pl.ds(0, 8), :], sem.at[2 * n + s])
               for s in range(2)] for n in range(1, ITERS)]
    fields = [None] + [pltpu.make_async_copy(saved_f.at[n - 1], f_buf.at[n, :, :, :, pl.ds(0, 8), :], sem.at[2 * ITERS + n]) for n in range(1, ITERS)]
    for c in fields[1:] + tracer[0] + tracer[1] + tracer[2]:
        c.start()
    sub = sub_iota()
    low = sub < 4
    high = jnp.logical_not(low)

    def put(ref, inside, ys, yn, half):
        south = ys if half == 0 else pltpu.roll(ys, 4, 0)
        north = yn if half == 1 else pltpu.roll(yn, 4, 0)
        ref[0:8, :] = jnp.where(low, south, inside)
        pltpu.store(ref.at[pl.ds(4, 8), :], north, mask=high)

    @pl.loop(0, LV, unroll=2)
    def _(k):
        for j in range(2):
            for t in range(PER):
                ys, yn = y_s[t * LV + k, j], y_n[t * LV + k, j]
                for half in range(2):
                    put(c_buf[0][half].at[t, k, j], kept[t + PER * half, k, j], ys, yn, half)
            for f, (buf, index, half) in enumerate(((h_first, 128, 0), (u_first, 128, 1), (v_first, 144, 0))):
                inside = keep_rows(0, lambda r: buf[k, j, r:r + 8, :])
                put(f_buf.at[0, f, k, j], inside, y_s[index + k, j], y_n[index + k, j], half)
            ys, yn = y_s[144 + k, j], y_n[144 + k, j]
            d_buf[k, j, 0:8, :] = ys
            d_buf[k, j, 8:16, :] = d_first[k, j, 8:16, :]
            d_buf[k, j, 16:24, :] = d_first[k, j, 16:24, :]
            d_buf[k, j, 24:32, :] = pltpu.roll(yn, 4, 0)

    for j in range(2):
        p_buf[j, 0:8, :] = y_s[160, j].astype(jnp.int32)
        p_buf[j, 8:24, :] = p_first[j, 8:24, :]
        p_buf[j, 24:32, :] = y_n[160, j].astype(jnp.int32)

    def gather(read, shift):
        return jnp.where(low, read(shift), read(shift + 2))

    pending, slot = None, 0
    for n in range(1, ITERS + 1):
        if n < ITERS:
            fields[n].wait()
            for c in tracer[n - 1]:
                c.wait()

        def at(buf, j, shift):
            return jnp.where(low, buf[j, 4 + n + shift:12 + n + shift, :], buf[j, 20 - n + shift:28 - n + shift, :])

        row = jnp.where(low, sub - 4 + n, sub + 12 - n) + scal[1]
        cor_c = coriolis_of(row, rows_total)
        cor_s = coriolis_of(row - 1, rows_total)
        d_c = [at(p_buf, j, 0) for j in range(2)]
        d_e = [jnp.minimum(a, b) for a, b in zip(d_c, from_east(d_c))]
        d_n = [jnp.minimum(d_c[j], at(p_buf, j, 1)) for j in range(2)]
        d_s = [jnp.minimum(d_c[j], at(p_buf, j, -1)) for j in range(2)]

        def dynamics(k, carry):
            up, prev = carry
            read = lambda f, shift: [gather(lambda r: f_buf[n - 1, f, k, j, r:r + 8, :], shift) for j in range(2)]
            diff = [at(d_buf.at[k], j, 0) for j in range(2)]
            h_new, u_new, v_new, co, links, ratios = level_step(
                k, read(0, 0), read(0, 1), read(0, 2), read(1, 0), read(1, 1), read(2, 0), read(2, 1),
                (d_c, d_e, d_n, d_s), cor_c, cor_s, diff, up, prev)
            for j in range(2):
                for f, x in enumerate((h_new[j], u_new[j], v_new[j])):
                    if n < ITERS:
                        pltpu.store(f_buf.at[n, f, k, j, pl.ds(0, 8), :], x, mask=low)
                        pltpu.store(f_buf.at[n, f, k, j, pl.ds(4, 8), :], x, mask=jnp.logical_not(low))
                    else:
                        out_f[f, k, j] = x
                for c in range(6):
                    coef[c, k, j] = co[j][c]
                ratio[n % 2, k, j] = co[j][6]
            return links, ratios

        lax.fori_loop(0, LV, dynamics, (zeros_like_tiles(8, 2), zeros_like_tiles(8, 2)), unroll=8)

        for s in range(2):
            def down(k, before, s=s, n=n, slot=slot):
                co = [[coef[c, k, j] for j in range(2)] for c in range(6)]

                def read(t, shift):
                    return [gather(lambda r: c_buf[n - 1][s][t, k, j, r:r + 8, :], shift) for j in range(2)]

                now = forward(co, [(read(t, 1), read(t, 0), read(t, 2)) for t in range(PER)], before)
                for t in range(PER):
                    for j in range(2):
                        solved[slot][k, t, j] = now[t][j]
                return now

            def upward(k, m, s=s, n=n, slot=slot):
                r = [ratio[n % 2, k, j] for j in range(2)]
                m = [[solved[slot][k, t, j] + r[j] * m[t][j] for j in range(2)] for t in range(PER)]
                outs = react(table[s], m)
                for t in range(PER):
                    for j in range(2):
                        if n < ITERS:
                            pltpu.store(c_buf[n][s].at[t, k, j, pl.ds(0, 8), :], outs[t][j], mask=low)
                            pltpu.store(c_buf[n][s].at[t, k, j, pl.ds(4, 8), :], outs[t][j], mask=high)
                        else:
                            out_c[s * PER + t, k, j] = outs[t][j]
                return m

            sweep(down, pending)
            pending = upward
            slot = 1 - slot

    sweep(None, pending)


def strip_kernel(rows_total, scal, own, own_f, halo, x_w, x_e, table, mid, mid_f, edge, edge_f, out, out_h, out_v,
                 c_buf, c_alt, h_buf, u_buf, v_buf, d_buf, p_buf, solved, coef, out_c, sem):
    lane = lane_iota()
    place = lane & 31
    low = sub_iota() < 4

    def whole(k, g, i, xg):
        rows = slice(8 * i, 8 * i + 8)
        a = pltpu.roll(x_w[k, rows, :], (-4 * xg) % 128, 1)
        b = pltpu.roll(x_e[k, rows, :], (28 - 4 * xg) % 128, 1)
        if i == 2:
            body = halo[k, g]
        elif g == 4:
            body = own_f[k, rows, :]
        else:
            body = own[k, g, rows, :]
        return jnp.where(place < 4, a, jnp.where(place >= 28, b, body))

    def put(ref, i, x):
        if i < 2:
            ref[12 + 8 * i:20 + 8 * i, :] = x
        else:
            pltpu.store(ref.at[pl.ds(8, 8), :], x, mask=low)
            pltpu.store(ref.at[pl.ds(24, 8), :], x, mask=jnp.logical_not(low))

    @pl.loop(0, LV, unroll=4)
    def _(k):
        for i in range(3):
            for g in range(4):
                put(c_buf.at[g, k], i, whole(k, g, i, g))
            x = whole(k, 4, i, 4)
            for f, buf in enumerate((h_buf, u_buf, v_buf, d_buf)):
                y = jnp.where(lane < 32, pltpu.roll(x, (-32 * f) % 128, 1), 0.0)
                y = y + pltpu.roll(y, 32, 1)
                y = y + pltpu.roll(y, 64, 1)
                put(buf.at[k], i, y)

    for i in range(3):
        put(p_buf, i, whole(LV, 4, i, 4).astype(jnp.int32))

    rows = lax.broadcasted_iota(jnp.int32, (24, 128), 0) - 4 + scal[1]
    cor_c = coriolis_of(rows, rows_total)
    cor_s = coriolis_of(rows - 1, rows_total)
    d_c = [p_buf[8:32, :]]
    d_e = [jnp.minimum(d_c[0], from_east(d_c)[0])]
    d_n = [jnp.minimum(d_c[0], p_buf[9:33, :])]
    d_s = [jnp.minimum(d_c[0], p_buf[7:31, :])]

    for n in range(1, ITERS + 1):
        src, dst = (c_buf, c_alt) if n % 2 else (c_alt, c_buf)

        def dynamics(k, carry):
            up, prev = carry
            read = lambda buf, r: [buf[k, r:r + 24, :]]
            h_new, u_new, v_new, co, links, ratios = level_step(
                k, read(h_buf, 7), read(h_buf, 8), read(h_buf, 9), read(u_buf, 7), read(u_buf, 8),
                read(v_buf, 7), read(v_buf, 8), (d_c, d_e, d_n, d_s), cor_c, cor_s, read(d_buf, 8), up, prev)
            h_buf[k, 8:32, :] = h_new[0]
            u_buf[k, 8:32, :] = u_new[0]
            v_buf[k, 8:32, :] = v_new[0]
            for c in range(7):
                coef[c, k] = co[0][c]
            return links, ratios

        lax.fori_loop(0, LV, dynamics, (zeros_like_tiles(24, 1), zeros_like_tiles(24, 1)), unroll=8)

        starts = (8, 16, 24) if n < ITERS else (12, 20)
        tiles = len(starts)

        def down(k, before):
            co = [[coef[c, k, r0 - 8:r0, :] for r0 in starts] for c in range(6)]
            read = lambda t, shift: [src[t, k, r0 + shift:r0 + shift + 8, :] for r0 in starts]
            now = forward(co, [(read(t, 0), read(t, -1), read(t, 1)) for t in range(4)], before, joined=False)
            for t in range(4):
                for i in range(tiles):
                    solved[k, t, i] = now[t][i]
            return now

        lax.fori_loop(0, LV, down, [zeros_like_tiles(8, tiles) for _ in range(4)], unroll=4)

        def upward(i, m):
            k = LV - 1 - i
            r = [coef[6, k, r0 - 8:r0, :] for r0 in starts]
            m = [[solved[k, t, i] + r[i] * m[t][i] for i in range(tiles)] for t in range(4)]
            for i, r0 in enumerate(starts):
                turned = [[m[t][i]] + [pltpu.roll(m[t][i], 32 * rho, 1) for rho in range(1, 4)] for t in range(4)]
                for s in range(2):
                    for go in range(2):
                        acc = None
                        for gi in range(2):
                            for rho in range(4):
                                term = table[((s * 2 + go) * 2 + gi) * 4 + rho] * turned[2 * s + gi][rho]
                                acc = term if acc is None else acc + term
                        dst[2 * s + go, k, r0:r0 + 8, :] = acc
            return m

        lax.fori_loop(0, LV, upward, [zeros_like_tiles(8, tiles) for _ in range(4)], unroll=4)

    final = c_buf if ITERS % 2 == 0 else c_alt

    def merge(inner, outer, strip, q, j, i):
        turned = pltpu.roll(inner, 4, 0)
        body = jnp.where(low, outer, turned) if i == 0 else jnp.where(low, turned, outer)
        if j == 0:
            return jnp.where(lane < 4, pltpu.roll(strip, (-(32 * q + 4)) % 128, 1), body)
        return jnp.where(lane >= 124, pltpu.roll(strip, (100 - 32 * q) % 128, 1), body)

    leaving = []
    for part in range(4):
        @pl.loop(4 * part, 4 * part + 4, unroll=2)
        def _(k):
            for t in range(NT):
                for i in range(2):
                    strip = final[t // 4, k, 12 + 8 * i:20 + 8 * i, :]
                    for j in range(2):
                        out_c[t, k, 8 * i:8 * i + 8, 128 * j:128 * j + 128] = merge(
                            mid[t, k, j], edge[t, k, j], strip, t % 4, j, i)
        levels = pl.ds(4 * part, 4)
        leaving.append(pltpu.make_async_copy(out_c.at[:, levels], out.at[:, levels], sem.at[part]))
        leaving[part].start()

    off = scal[0] * (LV // 2)

    @pl.loop(0, LV // 2, unroll=4)
    def _(k):
        for f, buf in enumerate((h_buf, u_buf, v_buf)):
            for i in range(2):
                strip = buf[k + off, 12 + 8 * i:20 + 8 * i, :]
                for j in range(2):
                    x = merge(mid_f[f, k + off, j], edge_f[f, k + off, j], strip, 0, j, i)
                    if f == 0:
                        out_h[k, 8 * i:8 * i + 8, 128 * j:128 * j + 128] = x
                    else:
                        out_v[f - 1, k, 8 * i:8 * i + 8, 128 * j:128 * j + 128] = x
    for c in leaving:
        c.wait()


def room(mebibytes):
    return pltpu.CompilerParams(vmem_limit_bytes=mebibytes * 1024 * 1024)


def sds(*shape):
    return jax.ShapeDtypeStruct(shape, F32)


def body(tracers, thickness, velocity, diffusivity, reaction, land_mask, level_count):
    rows_local = thickness.shape[1]
    rows_total = rows_local * lax.axis_size("ty")
    set_index = lax.axis_index("set").astype(jnp.int32)
    row_start = lax.axis_index("ty").astype(jnp.int32) * rows_local
    scal = jnp.stack([set_index, row_start])
    swap = [(0, 1), (1, 0)]
    h_pair = lax.ppermute(thickness, "set", swap)
    v_pair = lax.ppermute(velocity, "set", swap)
    field = sds(LV, 2, 32, 128)
    y_shape = sds(161, 2, 8, 128)
    up_part, dn_part, own, r_own, l_own, c_first, kept, table, s_table = pl.pallas_call(
        tracer_pack_kernel,
        out_shape=[y_shape, y_shape, sds(LV, 4, 16, 128), sds(LV, 16, 128), sds(LV, 16, 128), sds(NT, LV, 2, 32, 128),
                   sds(NT, LV, 2, 8, 128), jax.ShapeDtypeStruct((2, 64, 256), BF16), sds(32, 8, 128)],
        in_specs=[ANY, SMEM], out_specs=[VMEM] * 9,
        scratch_shapes=[pltpu.SemaphoreType.DMA((4,))],
        compiler_params=room(4), name="tracer_pack")(tracers, reaction)
    h_pair, v_pair, up_part, dn_part = lax.optimization_barrier((h_pair, v_pair, up_part, dn_part))
    y_up, y_dn, own_f, h_first, u_first, v_first, d_first, p_first = pl.pallas_call(
        field_pack_kernel, out_shape=[y_shape, y_shape, sds(LV + 1, 16, 128)] + [field] * 4 + [jax.ShapeDtypeStruct((2, 32, 128), jnp.int32)],
        in_specs=[SMEM] + [ANY] * 9, out_specs=[ANY, ANY] + [VMEM] * 6,
        input_output_aliases={8: 0, 9: 1},
        scratch_shapes=[pltpu.VMEM((33, 2, 8, 128), F32), pltpu.VMEM((33, 2, 8, 128), F32),
                        pltpu.VMEM((2, 2, 16, 128), jnp.int32),
                        pltpu.SemaphoreType.DMA((18,)), pltpu.SemaphoreType.DMA((2,))],
        compiler_params=room(4), name="field_pack")(
            scal, thickness, h_pair, velocity, v_pair, diffusivity, land_mask, level_count, up_part, dn_part)
    ty = lax.axis_size("ty")
    north = [(i, i + 1) for i in range(ty - 1)]
    south = [(j, i) for i, j in north]
    y_s = lax.ppermute(y_up, "ty", north)
    y_n = lax.ppermute(y_dn, "ty", south)
    saved, saved_f, mid, mid_f = pl.pallas_call(
        lambda *a: inner_kernel(rows_total, *a),
        out_shape=[sds(ITERS - 1, NT, LV, 2, 8, 128), sds(ITERS - 1, 3, LV, 2, 8, 128), sds(NT, LV, 2, 8, 128), sds(3, LV, 2, 8, 128)],
        in_specs=[SMEM] + [VMEM] * 7, out_specs=[VMEM] * 4,
        scratch_shapes=[pltpu.VMEM((LV, 2, 32, 128), F32)] * 3 + [
            pltpu.VMEM((PER, LV, 2, 32, 128), F32)] * 4 + [
            pltpu.VMEM((LV, PER, 2, 8, 128), F32),
            pltpu.VMEM((LV, PER, 2, 8, 128), F32),
            pltpu.VMEM((6, LV, 2, 16, 128), F32),
            pltpu.VMEM((2, LV, 2, 16, 128), F32)],
        compiler_params=room(26), name="inner")(scal, c_first, h_first, u_first, v_first, d_first, p_first, table)
    y_s, y_n, mid_f = lax.optimization_barrier((y_s, y_n, mid_f))
    halo, x_r, x_l = pl.pallas_call(
        halo_pack_kernel, out_shape=[sds(LV + 1, 5, 8, 128), sds(LV + 1, 24, 128), sds(LV + 1, 24, 128)],
        in_specs=[VMEM] * 5, out_specs=[VMEM] * 3,
        compiler_params=room(4), name="halo_pack")(y_s, y_n, own_f, r_own, l_own)
    tx = lax.axis_size("tx")
    east = [(i, (i + 1) % tx) for i in range(tx)]
    west = [(j, i) for i, j in east]
    x_w = lax.ppermute(x_r, "tx", east)
    x_e = lax.ppermute(x_l, "tx", west)
    edge, edge_f = pl.pallas_call(
        lambda *a: edge_kernel(rows_total, *a),
        out_shape=[sds(NT, LV, 2, 8, 128), sds(3, LV, 2, 8, 128)],
        in_specs=[SMEM] + [VMEM] * 11, out_specs=[VMEM] * 2,
        scratch_shapes=[pltpu.VMEM((PER, LV, 2, 16, 128), F32)] * (2 * ITERS) + [
            pltpu.VMEM((ITERS, 3, LV, 2, 16, 128), F32),
            pltpu.VMEM((LV, 2, 32, 128), F32),
            pltpu.VMEM((2, 32, 128), jnp.int32),
            pltpu.VMEM((LV, PER, 2, 8, 128), F32),
            pltpu.VMEM((LV, PER, 2, 8, 128), F32),
            pltpu.VMEM((6, LV, 2, 8, 128), F32),
            pltpu.VMEM((2, LV, 2, 8, 128), F32),
            pltpu.SemaphoreType.DMA((3 * ITERS,))],
        compiler_params=room(25), name="edge")(
            scal, kept, saved, saved_f, h_first, u_first, v_first, y_s, y_n, d_first, p_first, table)
    return pl.pallas_call(
        lambda *a: strip_kernel(rows_total, *a),
        out_shape=[sds(*tracers.shape), sds(*thickness.shape), sds(*velocity.shape)],
        in_specs=[SMEM] + [VMEM] * 10, out_specs=[ANY, VMEM, VMEM],
        scratch_shapes=[
            pltpu.VMEM((4, LV, 40, 128), F32),
            pltpu.VMEM((4, LV, 40, 128), F32),
            pltpu.VMEM((LV, 40, 128), F32),
            pltpu.VMEM((LV, 40, 128), F32),
            pltpu.VMEM((LV, 40, 128), F32),
            pltpu.VMEM((LV, 40, 128), F32),
            pltpu.VMEM((40, 128), jnp.int32),
            pltpu.VMEM((LV, 4, 3, 8, 128), F32),
            pltpu.VMEM((7, LV, 24, 128), F32),
            pltpu.VMEM((NT, LV, 16, 256), F32),
            pltpu.SemaphoreType.DMA((4,))],
        compiler_params=room(14), name="strips")(scal, own, own_f, halo, x_w, x_e, s_table, mid, mid_f, edge, edge_f)


def solution(mesh):
    placed = (
        P("set", None, "ty", "tx"),
        P("set", "ty", "tx"),
        P(None, "set", "ty", "tx"),
        P(None, "ty", "tx"),
        P("set", None, None),
        P("ty", "tx"),
        P("ty", "tx"),
    )

    def whole(*args):
        return tuple(body(*args))

    return jax.shard_map(
        whole,
        mesh=mesh,
        in_specs=placed,
        out_specs=(P("set", None, "ty", "tx"), P("set", "ty", "tx"), P(None, "set", "ty", "tx")),
        check_vma=False,
    )
```

```python
import jax
import jax.numpy as jnp
from jax import lax
from jax.experimental import pallas as pl
from jax.experimental.pallas import tpu as pltpu
from jax.sharding import PartitionSpec as P

ITERS = 4
DT = 0.2
G = 1.0
ROTATION = 0.5
LV = 16
NT = 16
PER = 8
F32 = jnp.float32
BF16 = jnp.bfloat16
ANY = pl.BlockSpec(memory_space=pl.ANY)
SMEM = pl.BlockSpec(memory_space=pltpu.SMEM)
VMEM = pl.BlockSpec(memory_space=pltpu.VMEM)


def sub_iota(rows=8):
    return lax.broadcasted_iota(jnp.int32, (rows, 128), 0)


def lane_iota(rows=8):
    return lax.broadcasted_iota(jnp.int32, (rows, 128), 1)


def from_east(tiles, joined=True):
    rolled = [pltpu.roll(x, 127, 1) for x in tiles]
    lane = lane_iota(tiles[0].shape[0])
    last = len(tiles) - 1
    return [rolled[i] if i == last or not joined else jnp.where(lane == 127, rolled[i + 1], rolled[i]) for i in range(last + 1)]


def from_west(tiles, joined=True):
    rolled = [pltpu.roll(x, 1, 1) for x in tiles]
    lane = lane_iota(tiles[0].shape[0])
    return [rolled[i] if i == 0 or not joined else jnp.where(lane == 0, rolled[i - 1], rolled[i]) for i in range(len(tiles))]


def coriolis_of(row, rows_total):
    return ROTATION * (2.0 * (row.astype(F32) + 0.5) / rows_total - 1.0)


def level_step(k, h_s, h_c, h_n, u_s, u_c, v_s, v_c, deep, cor_c, cor_s, diff, up, prev):
    d_c, d_e, d_n, d_s = deep
    h_e = from_east(h_c)
    count = len(h_c)
    u_new, v_new, u_flux, v_flux, s_flux = [], [], [], [], []
    for j in range(count):
        un = jnp.where(k < d_e[j], u_c[j] + DT * (cor_c * v_c[j] - G * (h_e[j] - h_c[j])), 0.0)
        vn = jnp.where(k < d_n[j], v_c[j] - DT * (cor_c * u_c[j] + G * (h_n[j] - h_c[j])), 0.0)
        vs = jnp.where(k < d_s[j], v_s[j] - DT * (cor_s * u_s[j] + G * (h_c[j] - h_s[j])), 0.0)
        u_new.append(un)
        v_new.append(vn)
        u_flux.append(un * 0.5 * (h_c[j] + h_e[j]))
        v_flux.append(vn * 0.5 * (h_c[j] + h_n[j]))
        s_flux.append(vs * 0.5 * (h_s[j] + h_c[j]))
    w_flux = from_west(u_flux)
    h_new, coefs, links, ratios = [], [], [], []
    for j in range(count):
        fe, fw, fn, fs = u_flux[j], w_flux[j], v_flux[j], s_flux[j]
        hn = h_c[j] - DT * ((fe - fw) + (fn - fs))
        link = jnp.where(k + 1 < d_c[j], DT * diff[j], 0.0)
        q = jnp.where(k < d_c[j], 1.0 / (hn + up[j] + link - up[j] * prev[j]), 0.0)
        r = link * q
        dq = DT * q
        ce = dq * jnp.maximum(-fe, 0.0)
        cw = dq * jnp.maximum(fw, 0.0)
        cn = dq * jnp.maximum(-fn, 0.0)
        cs = dq * jnp.maximum(fs, 0.0)
        out = (jnp.maximum(fe, 0.0) - jnp.minimum(fw, 0.0)) + (jnp.maximum(fn, 0.0) - jnp.minimum(fs, 0.0))
        ca = q * h_c[j] - dq * out
        h_new.append(hn)
        links.append(link)
        ratios.append(r)
        coefs.append((ca, ce, cw, cn, cs, up[j] * q, r))
    return h_new, u_new, v_new, coefs, links, ratios


def forward(coefs, cells, before, joined=True):
    result = []
    for t, (c, s, n) in enumerate(cells):
        e = from_east(c, joined)
        w = from_west(c, joined)
        result.append([
            ((coefs[0][j] * c[j] + coefs[1][j] * e[j]) + (coefs[2][j] * w[j] + coefs[3][j] * n[j]))
            + (coefs[4][j] * s[j] + coefs[5][j] * before[t][j])
            for j in range(len(c))
        ])
    return result


def react(weights, m):
    x = jnp.concatenate([jnp.concatenate([m[t][j] for t in range(PER)], axis=0) for j in range(2)], axis=1)
    high = x.astype(BF16)
    rest = (x - high.astype(F32)).astype(BF16)
    parts = jnp.concatenate([high, rest, high], axis=0)
    out = jnp.dot(weights[:, :192], parts, preferred_element_type=F32)
    return [[out[8 * t:8 * t + 8, 128 * j:128 * j + 128] for j in range(2)] for t in range(PER)]


def sweep(down, upward, unroll=8):
    def step(i, carry):
        before, m = carry
        if down is not None:
            before = down(i, before)
        if upward is not None:
            m = upward(LV - 1 - i, m)
        return before, m

    start = [zeros_like_tiles(8, 2) for _ in range(PER)]
    lax.fori_loop(0, LV, step, (start if down is not None else 0, start if upward is not None else 0), unroll=unroll)


def zeros_like_tiles(rows, count):
    return [jnp.zeros((rows, 128), F32) for _ in range(count)]


def pack_lanes(sources):
    lane = lane_iota()
    place, slot = lane & 31, lane >> 5
    acc = None
    for q, (left, right) in enumerate(sources):
        a = pltpu.roll(left, (4 + 32 * q) % 128, 1)
        b = pltpu.roll(right, (28 + 32 * q) % 128, 1)
        x = jnp.where(place < 16, a, b)
        acc = x if acc is None else jnp.where(slot == q, x, acc)
    return acc


def to_east(packed, g):
    return pltpu.roll(packed, (4 * g - 24) % 128, 1)


def to_west(packed, g):
    return pltpu.roll(packed, (4 * g - 4) % 128, 1)


def tracer_pack_kernel(tr, reaction, y_up, y_dn, own, x_r, x_l, c_buf, kept, table, s_table, sem):
    copies = [pltpu.make_async_copy(
        tr.at[pl.ds(8 * s, 8), :, :, pl.ds(128 * j, 128)],
        c_buf.at[pl.ds(8 * s, 8), :, j, pl.ds(8, 16), :], sem.at[2 * s + j]) for s in range(2) for j in range(2)]
    for c in copies:
        c.start()
    low = sub_iota() < 4
    place = lane_iota() & 31
    same = (lane_iota() & 7) == sub_iota()
    column = (lane_iota() >> 3) & 7
    for s in range(2):
        blocks = []
        for a in range(PER):
            v = jnp.zeros((8, 128), F32)
            for b in range(PER):
                w = DT * reaction[s, a, b] + (1.0 if a == b else 0.0)
                v = jnp.where(same & (column == b), jnp.full((8, 128), w, F32), v)
            blocks.append(v)
        v = jnp.concatenate(blocks, axis=0)
        high = v.astype(BF16)
        table[s, :, 0:128] = high
        table[s, :, 128:256] = (v - high.astype(F32)).astype(BF16)
    slot = lane_iota() >> 5
    for s in range(2):
        for b in range(PER):
            spread = []
            for go in range(2):
                v = jnp.zeros((8, 128), F32)
                for q in range(4):
                    a = 4 * go + q
                    w = DT * reaction[s, a, b] + (1.0 if a == b else 0.0)
                    v = jnp.where(slot == q, jnp.full((8, 128), w, F32), v)
                spread.append(v)
            for go in range(2):
                tiles = [jnp.where((lane_iota() & 31) == sub_iota() + 8 * r, spread[go], 0.0) for r in range(4)]
                v = jnp.concatenate(tiles, axis=0)
                high = v.astype(BF16)
                lanes = slice(128 * go, 128 * go + 128)
                s_table[s, 32 * b:32 * b + 32, lanes] = high
                s_table[s, 256 + 32 * b:288 + 32 * b, lanes] = high
                s_table[s, 512 + 32 * b:544 + 32 * b, lanes] = (v - high.astype(F32)).astype(BF16)
    for c in copies:
        c.wait()

    @pl.loop(0, LV, unroll=2)
    def _(k):
        for j in range(2):
            for t in range(PER):
                read = lambda b, r: c_buf[t + b, k, j, r:r + 8, :]
                y_up[t * LV + k, j] = jnp.where(low, read(0, 20), read(PER, 16))
                y_dn[t * LV + k, j] = jnp.where(low, read(0, 8), read(PER, 4))
            for t in range(NT):
                kept[t, k, j] = keep_rows(0, lambda r: c_buf[t, k, j, r:r + 8, :])
        for i in range(2):
            rows = slice(8 * i, 8 * i + 8)
            xr, xl = None, None
            for g in range(4):
                packed = pack_lanes([[c_buf[4 * g + q, k, j, 8 + 8 * i:16 + 8 * i, :] for j in range(2)] for q in range(4)])
                own[k, g, rows, :] = packed
                here = place >= 4 * g
                xr = to_east(packed, g) if g == 0 else jnp.where(here, to_east(packed, g), xr)
                xl = to_west(packed, g) if g == 0 else jnp.where(here, to_west(packed, g), xl)
            x_r[k, rows, :] = xr
            x_l[k, rows, :] = xl


def keep_rows(n, read):
    return jnp.where(sub_iota() < 6, read(4 + n), read(16 - n))


def field_pack_kernel(scal, ho, hp, vo, vp, df, land, level, up_in, dn_in, y_up, y_dn, own, h_buf, u_buf, v_buf, d_buf, p_buf,
                      f_up, f_dn, l_buf, sem, out_sem):
    off = scal[0] * (LV // 2)
    part = LV // 2
    rows = pl.ds(8, 16)
    copies = []
    for j in range(2):
        lanes = pl.ds(128 * j, 128)
        for i, (h, v, at) in enumerate(((ho, vo, off), (hp, vp, part - off))):
            levels = pl.ds(at, part)
            copies.append(pltpu.make_async_copy(h.at[:, :, lanes], h_buf.at[levels, j, rows, :], sem.at[6 * j + 3 * i]))
            copies.append(pltpu.make_async_copy(v.at[0, :, :, lanes], u_buf.at[levels, j, rows, :], sem.at[6 * j + 3 * i + 1]))
            copies.append(pltpu.make_async_copy(v.at[1, :, :, lanes], v_buf.at[levels, j, rows, :], sem.at[6 * j + 3 * i + 2]))
        copies.append(pltpu.make_async_copy(df.at[:, :, lanes], d_buf.at[:, j, rows, :], sem.at[12 + j]))
        copies.append(pltpu.make_async_copy(land.at[:, lanes], l_buf.at[0, j], sem.at[14 + j]))
        copies.append(pltpu.make_async_copy(level.at[:, lanes], l_buf.at[1, j], sem.at[16 + j]))
    for c in copies:
        c.start()
    low = sub_iota() < 4
    for c in copies:
        c.wait()

    for j in range(2):
        p_buf[j, 8:24, :] = jnp.where(l_buf[0, j] == 1, l_buf[1, j], 0)

    def put(index, j, first, second):
        f_up[index, j] = jnp.where(low, first(20), second(16))
        f_dn[index, j] = jnp.where(low, first(8), second(4))

    @pl.loop(0, LV, unroll=4)
    def _(k):
        for j in range(2):
            put(k, j, lambda r: h_buf[k, j, r:r + 8, :], lambda r: u_buf[k, j, r:r + 8, :])
            put(16 + k, j, lambda r: v_buf[k, j, r:r + 8, :], lambda r: d_buf[k, j, r:r + 8, :])

    for j in range(2):
        get = lambda r: p_buf[j, r:r + 8, :].astype(F32)
        put(32, j, get, get)
    leaving = [pltpu.make_async_copy(f, y.at[pl.ds(128, 33)], out_sem.at[i]) for i, (f, y) in enumerate(((f_up, y_up), (f_dn, y_dn)))]
    for c in leaving:
        c.start()

    @pl.loop(0, LV, unroll=4)
    def _(k):
        for i in range(2):
            own[k, 8 * i:8 * i + 8, :] = pack_lanes(
                [[buf[k, j, 8 + 8 * i:16 + 8 * i, :] for j in range(2)] for buf in (h_buf, u_buf, v_buf, d_buf)])

    for i in range(2):
        own[LV, 8 * i:8 * i + 8, :] = pack_lanes([[p_buf[j, 8 + 8 * i:16 + 8 * i, :].astype(F32) for j in range(2)]] * 4)
    for c in leaving:
        c.wait()


def inner_kernel(rows_total, scal, c_first, h_first, u_first, v_first, d_buf, p_buf, table, saved, saved_f, mid, mid_f,
                 h_buf, u_buf, v_buf, one_a, one_b, two_a, two_b, solved_a, solved_b, coef, ratio):
    rows = lax.broadcasted_iota(jnp.int32, (16, 128), 0) + scal[1]
    cor_c = coriolis_of(rows, rows_total)
    cor_s = coriolis_of(rows - 1, rows_total)
    d_c = [p_buf[j, 8:24, :] for j in range(2)]
    d_e = [jnp.minimum(a, b) for a, b in zip(d_c, from_east(d_c))]
    d_n = [jnp.minimum(d_c[j], p_buf[j, 9:25, :]) for j in range(2)]
    d_s = [jnp.minimum(d_c[j], p_buf[j, 7:23, :]) for j in range(2)]
    c_one, c_two = (one_a, one_b), (two_a, two_b)
    buffers = ((c_first.at[pl.ds(0, PER)], c_first.at[pl.ds(PER, PER)]), c_one, c_two, c_one, None)
    solved = (solved_a, solved_b)
    pending, keep, slot = None, None, 0
    for n in range(1, ITERS + 1):
        src, dst = buffers[n - 1], buffers[n]
        old = (h_first, u_first, v_first) if n == 1 else (h_buf, u_buf, v_buf)

        def dynamics(k, carry):
            up, prev = carry
            read = lambda buf, r: [buf[k, j, r:r + 16, :] for j in range(2)]
            h_new, u_new, v_new, co, links, ratios = level_step(
                k, read(old[0], 7), read(old[0], 8), read(old[0], 9), read(old[1], 7), read(old[1], 8),
                read(old[2], 7), read(old[2], 8), (d_c, d_e, d_n, d_s), cor_c, cor_s, read(d_buf, 8), up, prev)
            for j in range(2):
                h_buf[k, j, 8:24, :] = h_new[j]
                u_buf[k, j, 8:24, :] = u_new[j]
                v_buf[k, j, 8:24, :] = v_new[j]
                for c in range(6):
                    coef[c, k, j] = co[j][c]
                ratio[n % 2, k, j] = co[j][6]
            return links, ratios

        lax.fori_loop(0, LV, dynamics, (zeros_like_tiles(16, 2), zeros_like_tiles(16, 2)), unroll=4)

        @pl.loop(0, LV)
        def _(k):
            for f, buf in enumerate((h_buf, u_buf, v_buf)):
                for j in range(2):
                    if n < ITERS:
                        saved_f[n - 1, f, k, j] = keep_rows(n, lambda r: buf[k, j, r:r + 8, :])
                    else:
                        mid_f[f, k, j] = buf[k, j, 12:20, :]

        for s in range(2):
            for r0 in ((8, 16) if n < ITERS else (12,)):
                def down(k, before, s=s, r0=r0, src=src, slot=slot):
                    co = [[coef[c, k, j, r0 - 8:r0, :] for j in range(2)] for c in range(6)]
                    read = lambda t, r: [src[s][t, k, j, r:r + 8, :] for j in range(2)]
                    now = forward(co, [(read(t, r0), read(t, r0 - 1), read(t, r0 + 1)) for t in range(PER)], before)
                    for t in range(PER):
                        for j in range(2):
                            solved[slot][k, t, j] = now[t][j]
                    return now

                def upward(k, m, s=s, r0=r0, dst=dst, slot=slot, n=n):
                    r = [ratio[n % 2, k, j, r0 - 8:r0, :] for j in range(2)]
                    m = [[solved[slot][k, t, j] + r[j] * m[t][j] for j in range(2)] for t in range(PER)]
                    outs = react(table[s], m)
                    for t in range(PER):
                        for j in range(2):
                            if n < ITERS:
                                dst[s][t, k, j, r0:r0 + 8, :] = outs[t][j]
                            else:
                                mid[s * PER + t, k, j, 4:12, :] = outs[t][j]
                    return m

                sweep(down, pending)
                pending = upward
                slot = 1 - slot
                if keep is not None:
                    keep()
                    keep = None

        def keep(n=n, dst=dst):
            @pl.loop(0, LV)
            def _(k):
                for t in range(NT):
                    for j in range(2):
                        saved[n - 1, t, k, j] = keep_rows(n, lambda r: dst[t // PER][t % PER, k, j, r:r + 8, :])

    sweep(None, pending)


def halo_pack_kernel(y_s, y_n, own_f, r_own, l_own, halo, x_r, x_l):
    low = sub_iota() < 4
    place = lane_iota() & 31
    for i in range(2):
        rows = slice(8 * i, 8 * i + 8)
        x_r[LV, rows, :] = to_east(own_f[LV, rows, :], 4)
        x_l[LV, rows, :] = to_west(own_f[LV, rows, :], 4)

    @pl.loop(0, LV, unroll=4)
    def _(k):
        for i in range(2):
            rows = slice(8 * i, 8 * i + 8)
            x_r[k, rows, :] = jnp.where(place >= 16, to_east(own_f[k, rows, :], 4), r_own[k, rows, :])
            x_l[k, rows, :] = jnp.where(place >= 16, to_west(own_f[k, rows, :], 4), l_own[k, rows, :])

    def pair(index, j):
        ys, yn = y_s[index, j], y_n[index, j]
        return jnp.where(low, ys, pltpu.roll(yn, 4, 0)), jnp.where(low, pltpu.roll(ys, 4, 0), yn)

    @pl.loop(0, LV, unroll=2)
    def _(k):
        pairs = [[pair(t * LV + k, j) for j in range(2)] for t in range(PER)]
        hu = [pair(128 + k, j) for j in range(2)]
        vd = [pair(144 + k, j) for j in range(2)]
        groups = [[[pairs[4 * (g % 2) + q][j][g // 2] for j in range(2)] for q in range(4)] for g in range(4)]
        groups.append([[x[j][w] for j in range(2)] for x in (hu, vd) for w in range(2)])
        xr, xl = None, None
        for g in range(5):
            packed = pack_lanes(groups[g])
            halo[k, g] = packed
            here = place >= 4 * g
            xr = to_east(packed, g) if g == 0 else jnp.where(here, to_east(packed, g), xr)
            xl = to_west(packed, g) if g == 0 else jnp.where(here, to_west(packed, g), xl)
        x_r[k, 16:24, :] = xr
        x_l[k, 16:24, :] = xl

    packed = pack_lanes([[pair(160, j)[0] for j in range(2)]] * 4)
    for g in range(5):
        halo[LV, g] = packed
    x_r[LV, 16:24, :] = to_east(packed, 4)
    x_l[LV, 16:24, :] = to_west(packed, 4)


def edge_kernel(rows_total, scal, kept, saved, saved_f, h_first, u_first, v_first, y_s, y_n, d_first, p_first, table, mid,
                out_c, out_f, *scratch):
    c_buf = [scratch[2 * n:2 * n + 2] for n in range(ITERS)]
    f_buf, d_buf, p_buf, solved_a, solved_b, coef, ratio, sem = scratch[2 * ITERS:]
    solved = (solved_a, solved_b)
    tracer = [[pltpu.make_async_copy(saved.at[n - 1, pl.ds(PER * s, PER)], c_buf[n][s].at[:, :, :, pl.ds(0, 8), :], sem.at[2 * n + s])
               for s in range(2)] for n in range(1, ITERS)]
    fields = [None] + [pltpu.make_async_copy(saved_f.at[n - 1], f_buf.at[n, :, :, :, pl.ds(0, 8), :], sem.at[2 * ITERS + n]) for n in range(1, ITERS)]
    for c in fields[1:] + tracer[0] + tracer[1] + tracer[2]:
        c.start()
    sub = sub_iota()
    low = sub < 4
    high = jnp.logical_not(low)

    def put(ref, inside, ys, yn, half):
        south = ys if half == 0 else pltpu.roll(ys, 4, 0)
        north = yn if half == 1 else pltpu.roll(yn, 4, 0)
        ref[0:8, :] = jnp.where(low, south, inside)
        pltpu.store(ref.at[pl.ds(4, 8), :], north, mask=high)

    @pl.loop(0, LV, unroll=2)
    def _(k):
        for j in range(2):
            for t in range(PER):
                ys, yn = y_s[t * LV + k, j], y_n[t * LV + k, j]
                for half in range(2):
                    put(c_buf[0][half].at[t, k, j], kept[t + PER * half, k, j], ys, yn, half)
            for f, (buf, index, half) in enumerate(((h_first, 128, 0), (u_first, 128, 1), (v_first, 144, 0))):
                inside = keep_rows(0, lambda r: buf[k, j, r:r + 8, :])
                put(f_buf.at[0, f, k, j], inside, y_s[index + k, j], y_n[index + k, j], half)
            ys, yn = y_s[144 + k, j], y_n[144 + k, j]
            d_buf[k, j, 0:8, :] = ys
            d_buf[k, j, 8:16, :] = d_first[k, j, 8:16, :]
            d_buf[k, j, 16:24, :] = d_first[k, j, 16:24, :]
            d_buf[k, j, 24:32, :] = pltpu.roll(yn, 4, 0)

    for j in range(2):
        p_buf[j, 0:8, :] = y_s[160, j].astype(jnp.int32)
        p_buf[j, 8:24, :] = p_first[j, 8:24, :]
        p_buf[j, 24:32, :] = y_n[160, j].astype(jnp.int32)

    def gather(read, shift):
        return jnp.where(low, read(shift), read(shift + 2))

    pending, slot = None, 0
    for n in range(1, ITERS + 1):
        if n < ITERS:
            fields[n].wait()
            for c in tracer[n - 1]:
                c.wait()

        def at(buf, j, shift):
            return jnp.where(low, buf[j, 4 + n + shift:12 + n + shift, :], buf[j, 20 - n + shift:28 - n + shift, :])

        row = jnp.where(low, sub - 4 + n, sub + 12 - n) + scal[1]
        cor_c = coriolis_of(row, rows_total)
        cor_s = coriolis_of(row - 1, rows_total)
        d_c = [at(p_buf, j, 0) for j in range(2)]
        d_e = [jnp.minimum(a, b) for a, b in zip(d_c, from_east(d_c))]
        d_n = [jnp.minimum(d_c[j], at(p_buf, j, 1)) for j in range(2)]
        d_s = [jnp.minimum(d_c[j], at(p_buf, j, -1)) for j in range(2)]

        def dynamics(k, carry):
            up, prev = carry
            read = lambda f, shift: [gather(lambda r: f_buf[n - 1, f, k, j, r:r + 8, :], shift) for j in range(2)]
            diff = [at(d_buf.at[k], j, 0) for j in range(2)]
            h_new, u_new, v_new, co, links, ratios = level_step(
                k, read(0, 0), read(0, 1), read(0, 2), read(1, 0), read(1, 1), read(2, 0), read(2, 1),
                (d_c, d_e, d_n, d_s), cor_c, cor_s, diff, up, prev)
            for j in range(2):
                for f, x in enumerate((h_new[j], u_new[j], v_new[j])):
                    if n < ITERS:
                        pltpu.store(f_buf.at[n, f, k, j, pl.ds(0, 8), :], x, mask=low)
                        pltpu.store(f_buf.at[n, f, k, j, pl.ds(4, 8), :], x, mask=jnp.logical_not(low))
                    else:
                        out_f[f, k, j] = x
                for c in range(6):
                    coef[c, k, j] = co[j][c]
                ratio[n % 2, k, j] = co[j][6]
            return links, ratios

        lax.fori_loop(0, LV, dynamics, (zeros_like_tiles(8, 2), zeros_like_tiles(8, 2)), unroll=8)

        for s in range(2):
            def down(k, before, s=s, n=n, slot=slot):
                co = [[coef[c, k, j] for j in range(2)] for c in range(6)]

                def read(t, shift):
                    return [gather(lambda r: c_buf[n - 1][s][t, k, j, r:r + 8, :], shift) for j in range(2)]

                now = forward(co, [(read(t, 1), read(t, 0), read(t, 2)) for t in range(PER)], before)
                for t in range(PER):
                    for j in range(2):
                        solved[slot][k, t, j] = now[t][j]
                return now

            def upward(k, m, s=s, n=n, slot=slot):
                r = [ratio[n % 2, k, j] for j in range(2)]
                m = [[solved[slot][k, t, j] + r[j] * m[t][j] for j in range(2)] for t in range(PER)]
                outs = react(table[s], m)
                for t in range(PER):
                    for j in range(2):
                        if n < ITERS:
                            pltpu.store(c_buf[n][s].at[t, k, j, pl.ds(0, 8), :], outs[t][j], mask=low)
                            pltpu.store(c_buf[n][s].at[t, k, j, pl.ds(4, 8), :], outs[t][j], mask=high)
                        else:
                            inside = mid.at[s * PER + t, k, j]
                            out_c[s * PER + t, k, j, 0:8, :] = jnp.where(low, outs[t][j], inside[0:8, :])
                            out_c[s * PER + t, k, j, 8:16, :] = jnp.where(low, inside[8:16, :], outs[t][j])
                return m

            sweep(down, pending)
            pending = upward
            slot = 1 - slot

    sweep(None, pending)


def strip_kernel(rows_total, scal, own, own_f, halo, x_w, x_e, table, mid_f, edge, edge_f, out, out_h, out_v,
                 c_buf, c_alt, h_buf, u_buf, v_buf, d_buf, p_buf, solved, coef, mixed, out_c, o_h, o_v, sem):
    lane = lane_iota()
    place = lane & 31
    slot = lane >> 5
    low = sub_iota() < 4

    def whole(k, g, i, xg):
        rows = slice(8 * i, 8 * i + 8)
        a = pltpu.roll(x_w[k, rows, :], (-4 * xg) % 128, 1)
        b = pltpu.roll(x_e[k, rows, :], (28 - 4 * xg) % 128, 1)
        if i == 2:
            body = halo[k, g]
        elif g == 4:
            body = own_f[k, rows, :]
        else:
            body = own[k, g, rows, :]
        return jnp.where(place < 4, a, jnp.where(place >= 28, b, body))

    def put(ref, i, x):
        if i < 2:
            ref[12 + 8 * i:20 + 8 * i, :] = x
        else:
            pltpu.store(ref.at[pl.ds(8, 8), :], x, mask=low)
            pltpu.store(ref.at[pl.ds(24, 8), :], x, mask=jnp.logical_not(low))

    @pl.loop(0, LV, unroll=4)
    def _(k):
        for i in range(3):
            for g in range(4):
                put(c_buf.at[g, k], i, whole(k, g, i, g))
            x = whole(k, 4, i, 4)
            turned = [x] + [pltpu.roll(x, 32 * rho, 1) for rho in range(1, 4)]
            for f, buf in enumerate((h_buf, u_buf, v_buf, d_buf)):
                y = turned[(3 - f) % 4]
                for q in range(3):
                    y = jnp.where(slot == q, turned[(q - f) % 4], y)
                put(buf.at[k], i, y)

    for i in range(3):
        put(p_buf, i, whole(LV, 4, i, 4).astype(jnp.int32))

    rows = lax.broadcasted_iota(jnp.int32, (24, 128), 0) - 4 + scal[1]
    cor_c = coriolis_of(rows, rows_total)
    cor_s = coriolis_of(rows - 1, rows_total)
    d_c = [p_buf[8:32, :]]
    d_e = [jnp.minimum(d_c[0], from_east(d_c)[0])]
    d_n = [jnp.minimum(d_c[0], p_buf[9:33, :])]
    d_s = [jnp.minimum(d_c[0], p_buf[7:31, :])]

    def merge(body, strip, q, j):
        if j == 0:
            return jnp.where(lane < 4, pltpu.roll(strip, (-(32 * q + 4)) % 128, 1), body)
        return jnp.where(lane >= 124, pltpu.roll(strip, (100 - 32 * q) % 128, 1), body)

    def dynamics(k, carry, side):
        up, prev = carry
        read = lambda buf, r: [buf[k, r:r + 24, :]]
        h_new, u_new, v_new, co, links, ratios = level_step(
            k, read(h_buf, 7), read(h_buf, 8), read(h_buf, 9), read(u_buf, 7), read(u_buf, 8),
            read(v_buf, 7), read(v_buf, 8), (d_c, d_e, d_n, d_s), cor_c, cor_s, read(d_buf, 8), up, prev)
        h_buf[k, 8:32, :] = h_new[0]
        u_buf[k, 8:32, :] = u_new[0]
        v_buf[k, 8:32, :] = v_new[0]
        for c in range(7):
            coef[side, c, k] = co[0][c]
        return links, ratios

    fresh = (zeros_like_tiles(24, 1), zeros_like_tiles(24, 1))
    lax.fori_loop(0, LV, lambda k, carry: dynamics(k, carry, 1), fresh, unroll=8)
    leaving = []
    for n in range(1, ITERS + 1):
        src, dst = (c_buf, c_alt) if n % 2 else (c_alt, c_buf)
        starts = (8, 16, 24) if n < ITERS else (12, 20)
        tiles = len(starts)

        def down(k, carry):
            before, after = carry
            co = [[coef[n % 2, c, k, r0 - 8:r0, :] for r0 in starts] for c in range(6)]
            read = lambda t, shift: [src[t, k, r0 + shift:r0 + shift + 8, :] for r0 in starts]
            now = forward(co, [(read(t, 0), read(t, -1), read(t, 1)) for t in range(4)], before, joined=False)
            for t in range(4):
                for i in range(tiles):
                    solved[k, t, i] = now[t][i]
            if n < ITERS:
                after = dynamics(k, after, (n + 1) % 2)
            return now, after

        lax.fori_loop(0, LV, down, ([zeros_like_tiles(8, tiles) for _ in range(4)], fresh if n < ITERS else 0), unroll=4)

        if n == ITERS - 1:
            off = scal[0] * (LV // 2)

            @pl.loop(0, LV // 2, unroll=4)
            def _(k):
                for f, buf in enumerate((h_buf, u_buf, v_buf)):
                    for i in range(2):
                        strip = buf[k + off, 12 + 8 * i:20 + 8 * i, :]
                        for j in range(2):
                            turned = pltpu.roll(mid_f[f, k + off, j], 4, 0)
                            outer = edge_f[f, k + off, j]
                            body = jnp.where(low, outer, turned) if i == 0 else jnp.where(low, turned, outer)
                            place_at = (k, slice(8 * i, 8 * i + 8), slice(128 * j, 128 * j + 128))
                            if f == 0:
                                o_h[place_at] = merge(body, strip, 0, j)
                            else:
                                o_v[(f - 1,) + place_at] = merge(body, strip, 0, j)

            leaving += [pltpu.make_async_copy(o_h, out_h, sem.at[8]), pltpu.make_async_copy(o_v, out_v, sem.at[9])]
            for c in leaving:
                c.start()

        def upward(i, m):
            k = LV - 1 - i
            r = [coef[n % 2, 6, k, r0 - 8:r0, :] for r0 in starts]
            m = [[solved[k, t, i] + r[i] * m[t][i] for i in range(tiles)] for t in range(4)]
            for t in range(4):
                for i in range(tiles):
                    mixed[t // 2, pl.ds(pl.multiple_of(8 * tiles * k + 8 * i, 8), 8), 128 * (t % 2):128 * (t % 2) + 128] = m[t][i]
            return m

        lax.fori_loop(0, LV, upward, [zeros_like_tiles(8, tiles) for _ in range(4)], unroll=4)

        size = 8 * tiles * LV // 2
        for s in range(2):
            for half in range(2):
                x = mixed[s, size * half:size * half + size, :]
                high = x.astype(BF16)
                rest = (x - high.astype(F32)).astype(BF16)
                made = jnp.dot(jnp.concatenate([high, rest, high], axis=1), table[s], preferred_element_type=F32)
                for k in range(LV // 2):
                    for i, r0 in enumerate(starts):
                        at = 8 * (tiles * k + i)
                        for go in range(2):
                            dst[2 * s + go, LV // 2 * half + k, r0:r0 + 8, :] = made[at:at + 8, 128 * go:128 * go + 128]

    final = c_buf if ITERS % 2 == 0 else c_alt
    for part in range(8):
        @pl.loop(2 * part, 2 * part + 2, unroll=2)
        def _(k):
            for t in range(NT):
                for i in range(2):
                    strip = final[t // 4, k, 12 + 8 * i:20 + 8 * i, :]
                    for j in range(2):
                        out_c[t, k, 8 * i:8 * i + 8, 128 * j:128 * j + 128] = merge(
                            edge[t, k, j, 8 * i:8 * i + 8, :], strip, t % 4, j)
        levels = pl.ds(2 * part, 2)
        leaving.append(pltpu.make_async_copy(out_c.at[:, levels], out.at[:, levels], sem.at[part]))
        leaving[-1].start()

    for c in leaving:
        c.wait()


def room(mebibytes):
    return pltpu.CompilerParams(vmem_limit_bytes=mebibytes * 1024 * 1024)


def sds(*shape):
    return jax.ShapeDtypeStruct(shape, F32)


def body(tracers, thickness, velocity, diffusivity, reaction, land_mask, level_count):
    rows_local = thickness.shape[1]
    rows_total = rows_local * lax.axis_size("ty")
    set_index = lax.axis_index("set").astype(jnp.int32)
    row_start = lax.axis_index("ty").astype(jnp.int32) * rows_local
    scal = jnp.stack([set_index, row_start])
    swap = [(0, 1), (1, 0)]
    h_pair = lax.ppermute(thickness, "set", swap)
    v_pair = lax.ppermute(velocity, "set", swap)
    field = sds(LV, 2, 32, 128)
    y_shape = sds(161, 2, 8, 128)
    up_part, dn_part, own, r_own, l_own, c_first, kept, table, s_table = pl.pallas_call(
        tracer_pack_kernel,
        out_shape=[y_shape, y_shape, sds(LV, 4, 16, 128), sds(LV, 16, 128), sds(LV, 16, 128), sds(NT, LV, 2, 32, 128),
                   sds(NT, LV, 2, 8, 128), jax.ShapeDtypeStruct((2, 64, 256), BF16), jax.ShapeDtypeStruct((2, 768, 256), BF16)],
        in_specs=[ANY, SMEM], out_specs=[VMEM] * 9,
        scratch_shapes=[pltpu.SemaphoreType.DMA((4,))],
        compiler_params=room(4), name="tracer_pack")(tracers, reaction)
    h_pair, v_pair, up_part, dn_part = lax.optimization_barrier((h_pair, v_pair, up_part, dn_part))
    y_up, y_dn, own_f, h_first, u_first, v_first, d_first, p_first = pl.pallas_call(
        field_pack_kernel, out_shape=[y_shape, y_shape, sds(LV + 1, 16, 128)] + [field] * 4 + [jax.ShapeDtypeStruct((2, 32, 128), jnp.int32)],
        in_specs=[SMEM] + [ANY] * 9, out_specs=[ANY, ANY] + [VMEM] * 6,
        input_output_aliases={8: 0, 9: 1},
        scratch_shapes=[pltpu.VMEM((33, 2, 8, 128), F32), pltpu.VMEM((33, 2, 8, 128), F32),
                        pltpu.VMEM((2, 2, 16, 128), jnp.int32),
                        pltpu.SemaphoreType.DMA((18,)), pltpu.SemaphoreType.DMA((2,))],
        compiler_params=room(4), name="field_pack")(
            scal, thickness, h_pair, velocity, v_pair, diffusivity, land_mask, level_count, up_part, dn_part)
    ty = lax.axis_size("ty")
    north = [(i, i + 1) for i in range(ty - 1)]
    south = [(j, i) for i, j in north]
    y_s = lax.ppermute(y_up, "ty", north)
    y_n = lax.ppermute(y_dn, "ty", south)
    saved, saved_f, mid, mid_f = pl.pallas_call(
        lambda *a: inner_kernel(rows_total, *a),
        out_shape=[sds(ITERS - 1, NT, LV, 2, 8, 128), sds(ITERS - 1, 3, LV, 2, 8, 128), sds(NT, LV, 2, 16, 128), sds(3, LV, 2, 8, 128)],
        in_specs=[SMEM] + [VMEM] * 7, out_specs=[VMEM] * 4,
        scratch_shapes=[pltpu.VMEM((LV, 2, 32, 128), F32)] * 3 + [
            pltpu.VMEM((PER, LV, 2, 32, 128), F32)] * 4 + [
            pltpu.VMEM((LV, PER, 2, 8, 128), F32),
            pltpu.VMEM((LV, PER, 2, 8, 128), F32),
            pltpu.VMEM((6, LV, 2, 16, 128), F32),
            pltpu.VMEM((2, LV, 2, 16, 128), F32)],
        compiler_params=room(26), name="inner")(scal, c_first, h_first, u_first, v_first, d_first, p_first, table)
    y_s, y_n, mid_f = lax.optimization_barrier((y_s, y_n, mid_f))
    halo, x_r, x_l = pl.pallas_call(
        halo_pack_kernel, out_shape=[sds(LV + 1, 5, 8, 128), sds(LV + 1, 24, 128), sds(LV + 1, 24, 128)],
        in_specs=[VMEM] * 5, out_specs=[VMEM] * 3,
        compiler_params=room(4), name="halo_pack")(y_s, y_n, own_f, r_own, l_own)
    tx = lax.axis_size("tx")
    east = [(i, (i + 1) % tx) for i in range(tx)]
    west = [(j, i) for i, j in east]
    x_w = lax.ppermute(x_r, "tx", east)
    x_e = lax.ppermute(x_l, "tx", west)
    edge, edge_f = pl.pallas_call(
        lambda *a: edge_kernel(rows_total, *a),
        out_shape=[sds(NT, LV, 2, 16, 128), sds(3, LV, 2, 8, 128)],
        in_specs=[SMEM] + [VMEM] * 12, out_specs=[VMEM] * 2,
        scratch_shapes=[pltpu.VMEM((PER, LV, 2, 16, 128), F32)] * (2 * ITERS) + [
            pltpu.VMEM((ITERS, 3, LV, 2, 16, 128), F32),
            pltpu.VMEM((LV, 2, 32, 128), F32),
            pltpu.VMEM((2, 32, 128), jnp.int32),
            pltpu.VMEM((LV, PER, 2, 8, 128), F32),
            pltpu.VMEM((LV, PER, 2, 8, 128), F32),
            pltpu.VMEM((6, LV, 2, 8, 128), F32),
            pltpu.VMEM((2, LV, 2, 8, 128), F32),
            pltpu.SemaphoreType.DMA((3 * ITERS,))],
        compiler_params=room(25), name="edge")(
            scal, kept, saved, saved_f, h_first, u_first, v_first, y_s, y_n, d_first, p_first, table, mid)
    return pl.pallas_call(
        lambda *a: strip_kernel(rows_total, *a),
        out_shape=[sds(*tracers.shape), sds(*thickness.shape), sds(*velocity.shape)],
        in_specs=[SMEM] + [VMEM] * 9, out_specs=[ANY] * 3,
        scratch_shapes=[
            pltpu.VMEM((4, LV, 40, 128), F32),
            pltpu.VMEM((4, LV, 40, 128), F32),
            pltpu.VMEM((LV, 40, 128), F32),
            pltpu.VMEM((LV, 40, 128), F32),
            pltpu.VMEM((LV, 40, 128), F32),
            pltpu.VMEM((LV, 40, 128), F32),
            pltpu.VMEM((40, 128), jnp.int32),
            pltpu.VMEM((LV, 4, 3, 8, 128), F32),
            pltpu.VMEM((2, 7, LV, 24, 128), F32),
            pltpu.VMEM((2, 24 * LV, 256), F32),
            pltpu.VMEM((NT, LV, 16, 256), F32),
            pltpu.VMEM(thickness.shape, F32),
            pltpu.VMEM(velocity.shape, F32),
            pltpu.SemaphoreType.DMA((10,))],
        compiler_params=room(17), name="strips")(scal, own, own_f, halo, x_w, x_e, s_table, mid_f, edge, edge_f)


def solution(mesh):
    placed = (
        P("set", None, "ty", "tx"),
        P("set", "ty", "tx"),
        P(None, "set", "ty", "tx"),
        P(None, "ty", "tx"),
        P("set", None, None),
        P("ty", "tx"),
        P("ty", "tx"),
    )

    def whole(*args):
        return tuple(body(*args))

    return jax.shard_map(
        whole,
        mesh=mesh,
        in_specs=placed,
        out_specs=(P("set", None, "ty", "tx"), P("set", "ty", "tx"), P(None, "set", "ty", "tx")),
        check_vma=False,
    )
```

```python
import jax
import jax.numpy as jnp
from jax import lax
from jax.experimental import pallas as pl
from jax.experimental.pallas import tpu as pltpu
from jax.sharding import PartitionSpec as P

ITERS = 4
DT = 0.2
G = 1.0
ROTATION = 0.5
LV = 16
NT = 16
PER = 8
F32 = jnp.float32
BF16 = jnp.bfloat16
ANY = pl.BlockSpec(memory_space=pl.ANY)
SMEM = pl.BlockSpec(memory_space=pltpu.SMEM)
VMEM = pl.BlockSpec(memory_space=pltpu.VMEM)


def sub_iota(rows=8):
    return lax.broadcasted_iota(jnp.int32, (rows, 128), 0)


def lane_iota(rows=8):
    return lax.broadcasted_iota(jnp.int32, (rows, 128), 1)


def from_east(tiles, joined=True):
    rolled = [pltpu.roll(x, 127, 1) for x in tiles]
    lane = lane_iota(tiles[0].shape[0])
    last = len(tiles) - 1
    return [rolled[i] if i == last or not joined else jnp.where(lane == 127, rolled[i + 1], rolled[i]) for i in range(last + 1)]


def from_west(tiles, joined=True):
    rolled = [pltpu.roll(x, 1, 1) for x in tiles]
    lane = lane_iota(tiles[0].shape[0])
    return [rolled[i] if i == 0 or not joined else jnp.where(lane == 0, rolled[i - 1], rolled[i]) for i in range(len(tiles))]


def coriolis_of(row, rows_total):
    return ROTATION * (2.0 * (row.astype(F32) + 0.5) / rows_total - 1.0)


def level_step(k, h_c, h_n, u_c, v_c, deep, cor_c, link, up, prev, south):
    d_c, d_e, d_n = deep
    h_e = from_east(h_c)
    count = len(h_c)
    u_new, v_new, u_flux, v_flux = [], [], [], []
    for j in range(count):
        un = jnp.where(k < d_e[j], u_c[j] + DT * (cor_c * v_c[j] - G * (h_e[j] - h_c[j])), 0.0)
        vn = jnp.where(k < d_n[j], v_c[j] - DT * (cor_c * u_c[j] + G * (h_n[j] - h_c[j])), 0.0)
        u_new.append(un)
        v_new.append(vn)
        u_flux.append(un * 0.5 * (h_c[j] + h_e[j]))
        v_flux.append(vn * 0.5 * (h_c[j] + h_n[j]))
    w_flux = from_west(u_flux)
    s_flux = south(v_flux)
    h_new, coefs, ratios = [], [], []
    for j in range(count):
        fe, fw, fn, fs = u_flux[j], w_flux[j], v_flux[j], s_flux[j]
        hn = h_c[j] - DT * ((fe - fw) + (fn - fs))
        q = jnp.where(k < d_c[j], 1.0 / (hn + up[j] + link[j] - up[j] * prev[j]), 0.0)
        r = link[j] * q
        dq = DT * q
        ce = dq * jnp.maximum(-fe, 0.0)
        cw = dq * jnp.maximum(fw, 0.0)
        cn = dq * jnp.maximum(-fn, 0.0)
        cs = dq * jnp.maximum(fs, 0.0)
        out = (jnp.maximum(fe, 0.0) - jnp.minimum(fw, 0.0)) + (jnp.maximum(fn, 0.0) - jnp.minimum(fs, 0.0))
        ca = q * h_c[j] - dq * out
        h_new.append(hn)
        ratios.append(r)
        coefs.append((ca, ce, cw, cn, cs, up[j] * q, r))
    return h_new, u_new, v_new, coefs, ratios


def forward(coefs, cells, before, joined=True):
    result = []
    for t, (c, s, n) in enumerate(cells):
        e = from_east(c, joined)
        w = from_west(c, joined)
        result.append([
            ((coefs[0][j] * c[j] + coefs[1][j] * e[j]) + (coefs[2][j] * w[j] + coefs[3][j] * n[j]))
            + (coefs[4][j] * s[j] + coefs[5][j] * before[t][j])
            for j in range(len(c))
        ])
    return result


def react(weights, m):
    x = jnp.concatenate([jnp.concatenate([m[t][j] for t in range(PER)], axis=0) for j in range(2)], axis=1)
    high = x.astype(BF16)
    rest = (x - high.astype(F32)).astype(BF16)
    parts = jnp.concatenate([high, rest, high], axis=0)
    out = jnp.dot(weights[:, :192], parts, preferred_element_type=F32)
    return [[out[8 * t:8 * t + 8, 128 * j:128 * j + 128] for j in range(2)] for t in range(PER)]


def sweep(down, upward, unroll=8):
    def step(i, carry):
        before, m = carry
        if down is not None:
            before = down(i, before)
        if upward is not None:
            m = upward(LV - 1 - i, m)
        return before, m

    start = [zeros_like_tiles(8, 2) for _ in range(PER)]
    lax.fori_loop(0, LV, step, (start if down is not None else 0, start if upward is not None else 0), unroll=unroll)


def zeros_like_tiles(rows, count):
    return [jnp.zeros((rows, 128), F32) for _ in range(count)]


def pack_lanes(sources):
    lane = lane_iota()
    place, slot = lane & 31, lane >> 5
    acc = None
    for q, (left, right) in enumerate(sources):
        a = pltpu.roll(left, (4 + 32 * q) % 128, 1)
        b = pltpu.roll(right, (28 + 32 * q) % 128, 1)
        x = jnp.where(place < 16, a, b)
        acc = x if acc is None else jnp.where(slot == q, x, acc)
    return acc


def to_east(packed, g):
    return pltpu.roll(packed, (4 * g - 24) % 128, 1)


def to_west(packed, g):
    return pltpu.roll(packed, (4 * g - 4) % 128, 1)


def tracer_pack_kernel(tr, reaction, y_up, y_dn, own, x_r, x_l, c_buf, kept, table, s_table, sem):
    copies = [pltpu.make_async_copy(
        tr.at[pl.ds(8 * s, 8), :, :, pl.ds(128 * j, 128)],
        c_buf.at[pl.ds(8 * s, 8), :, j, pl.ds(8, 16), :], sem.at[2 * s + j]) for s in range(2) for j in range(2)]
    for c in copies:
        c.start()
    low = sub_iota() < 4
    place = lane_iota() & 31
    same = (lane_iota() & 7) == sub_iota()
    column = (lane_iota() >> 3) & 7
    for s in range(2):
        blocks = []
        for a in range(PER):
            v = jnp.zeros((8, 128), F32)
            for b in range(PER):
                w = DT * reaction[s, a, b] + (1.0 if a == b else 0.0)
                v = jnp.where(same & (column == b), jnp.full((8, 128), w, F32), v)
            blocks.append(v)
        v = jnp.concatenate(blocks, axis=0)
        high = v.astype(BF16)
        table[s, :, 0:128] = high
        table[s, :, 128:256] = (v - high.astype(F32)).astype(BF16)
    slot = lane_iota() >> 5
    for s in range(2):
        for b in range(PER):
            spread = []
            for go in range(2):
                v = jnp.zeros((8, 128), F32)
                for q in range(4):
                    a = 4 * go + q
                    w = DT * reaction[s, a, b] + (1.0 if a == b else 0.0)
                    v = jnp.where(slot == q, jnp.full((8, 128), w, F32), v)
                spread.append(v)
            for go in range(2):
                tiles = [jnp.where((lane_iota() & 31) == sub_iota() + 8 * r, spread[go], 0.0) for r in range(4)]
                v = jnp.concatenate(tiles, axis=0)
                high = v.astype(BF16)
                lanes = slice(128 * go, 128 * go + 128)
                s_table[s, 32 * b:32 * b + 32, lanes] = high
                s_table[s, 256 + 32 * b:288 + 32 * b, lanes] = high
                s_table[s, 512 + 32 * b:544 + 32 * b, lanes] = (v - high.astype(F32)).astype(BF16)
    for c in copies:
        c.wait()

    @pl.loop(0, LV, unroll=2)
    def _(k):
        for j in range(2):
            for t in range(PER):
                read = lambda b, r: c_buf[t + b, k, j, r:r + 8, :]
                y_up[t * LV + k, j] = jnp.where(low, read(0, 20), read(PER, 16))
                y_dn[t * LV + k, j] = jnp.where(low, read(0, 8), read(PER, 4))
            for t in range(NT):
                kept[t, k, j] = keep_rows(0, lambda r: c_buf[t, k, j, r:r + 8, :])
        for i in range(2):
            rows = slice(8 * i, 8 * i + 8)
            xr, xl = None, None
            for g in range(4):
                packed = pack_lanes([[c_buf[4 * g + q, k, j, 8 + 8 * i:16 + 8 * i, :] for j in range(2)] for q in range(4)])
                own[k, g, rows, :] = packed
                here = place >= 4 * g
                xr = to_east(packed, g) if g == 0 else jnp.where(here, to_east(packed, g), xr)
                xl = to_west(packed, g) if g == 0 else jnp.where(here, to_west(packed, g), xl)
            x_r[k, rows, :] = xr
            x_l[k, rows, :] = xl


def keep_rows(n, read):
    return jnp.where(sub_iota() < 6, read(4 + n), read(16 - n))


def field_pack_kernel(scal, ho, hp, vo, vp, df, land, level, up_in, dn_in, y_up, y_dn, own, h_buf, u_buf, v_buf, d_buf, p_buf,
                      f_up, f_dn, l_buf, sem, out_sem):
    off = scal[0] * (LV // 2)
    part = LV // 2
    rows = pl.ds(8, 16)
    copies = []
    for j in range(2):
        lanes = pl.ds(128 * j, 128)
        for i, (h, v, at) in enumerate(((ho, vo, off), (hp, vp, part - off))):
            levels = pl.ds(at, part)
            copies.append(pltpu.make_async_copy(h.at[:, :, lanes], h_buf.at[levels, j, rows, :], sem.at[6 * j + 3 * i]))
            copies.append(pltpu.make_async_copy(v.at[0, :, :, lanes], u_buf.at[levels, j, rows, :], sem.at[6 * j + 3 * i + 1]))
            copies.append(pltpu.make_async_copy(v.at[1, :, :, lanes], v_buf.at[levels, j, rows, :], sem.at[6 * j + 3 * i + 2]))
        copies.append(pltpu.make_async_copy(df.at[:, :, lanes], d_buf.at[:, j, rows, :], sem.at[12 + j]))
        copies.append(pltpu.make_async_copy(land.at[:, lanes], l_buf.at[0, j], sem.at[14 + j]))
        copies.append(pltpu.make_async_copy(level.at[:, lanes], l_buf.at[1, j], sem.at[16 + j]))
    for c in copies:
        c.start()
    low = sub_iota() < 4
    for c in copies:
        c.wait()

    for j in range(2):
        p_buf[j, 8:24, :] = jnp.where(l_buf[0, j] == 1, l_buf[1, j], 0)

    @pl.loop(0, LV, unroll=4)
    def _(k):
        for j in range(2):
            d_buf[k, j, 8:24, :] = jnp.where(k + 1 < p_buf[j, 8:24, :], DT * d_buf[k, j, 8:24, :], 0.0)

    def put(index, j, first, second):
        f_up[index, j] = jnp.where(low, first(20), second(16))
        f_dn[index, j] = jnp.where(low, first(8), second(4))

    @pl.loop(0, LV, unroll=4)
    def _(k):
        for j in range(2):
            put(k, j, lambda r: h_buf[k, j, r:r + 8, :], lambda r: u_buf[k, j, r:r + 8, :])
            put(16 + k, j, lambda r: v_buf[k, j, r:r + 8, :], lambda r: d_buf[k, j, r:r + 8, :])

    for j in range(2):
        get = lambda r: p_buf[j, r:r + 8, :].astype(F32)
        put(32, j, get, get)
    leaving = [pltpu.make_async_copy(f, y.at[pl.ds(128, 33)], out_sem.at[i]) for i, (f, y) in enumerate(((f_up, y_up), (f_dn, y_dn)))]
    for c in leaving:
        c.start()

    @pl.loop(0, LV, unroll=4)
    def _(k):
        for i in range(2):
            own[k, 8 * i:8 * i + 8, :] = pack_lanes(
                [[buf[k, j, 8 + 8 * i:16 + 8 * i, :] for j in range(2)] for buf in (h_buf, u_buf, v_buf, d_buf)])

    for i in range(2):
        own[LV, 8 * i:8 * i + 8, :] = pack_lanes([[p_buf[j, 8 + 8 * i:16 + 8 * i, :].astype(F32) for j in range(2)]] * 4)
    for c in leaving:
        c.wait()


def inner_kernel(rows_total, scal, c_first, h_first, u_first, v_first, d_buf, p_buf, table, saved, saved_f, mid, mid_f,
                 h_buf, u_buf, v_buf, flux, one_a, one_b, two_a, two_b, solved_a, solved_b, coef, ratio):
    rows = lax.broadcasted_iota(jnp.int32, (16, 128), 0) + scal[1]
    cor_c = coriolis_of(rows, rows_total)
    d_c = [p_buf[j, 8:24, :] for j in range(2)]
    d_e = [jnp.minimum(a, b) for a, b in zip(d_c, from_east(d_c))]
    d_n = [jnp.minimum(d_c[j], p_buf[j, 9:25, :]) for j in range(2)]
    c_one, c_two = (one_a, one_b), (two_a, two_b)
    buffers = ((c_first.at[pl.ds(0, PER)], c_first.at[pl.ds(PER, PER)]), c_one, c_two, c_one, None)
    solved = (solved_a, solved_b)
    pending, keep, slot = None, None, 0
    for n in range(1, ITERS + 1):
        src, dst = buffers[n - 1], buffers[n]
        old = (h_first, u_first, v_first) if n == 1 else (h_buf, u_buf, v_buf)

        def dynamics(k, carry):
            up, prev = carry
            read = lambda buf, r: [buf[k, j, r:r + 16, :] for j in range(2)]
            link = read(d_buf, 8)

            def south(fluxes):
                for j in range(2):
                    flux[k, j, 8:24, :] = fluxes[j]
                return read(flux, 7)

            h_new, u_new, v_new, co, ratios = level_step(
                k, read(old[0], 8), read(old[0], 9), read(old[1], 8), read(old[2], 8), (d_c, d_e, d_n), cor_c, link, up, prev, south)
            for j in range(2):
                h_buf[k, j, 8:24, :] = h_new[j]
                u_buf[k, j, 8:24, :] = u_new[j]
                v_buf[k, j, 8:24, :] = v_new[j]
                for c in range(6):
                    coef[c, k, j] = co[j][c]
                ratio[n % 2, k, j] = co[j][6]
            return link, ratios

        lax.fori_loop(0, LV, dynamics, (zeros_like_tiles(16, 2), zeros_like_tiles(16, 2)), unroll=4)

        @pl.loop(0, LV, unroll=4)
        def _(k):
            for f, buf in enumerate((h_buf, u_buf, v_buf)):
                for j in range(2):
                    if n < ITERS:
                        saved_f[n - 1, f, k, j] = keep_rows(n, lambda r: buf[k, j, r:r + 8, :])
                    else:
                        mid_f[f, k, j] = buf[k, j, 12:20, :]

        for s in range(2):
            for r0 in ((8, 16) if n < ITERS else (12,)):
                def down(k, before, s=s, r0=r0, src=src, slot=slot):
                    co = [[coef[c, k, j, r0 - 8:r0, :] for j in range(2)] for c in range(6)]
                    read = lambda t, r: [src[s][t, k, j, r:r + 8, :] for j in range(2)]
                    now = forward(co, [(read(t, r0), read(t, r0 - 1), read(t, r0 + 1)) for t in range(PER)], before)
                    for t in range(PER):
                        for j in range(2):
                            solved[slot][k, t, j] = now[t][j]
                    return now

                def upward(k, m, s=s, r0=r0, dst=dst, slot=slot, n=n):
                    r = [ratio[n % 2, k, j, r0 - 8:r0, :] for j in range(2)]
                    m = [[solved[slot][k, t, j] + r[j] * m[t][j] for j in range(2)] for t in range(PER)]
                    outs = react(table[s], m)
                    for t in range(PER):
                        for j in range(2):
                            if n < ITERS:
                                dst[s][t, k, j, r0:r0 + 8, :] = outs[t][j]
                            else:
                                mid[s * PER + t, k, j, 4:12, :] = outs[t][j]
                    return m

                sweep(down, pending)
                pending = upward
                slot = 1 - slot
                if keep is not None:
                    keep()
                    keep = None

        def keep(n=n, dst=dst):
            @pl.loop(0, LV, unroll=2)
            def _(k):
                for t in range(NT):
                    for j in range(2):
                        saved[n - 1, t, k, j] = keep_rows(n, lambda r: dst[t // PER][t % PER, k, j, r:r + 8, :])

    sweep(None, pending)


def halo_pack_kernel(y_s, y_n, own_f, r_own, l_own, halo, x_r, x_l):
    low = sub_iota() < 4
    place = lane_iota() & 31
    for i in range(2):
        rows = slice(8 * i, 8 * i + 8)
        x_r[LV, rows, :] = to_east(own_f[LV, rows, :], 4)
        x_l[LV, rows, :] = to_west(own_f[LV, rows, :], 4)

    @pl.loop(0, LV, unroll=4)
    def _(k):
        for i in range(2):
            rows = slice(8 * i, 8 * i + 8)
            x_r[k, rows, :] = jnp.where(place >= 16, to_east(own_f[k, rows, :], 4), r_own[k, rows, :])
            x_l[k, rows, :] = jnp.where(place >= 16, to_west(own_f[k, rows, :], 4), l_own[k, rows, :])

    def pair(index, j):
        ys, yn = y_s[index, j], y_n[index, j]
        return jnp.where(low, ys, pltpu.roll(yn, 4, 0)), jnp.where(low, pltpu.roll(ys, 4, 0), yn)

    @pl.loop(0, LV, unroll=2)
    def _(k):
        pairs = [[pair(t * LV + k, j) for j in range(2)] for t in range(PER)]
        hu = [pair(128 + k, j) for j in range(2)]
        vd = [pair(144 + k, j) for j in range(2)]
        groups = [[[pairs[4 * (g % 2) + q][j][g // 2] for j in range(2)] for q in range(4)] for g in range(4)]
        groups.append([[x[j][w] for j in range(2)] for x in (hu, vd) for w in range(2)])
        xr, xl = None, None
        for g in range(5):
            packed = pack_lanes(groups[g])
            halo[k, g] = packed
            here = place >= 4 * g
            xr = to_east(packed, g) if g == 0 else jnp.where(here, to_east(packed, g), xr)
            xl = to_west(packed, g) if g == 0 else jnp.where(here, to_west(packed, g), xl)
        x_r[k, 16:24, :] = xr
        x_l[k, 16:24, :] = xl

    packed = pack_lanes([[pair(160, j)[0] for j in range(2)]] * 4)
    for g in range(5):
        halo[LV, g] = packed
    x_r[LV, 16:24, :] = to_east(packed, 4)
    x_l[LV, 16:24, :] = to_west(packed, 4)


def edge_kernel(rows_total, scal, kept, saved, saved_f, h_first, u_first, v_first, y_s, y_n, d_first, p_first, table, mid,
                out_c, out_f, *scratch):
    c_buf = [scratch[2 * n:2 * n + 2] for n in range(ITERS)]
    f_buf, d_buf, p_buf, solved_a, solved_b, coef, ratio = scratch[2 * ITERS:]
    solved = (solved_a, solved_b)
    sub = sub_iota()
    low = sub < 4
    high = jnp.logical_not(low)

    def put(ref, inside, ys, yn, half):
        south = ys if half == 0 else pltpu.roll(ys, 4, 0)
        north = yn if half == 1 else pltpu.roll(yn, 4, 0)
        ref[0:8, :] = jnp.where(low, south, inside)
        pltpu.store(ref.at[pl.ds(4, 8), :], north, mask=high)

    @pl.loop(0, LV, unroll=2)
    def _(k):
        for j in range(2):
            for t in range(PER):
                ys, yn = y_s[t * LV + k, j], y_n[t * LV + k, j]
                for half in range(2):
                    put(c_buf[0][half].at[t, k, j], kept[t + PER * half, k, j], ys, yn, half)
            for f, (buf, index, half) in enumerate(((h_first, 128, 0), (u_first, 128, 1), (v_first, 144, 0))):
                inside = keep_rows(0, lambda r: buf[k, j, r:r + 8, :])
                put(f_buf.at[0, f, k, j], inside, y_s[index + k, j], y_n[index + k, j], half)
            ys, yn = y_s[144 + k, j], y_n[144 + k, j]
            d_buf[k, j, 0:8, :] = ys
            d_buf[k, j, 8:16, :] = d_first[k, j, 8:16, :]
            d_buf[k, j, 16:24, :] = d_first[k, j, 16:24, :]
            d_buf[k, j, 24:32, :] = pltpu.roll(yn, 4, 0)

    for j in range(2):
        p_buf[j, 0:8, :] = y_s[160, j].astype(jnp.int32)
        p_buf[j, 8:24, :] = p_first[j, 8:24, :]
        p_buf[j, 24:32, :] = y_n[160, j].astype(jnp.int32)

    def gather(read, shift):
        return jnp.where(low, read(shift), read(shift + 2))

    pending, slot = None, 0
    for n in range(1, ITERS + 1):
        def at(buf, j, shift):
            return jnp.where(low, buf[j, 4 + n + shift:12 + n + shift, :], buf[j, 20 - n + shift:28 - n + shift, :])

        row = jnp.where(low, sub - 4 + n, sub + 12 - n) + scal[1]
        cor_c = coriolis_of(row, rows_total)
        cor_s = coriolis_of(row - 1, rows_total)
        d_c = [at(p_buf, j, 0) for j in range(2)]
        d_e = [jnp.minimum(a, b) for a, b in zip(d_c, from_east(d_c))]
        d_n = [jnp.minimum(d_c[j], at(p_buf, j, 1)) for j in range(2)]
        d_s = [jnp.minimum(d_c[j], at(p_buf, j, -1)) for j in range(2)]

        def dynamics(k, carry):
            up, prev = carry
            read = lambda f, shift: [gather(lambda r: f_buf[n - 1, f, k, j, r:r + 8, :], shift) for j in range(2)]
            link = [at(d_buf.at[k], j, 0) for j in range(2)]
            h_c = read(0, 1)

            def south(_):
                h_s, u_s, v_s = read(0, 0), read(1, 0), read(2, 0)
                return [jnp.where(k < d_s[j], v_s[j] - DT * (cor_s * u_s[j] + G * (h_c[j] - h_s[j])), 0.0)
                        * 0.5 * (h_s[j] + h_c[j]) for j in range(2)]

            h_new, u_new, v_new, co, ratios = level_step(
                k, h_c, read(0, 2), read(1, 1), read(2, 1), (d_c, d_e, d_n), cor_c, link, up, prev, south)
            for j in range(2):
                for f, x in enumerate((h_new[j], u_new[j], v_new[j])):
                    if n < ITERS:
                        f_buf[n, f, k, j, 0:8, :] = jnp.where(low, x, saved_f[n - 1, f, k, j])
                        pltpu.store(f_buf.at[n, f, k, j, pl.ds(4, 8), :], x, mask=jnp.logical_not(low))
                    else:
                        out_f[f, k, j] = x
                for c in range(6):
                    coef[c, k, j] = co[j][c]
                ratio[n % 2, k, j] = co[j][6]
            return link, ratios

        lax.fori_loop(0, LV, dynamics, (zeros_like_tiles(8, 2), zeros_like_tiles(8, 2)), unroll=8)

        for s in range(2):
            def down(k, before, s=s, n=n, slot=slot):
                co = [[coef[c, k, j] for j in range(2)] for c in range(6)]

                def read(t, shift):
                    return [gather(lambda r: c_buf[n - 1][s][t, k, j, r:r + 8, :], shift) for j in range(2)]

                now = forward(co, [(read(t, 1), read(t, 0), read(t, 2)) for t in range(PER)], before)
                for t in range(PER):
                    for j in range(2):
                        solved[slot][k, t, j] = now[t][j]
                return now

            def upward(k, m, s=s, n=n, slot=slot):
                r = [ratio[n % 2, k, j] for j in range(2)]
                m = [[solved[slot][k, t, j] + r[j] * m[t][j] for j in range(2)] for t in range(PER)]
                outs = react(table[s], m)
                for t in range(PER):
                    for j in range(2):
                        if n < ITERS:
                            c_buf[n][s][t, k, j, 0:8, :] = jnp.where(low, outs[t][j], saved[n - 1, s * PER + t, k, j])
                            pltpu.store(c_buf[n][s].at[t, k, j, pl.ds(4, 8), :], outs[t][j], mask=high)
                        else:
                            inside = mid.at[s * PER + t, k, j]
                            out_c[s * PER + t, k, j, 0:8, :] = jnp.where(low, outs[t][j], inside[0:8, :])
                            out_c[s * PER + t, k, j, 8:16, :] = jnp.where(low, inside[8:16, :], outs[t][j])
                return m

            sweep(down, pending)
            pending = upward
            slot = 1 - slot

    sweep(None, pending)


def strip_kernel(rows_total, scal, own, own_f, halo, x_w, x_e, table, mid_f, edge, edge_f, out, out_h, out_v,
                 c_buf, c_alt, h_buf, u_buf, v_buf, flux, d_buf, p_buf, solved, coef, mixed, out_c, o_h, o_v, sem):
    lane = lane_iota()
    place = lane & 31
    slot = lane >> 5
    low = sub_iota() < 4

    def whole(k, g, i, xg):
        rows = slice(8 * i, 8 * i + 8)
        a = pltpu.roll(x_w[k, rows, :], (-4 * xg) % 128, 1)
        b = pltpu.roll(x_e[k, rows, :], (28 - 4 * xg) % 128, 1)
        if i == 2:
            body = halo[k, g]
        elif g == 4:
            body = own_f[k, rows, :]
        else:
            body = own[k, g, rows, :]
        return jnp.where(place < 4, a, jnp.where(place >= 28, b, body))

    def put(ref, i, x):
        if i < 2:
            ref[12 + 8 * i:20 + 8 * i, :] = x
        else:
            pltpu.store(ref.at[pl.ds(8, 8), :], x, mask=low)
            pltpu.store(ref.at[pl.ds(24, 8), :], x, mask=jnp.logical_not(low))

    @pl.loop(0, LV, unroll=4)
    def _(k):
        for i in range(3):
            for g in range(4):
                put(c_buf.at[g, k], i, whole(k, g, i, g))
            x = whole(k, 4, i, 4)
            turned = [x] + [pltpu.roll(x, 32 * rho, 1) for rho in range(1, 4)]
            for f, buf in enumerate((h_buf, u_buf, v_buf, d_buf)):
                y = turned[(3 - f) % 4]
                for q in range(3):
                    y = jnp.where(slot == q, turned[(q - f) % 4], y)
                put(buf.at[k], i, y)

    for i in range(3):
        put(p_buf, i, whole(LV, 4, i, 4).astype(jnp.int32))

    rows = lax.broadcasted_iota(jnp.int32, (24, 128), 0) - 4 + scal[1]
    cor_c = coriolis_of(rows, rows_total)
    d_c = [p_buf[8:32, :]]
    d_e = [jnp.minimum(d_c[0], from_east(d_c)[0])]
    d_n = [jnp.minimum(d_c[0], p_buf[9:33, :])]

    def merge(body, strip, q, j):
        if j == 0:
            return jnp.where(lane < 4, pltpu.roll(strip, (-(32 * q + 4)) % 128, 1), body)
        return jnp.where(lane >= 124, pltpu.roll(strip, (100 - 32 * q) % 128, 1), body)

    def dynamics(k, carry, side):
        up, prev = carry
        read = lambda buf, r: [buf[k, r:r + 24, :]]
        link = read(d_buf, 8)

        def south(fluxes):
            flux[k, 8:32, :] = fluxes[0]
            return read(flux, 7)

        h_new, u_new, v_new, co, ratios = level_step(
            k, read(h_buf, 8), read(h_buf, 9), read(u_buf, 8), read(v_buf, 8), (d_c, d_e, d_n), cor_c, link, up, prev, south)
        h_buf[k, 8:32, :] = h_new[0]
        u_buf[k, 8:32, :] = u_new[0]
        v_buf[k, 8:32, :] = v_new[0]
        for c in range(7):
            coef[side, c, k] = co[0][c]
        return link, ratios

    fresh = (zeros_like_tiles(24, 1), zeros_like_tiles(24, 1))
    lax.fori_loop(0, LV, lambda k, carry: dynamics(k, carry, 1), fresh, unroll=8)
    leaving = []
    for n in range(1, ITERS + 1):
        src, dst = (c_buf, c_alt) if n % 2 else (c_alt, c_buf)
        starts = (8, 16, 24) if n < ITERS else (12, 20)
        tiles = len(starts)

        def down(k, carry):
            before, after = carry
            co = [[coef[n % 2, c, k, r0 - 8:r0, :] for r0 in starts] for c in range(6)]
            read = lambda t, shift: [src[t, k, r0 + shift:r0 + shift + 8, :] for r0 in starts]
            now = forward(co, [(read(t, 0), read(t, -1), read(t, 1)) for t in range(4)], before, joined=False)
            for t in range(4):
                for i in range(tiles):
                    solved[k, t, i] = now[t][i]
            if n < ITERS:
                after = dynamics(k, after, (n + 1) % 2)
            return now, after

        lax.fori_loop(0, LV, down, ([zeros_like_tiles(8, tiles) for _ in range(4)], fresh if n < ITERS else 0), unroll=4)

        if n == ITERS - 1:
            off = scal[0] * (LV // 2)

            @pl.loop(0, LV // 2, unroll=4)
            def _(k):
                for f, buf in enumerate((h_buf, u_buf, v_buf)):
                    for i in range(2):
                        strip = buf[k + off, 12 + 8 * i:20 + 8 * i, :]
                        for j in range(2):
                            turned = pltpu.roll(mid_f[f, k + off, j], 4, 0)
                            outer = edge_f[f, k + off, j]
                            body = jnp.where(low, outer, turned) if i == 0 else jnp.where(low, turned, outer)
                            place_at = (k, slice(8 * i, 8 * i + 8), slice(128 * j, 128 * j + 128))
                            if f == 0:
                                o_h[place_at] = merge(body, strip, 0, j)
                            else:
                                o_v[(f - 1,) + place_at] = merge(body, strip, 0, j)

            leaving += [pltpu.make_async_copy(o_h, out_h, sem.at[8]), pltpu.make_async_copy(o_v, out_v, sem.at[9])]
            for c in leaving:
                c.start()

        def upward(i, m):
            k = LV - 1 - i
            r = [coef[n % 2, 6, k, r0 - 8:r0, :] for r0 in starts]
            m = [[solved[k, t, i] + r[i] * m[t][i] for i in range(tiles)] for t in range(4)]
            for t in range(4):
                for i in range(tiles):
                    mixed[t // 2, pl.ds(pl.multiple_of(8 * tiles * k + 8 * i, 8), 8), 128 * (t % 2):128 * (t % 2) + 128] = m[t][i]
            return m

        lax.fori_loop(0, LV, upward, [zeros_like_tiles(8, tiles) for _ in range(4)], unroll=4)

        size = 8 * tiles * LV // 2
        for s in range(2):
            for half in range(2):
                x = mixed[s, size * half:size * half + size, :]
                high = x.astype(BF16)
                rest = (x - high.astype(F32)).astype(BF16)
                made = jnp.dot(jnp.concatenate([high, rest, high], axis=1), table[s], preferred_element_type=F32)
                for k in range(LV // 2):
                    for i, r0 in enumerate(starts):
                        at = 8 * (tiles * k + i)
                        for go in range(2):
                            dst[2 * s + go, LV // 2 * half + k, r0:r0 + 8, :] = made[at:at + 8, 128 * go:128 * go + 128]

    final = c_buf if ITERS % 2 == 0 else c_alt
    for part in range(8):
        @pl.loop(2 * part, 2 * part + 2, unroll=2)
        def _(k):
            for t in range(NT):
                for i in range(2):
                    strip = final[t // 4, k, 12 + 8 * i:20 + 8 * i, :]
                    for j in range(2):
                        out_c[t, k, 8 * i:8 * i + 8, 128 * j:128 * j + 128] = merge(
                            edge[t, k, j, 8 * i:8 * i + 8, :], strip, t % 4, j)
        levels = pl.ds(2 * part, 2)
        leaving.append(pltpu.make_async_copy(out_c.at[:, levels], out.at[:, levels], sem.at[part]))
        leaving[-1].start()

    for c in leaving:
        c.wait()


def room(mebibytes):
    return pltpu.CompilerParams(vmem_limit_bytes=mebibytes * 1024 * 1024)


def sds(*shape):
    return jax.ShapeDtypeStruct(shape, F32)


def body(tracers, thickness, velocity, diffusivity, reaction, land_mask, level_count):
    rows_local = thickness.shape[1]
    rows_total = rows_local * lax.axis_size("ty")
    set_index = lax.axis_index("set").astype(jnp.int32)
    row_start = lax.axis_index("ty").astype(jnp.int32) * rows_local
    scal = jnp.stack([set_index, row_start])
    swap = [(0, 1), (1, 0)]
    h_pair = lax.ppermute(thickness, "set", swap)
    v_pair = lax.ppermute(velocity, "set", swap)
    field = sds(LV, 2, 32, 128)
    y_shape = sds(161, 2, 8, 128)
    up_part, dn_part, own, r_own, l_own, c_first, kept, table, s_table = pl.pallas_call(
        tracer_pack_kernel,
        out_shape=[y_shape, y_shape, sds(LV, 4, 16, 128), sds(LV, 16, 128), sds(LV, 16, 128), sds(NT, LV, 2, 32, 128),
                   sds(NT, LV, 2, 8, 128), jax.ShapeDtypeStruct((2, 64, 256), BF16), jax.ShapeDtypeStruct((2, 768, 256), BF16)],
        in_specs=[ANY, SMEM], out_specs=[VMEM] * 9,
        scratch_shapes=[pltpu.SemaphoreType.DMA((4,))],
        compiler_params=room(4), name="tracer_pack")(tracers, reaction)
    h_pair, v_pair, up_part, dn_part = lax.optimization_barrier((h_pair, v_pair, up_part, dn_part))
    y_up, y_dn, own_f, h_first, u_first, v_first, d_first, p_first = pl.pallas_call(
        field_pack_kernel, out_shape=[y_shape, y_shape, sds(LV + 1, 16, 128)] + [field] * 4 + [jax.ShapeDtypeStruct((2, 32, 128), jnp.int32)],
        in_specs=[SMEM] + [ANY] * 9, out_specs=[ANY, ANY] + [VMEM] * 6,
        input_output_aliases={8: 0, 9: 1},
        scratch_shapes=[pltpu.VMEM((33, 2, 8, 128), F32), pltpu.VMEM((33, 2, 8, 128), F32),
                        pltpu.VMEM((2, 2, 16, 128), jnp.int32),
                        pltpu.SemaphoreType.DMA((18,)), pltpu.SemaphoreType.DMA((2,))],
        compiler_params=room(4), name="field_pack")(
            scal, thickness, h_pair, velocity, v_pair, diffusivity, land_mask, level_count, up_part, dn_part)
    ty = lax.axis_size("ty")
    north = [(i, i + 1) for i in range(ty - 1)]
    south = [(j, i) for i, j in north]
    y_s = lax.ppermute(y_up, "ty", north)
    y_n = lax.ppermute(y_dn, "ty", south)
    saved, saved_f, mid, mid_f = pl.pallas_call(
        lambda *a: inner_kernel(rows_total, *a),
        out_shape=[sds(ITERS - 1, NT, LV, 2, 8, 128), sds(ITERS - 1, 3, LV, 2, 8, 128), sds(NT, LV, 2, 16, 128), sds(3, LV, 2, 8, 128)],
        in_specs=[SMEM] + [VMEM] * 7, out_specs=[VMEM] * 4,
        scratch_shapes=[pltpu.VMEM((LV, 2, 32, 128), F32)] * 4 + [
            pltpu.VMEM((PER, LV, 2, 32, 128), F32)] * 4 + [
            pltpu.VMEM((LV, PER, 2, 8, 128), F32),
            pltpu.VMEM((LV, PER, 2, 8, 128), F32),
            pltpu.VMEM((6, LV, 2, 16, 128), F32),
            pltpu.VMEM((2, LV, 2, 16, 128), F32)],
        compiler_params=room(26), name="inner")(scal, c_first, h_first, u_first, v_first, d_first, p_first, table)
    y_s, y_n, mid_f = lax.optimization_barrier((y_s, y_n, mid_f))
    halo, x_r, x_l = pl.pallas_call(
        halo_pack_kernel, out_shape=[sds(LV + 1, 5, 8, 128), sds(LV + 1, 24, 128), sds(LV + 1, 24, 128)],
        in_specs=[VMEM] * 5, out_specs=[VMEM] * 3,
        compiler_params=room(4), name="halo_pack")(y_s, y_n, own_f, r_own, l_own)
    tx = lax.axis_size("tx")
    east = [(i, (i + 1) % tx) for i in range(tx)]
    west = [(j, i) for i, j in east]
    x_w = lax.ppermute(x_r, "tx", east)
    x_e = lax.ppermute(x_l, "tx", west)
    edge, edge_f = pl.pallas_call(
        lambda *a: edge_kernel(rows_total, *a),
        out_shape=[sds(NT, LV, 2, 16, 128), sds(3, LV, 2, 8, 128)],
        in_specs=[SMEM] + [VMEM] * 12, out_specs=[VMEM] * 2,
        scratch_shapes=[pltpu.VMEM((PER, LV, 2, 16, 128), F32)] * (2 * ITERS) + [
            pltpu.VMEM((ITERS, 3, LV, 2, 16, 128), F32),
            pltpu.VMEM((LV, 2, 32, 128), F32),
            pltpu.VMEM((2, 32, 128), jnp.int32),
            pltpu.VMEM((LV, PER, 2, 8, 128), F32),
            pltpu.VMEM((LV, PER, 2, 8, 128), F32),
            pltpu.VMEM((6, LV, 2, 8, 128), F32),
            pltpu.VMEM((2, LV, 2, 8, 128), F32)],
        compiler_params=room(25), name="edge")(
            scal, kept, saved, saved_f, h_first, u_first, v_first, y_s, y_n, d_first, p_first, table, mid)
    return pl.pallas_call(
        lambda *a: strip_kernel(rows_total, *a),
        out_shape=[sds(*tracers.shape), sds(*thickness.shape), sds(*velocity.shape)],
        in_specs=[SMEM] + [VMEM] * 9, out_specs=[ANY] * 3,
        scratch_shapes=[
            pltpu.VMEM((4, LV, 40, 128), F32),
            pltpu.VMEM((4, LV, 40, 128), F32),
            pltpu.VMEM((LV, 40, 128), F32),
            pltpu.VMEM((LV, 40, 128), F32),
            pltpu.VMEM((LV, 40, 128), F32),
            pltpu.VMEM((LV, 40, 128), F32),
            pltpu.VMEM((LV, 40, 128), F32),
            pltpu.VMEM((40, 128), jnp.int32),
            pltpu.VMEM((LV, 4, 3, 8, 128), F32),
            pltpu.VMEM((2, 7, LV, 24, 128), F32),
            pltpu.VMEM((2, 24 * LV, 256), F32),
            pltpu.VMEM((NT, LV, 16, 256), F32),
            pltpu.VMEM(thickness.shape, F32),
            pltpu.VMEM(velocity.shape, F32),
            pltpu.SemaphoreType.DMA((10,))],
        compiler_params=room(17), name="strips")(scal, own, own_f, halo, x_w, x_e, s_table, mid_f, edge, edge_f)


def solution(mesh):
    placed = (
        P("set", None, "ty", "tx"),
        P("set", "ty", "tx"),
        P(None, "set", "ty", "tx"),
        P(None, "ty", "tx"),
        P("set", None, None),
        P("ty", "tx"),
        P("ty", "tx"),
    )

    def whole(*args):
        return tuple(body(*args))

    return jax.shard_map(
        whole,
        mesh=mesh,
        in_specs=placed,
        out_specs=(P("set", None, "ty", "tx"), P("set", "ty", "tx"), P(None, "set", "ty", "tx")),
        check_vma=False,
    )
```

```python
import jax
import jax.numpy as jnp
from jax import lax
from jax.experimental import pallas as pl
from jax.experimental.pallas import tpu as pltpu
from jax.sharding import PartitionSpec as P

ITERS = 4
DT = 0.2
G = 1.0
ROTATION = 0.5
LV = 16
NT = 16
PER = 8
F32 = jnp.float32
BF16 = jnp.bfloat16
ANY = pl.BlockSpec(memory_space=pl.ANY)
SMEM = pl.BlockSpec(memory_space=pltpu.SMEM)
VMEM = pl.BlockSpec(memory_space=pltpu.VMEM)


def sub_iota(rows=8):
    return lax.broadcasted_iota(jnp.int32, (rows, 128), 0)


def lane_iota(rows=8):
    return lax.broadcasted_iota(jnp.int32, (rows, 128), 1)


def from_east(tiles, joined=True):
    rolled = [pltpu.roll(x, 127, 1) for x in tiles]
    lane = lane_iota(tiles[0].shape[0])
    last = len(tiles) - 1
    return [rolled[i] if i == last or not joined else jnp.where(lane == 127, rolled[i + 1], rolled[i]) for i in range(last + 1)]


def from_west(tiles, joined=True):
    rolled = [pltpu.roll(x, 1, 1) for x in tiles]
    lane = lane_iota(tiles[0].shape[0])
    return [rolled[i] if i == 0 or not joined else jnp.where(lane == 0, rolled[i - 1], rolled[i]) for i in range(len(tiles))]


def coriolis_of(row, rows_total):
    return ROTATION * (2.0 * (row.astype(F32) + 0.5) / rows_total - 1.0)


def level_step(k, h_c, h_n, u_c, v_c, deep, cor_c, link, up, prev, south):
    d_c, d_e, d_n = deep
    h_e = from_east(h_c)
    count = len(h_c)
    u_new, v_new, u_flux, v_flux = [], [], [], []
    for j in range(count):
        un = jnp.where(k < d_e[j], u_c[j] + DT * (cor_c * v_c[j] - G * (h_e[j] - h_c[j])), 0.0)
        vn = jnp.where(k < d_n[j], v_c[j] - DT * (cor_c * u_c[j] + G * (h_n[j] - h_c[j])), 0.0)
        u_new.append(un)
        v_new.append(vn)
        u_flux.append(un * 0.5 * (h_c[j] + h_e[j]))
        v_flux.append(vn * 0.5 * (h_c[j] + h_n[j]))
    w_flux = from_west(u_flux)
    s_flux = south(v_flux)
    h_new, coefs, ratios = [], [], []
    for j in range(count):
        fe, fw, fn, fs = u_flux[j], w_flux[j], v_flux[j], s_flux[j]
        hn = h_c[j] - DT * ((fe - fw) + (fn - fs))
        q = jnp.where(k < d_c[j], 1.0 / (hn + up[j] + link[j] - up[j] * prev[j]), 0.0)
        r = link[j] * q
        dq = DT * q
        ce = dq * jnp.maximum(-fe, 0.0)
        cw = dq * jnp.maximum(fw, 0.0)
        cn = dq * jnp.maximum(-fn, 0.0)
        cs = dq * jnp.maximum(fs, 0.0)
        out = (jnp.maximum(fe, 0.0) - jnp.minimum(fw, 0.0)) + (jnp.maximum(fn, 0.0) - jnp.minimum(fs, 0.0))
        ca = q * h_c[j] - dq * out
        h_new.append(hn)
        ratios.append(r)
        coefs.append((ca, ce, cw, cn, cs, up[j] * q, r))
    return h_new, u_new, v_new, coefs, ratios


def forward(coefs, cells, before, joined=True):
    result = []
    for t, (c, s, n) in enumerate(cells):
        e = from_east(c, joined)
        w = from_west(c, joined)
        result.append([
            ((coefs[0][j] * c[j] + coefs[1][j] * e[j]) + (coefs[2][j] * w[j] + coefs[3][j] * n[j]))
            + (coefs[4][j] * s[j] + coefs[5][j] * before[t][j])
            for j in range(len(c))
        ])
    return result


def react(weights, m):
    x = jnp.concatenate([jnp.concatenate([m[t][j] for t in range(PER)], axis=0) for j in range(2)], axis=1)
    high = x.astype(BF16)
    rest = (x - high.astype(F32)).astype(BF16)
    parts = jnp.concatenate([high, rest, high], axis=0)
    out = jnp.dot(weights[:, :192], parts, preferred_element_type=F32)
    return [[out[8 * t:8 * t + 8, 128 * j:128 * j + 128] for j in range(2)] for t in range(PER)]


def sweep(down, upward, unroll=8):
    def step(i, carry):
        before, m = carry
        if down is not None:
            before = down(i, before)
        if upward is not None:
            m = upward(LV - 1 - i, m)
        return before, m

    start = [zeros_like_tiles(8, 2) for _ in range(PER)]
    lax.fori_loop(0, LV, step, (start if down is not None else 0, start if upward is not None else 0), unroll=unroll)


def zeros_like_tiles(rows, count):
    return [jnp.zeros((rows, 128), F32) for _ in range(count)]


def pack_lanes(sources):
    lane = lane_iota()
    place, slot = lane & 31, lane >> 5
    acc = None
    for q, (left, right) in enumerate(sources):
        a = pltpu.roll(left, (4 + 32 * q) % 128, 1)
        b = pltpu.roll(right, (28 + 32 * q) % 128, 1)
        x = jnp.where(place < 16, a, b)
        acc = x if acc is None else jnp.where(slot == q, x, acc)
    return acc


def to_east(packed, g):
    return pltpu.roll(packed, (4 * g - 24) % 128, 1)


def to_west(packed, g):
    return pltpu.roll(packed, (4 * g - 4) % 128, 1)


def tracer_pack_kernel(tr, reaction, y_up, y_dn, own, x_r, x_l, c_buf, kept, table, s_table, sem):
    copies = [pltpu.make_async_copy(
        tr.at[pl.ds(8 * s, 8), :, :, pl.ds(128 * j, 128)],
        c_buf.at[pl.ds(8 * s, 8), :, j, pl.ds(8, 16), :], sem.at[2 * s + j]) for s in range(2) for j in range(2)]
    for c in copies:
        c.start()
    low = sub_iota() < 4
    place = lane_iota() & 31
    same = (lane_iota() & 7) == sub_iota()
    column = (lane_iota() >> 3) & 7
    for s in range(2):
        blocks = []
        for a in range(PER):
            v = jnp.zeros((8, 128), F32)
            for b in range(PER):
                w = DT * reaction[s, a, b] + (1.0 if a == b else 0.0)
                v = jnp.where(same & (column == b), jnp.full((8, 128), w, F32), v)
            blocks.append(v)
        v = jnp.concatenate(blocks, axis=0)
        high = v.astype(BF16)
        table[s, :, 0:128] = high
        table[s, :, 128:256] = (v - high.astype(F32)).astype(BF16)
    slot = lane_iota() >> 5
    for s in range(2):
        for b in range(PER):
            spread = []
            for go in range(2):
                v = jnp.zeros((8, 128), F32)
                for q in range(4):
                    a = 4 * go + q
                    w = DT * reaction[s, a, b] + (1.0 if a == b else 0.0)
                    v = jnp.where(slot == q, jnp.full((8, 128), w, F32), v)
                spread.append(v)
            for go in range(2):
                tiles = [jnp.where((lane_iota() & 31) == sub_iota() + 8 * r, spread[go], 0.0) for r in range(4)]
                v = jnp.concatenate(tiles, axis=0)
                high = v.astype(BF16)
                lanes = slice(128 * go, 128 * go + 128)
                s_table[s, 32 * b:32 * b + 32, lanes] = high
                s_table[s, 256 + 32 * b:288 + 32 * b, lanes] = high
                s_table[s, 512 + 32 * b:544 + 32 * b, lanes] = (v - high.astype(F32)).astype(BF16)
    for c in copies:
        c.wait()

    @pl.loop(0, LV, unroll=2)
    def _(k):
        for j in range(2):
            for t in range(PER):
                read = lambda b, r: c_buf[t + b, k, j, r:r + 8, :]
                y_up[t * LV + k, j] = jnp.where(low, read(0, 20), read(PER, 16))
                y_dn[t * LV + k, j] = jnp.where(low, read(0, 8), read(PER, 4))
            for t in range(NT):
                kept[t, k, j] = keep_rows(0, lambda r: c_buf[t, k, j, r:r + 8, :])
        for i in range(2):
            rows = slice(8 * i, 8 * i + 8)
            xr, xl = None, None
            for g in range(4):
                packed = pack_lanes([[c_buf[4 * g + q, k, j, 8 + 8 * i:16 + 8 * i, :] for j in range(2)] for q in range(4)])
                own[k, g, rows, :] = packed
                here = place >= 4 * g
                xr = to_east(packed, g) if g == 0 else jnp.where(here, to_east(packed, g), xr)
                xl = to_west(packed, g) if g == 0 else jnp.where(here, to_west(packed, g), xl)
            x_r[k, rows, :] = xr
            x_l[k, rows, :] = xl


def keep_rows(n, read):
    return jnp.where(sub_iota() < 6, read(4 + n), read(16 - n))


def field_pack_kernel(scal, ho, hp, vo, vp, df, land, level, up_in, dn_in, y_up, y_dn, own, h_buf, u_buf, v_buf, d_buf, p_buf,
                      f_up, f_dn, l_buf, sem, out_sem):
    off = scal[0] * (LV // 2)
    part = LV // 2
    rows = pl.ds(8, 16)
    copies = []
    for j in range(2):
        lanes = pl.ds(128 * j, 128)
        for i, (h, v, at) in enumerate(((ho, vo, off), (hp, vp, part - off))):
            levels = pl.ds(at, part)
            copies.append(pltpu.make_async_copy(h.at[:, :, lanes], h_buf.at[levels, j, rows, :], sem.at[6 * j + 3 * i]))
            copies.append(pltpu.make_async_copy(v.at[0, :, :, lanes], u_buf.at[levels, j, rows, :], sem.at[6 * j + 3 * i + 1]))
            copies.append(pltpu.make_async_copy(v.at[1, :, :, lanes], v_buf.at[levels, j, rows, :], sem.at[6 * j + 3 * i + 2]))
        copies.append(pltpu.make_async_copy(df.at[:, :, lanes], d_buf.at[:, j, rows, :], sem.at[12 + j]))
        copies.append(pltpu.make_async_copy(land.at[:, lanes], l_buf.at[0, j], sem.at[14 + j]))
        copies.append(pltpu.make_async_copy(level.at[:, lanes], l_buf.at[1, j], sem.at[16 + j]))
    for c in copies:
        c.start()
    low = sub_iota() < 4
    for c in copies:
        c.wait()

    for j in range(2):
        p_buf[j, 8:24, :] = jnp.where(l_buf[0, j] == 1, l_buf[1, j], 0)

    @pl.loop(0, LV, unroll=4)
    def _(k):
        for j in range(2):
            d_buf[k, j, 8:24, :] = jnp.where(k + 1 < p_buf[j, 8:24, :], DT * d_buf[k, j, 8:24, :], 0.0)

    def put(index, j, first, second):
        f_up[index, j] = jnp.where(low, first(20), second(16))
        f_dn[index, j] = jnp.where(low, first(8), second(4))

    @pl.loop(0, LV, unroll=4)
    def _(k):
        for j in range(2):
            put(k, j, lambda r: h_buf[k, j, r:r + 8, :], lambda r: u_buf[k, j, r:r + 8, :])
            put(16 + k, j, lambda r: v_buf[k, j, r:r + 8, :], lambda r: d_buf[k, j, r:r + 8, :])

    for j in range(2):
        get = lambda r: p_buf[j, r:r + 8, :].astype(F32)
        put(32, j, get, get)
    leaving = [pltpu.make_async_copy(f, y.at[pl.ds(128, 33)], out_sem.at[i]) for i, (f, y) in enumerate(((f_up, y_up), (f_dn, y_dn)))]
    for c in leaving:
        c.start()

    @pl.loop(0, LV, unroll=4)
    def _(k):
        for i in range(2):
            own[k, 8 * i:8 * i + 8, :] = pack_lanes(
                [[buf[k, j, 8 + 8 * i:16 + 8 * i, :] for j in range(2)] for buf in (h_buf, u_buf, v_buf, d_buf)])

    for i in range(2):
        own[LV, 8 * i:8 * i + 8, :] = pack_lanes([[p_buf[j, 8 + 8 * i:16 + 8 * i, :].astype(F32) for j in range(2)]] * 4)
    for c in leaving:
        c.wait()


def inner_kernel(rows_total, scal, c_first, h_first, u_first, v_first, d_buf, p_buf, table, one_a, one_b, two_a, two_b, three_a, three_b, saved_f, mid, mid_f,
                 h_buf, u_buf, v_buf, flux, solved_a, solved_b, coef, ratio):
    rows = lax.broadcasted_iota(jnp.int32, (16, 128), 0) + scal[1]
    cor_c = coriolis_of(rows, rows_total)
    d_c = [p_buf[j, 8:24, :] for j in range(2)]
    d_e = [jnp.minimum(a, b) for a, b in zip(d_c, from_east(d_c))]
    d_n = [jnp.minimum(d_c[j], p_buf[j, 9:25, :]) for j in range(2)]
    buffers = ((c_first.at[pl.ds(0, PER)], c_first.at[pl.ds(PER, PER)]), (one_a, one_b), (two_a, two_b), (three_a, three_b), None)
    solved = (solved_a, solved_b)
    pending, slot = None, 0
    for n in range(1, ITERS + 1):
        src, dst = buffers[n - 1], buffers[n]
        old = (h_first, u_first, v_first) if n == 1 else (h_buf, u_buf, v_buf)

        def dynamics(k, carry):
            up, prev = carry
            read = lambda buf, r: [buf[k, j, r:r + 16, :] for j in range(2)]
            link = read(d_buf, 8)

            def south(fluxes):
                for j in range(2):
                    flux[k, j, 8:24, :] = fluxes[j]
                return read(flux, 7)

            h_new, u_new, v_new, co, ratios = level_step(
                k, read(old[0], 8), read(old[0], 9), read(old[1], 8), read(old[2], 8), (d_c, d_e, d_n), cor_c, link, up, prev, south)
            for j in range(2):
                h_buf[k, j, 8:24, :] = h_new[j]
                u_buf[k, j, 8:24, :] = u_new[j]
                v_buf[k, j, 8:24, :] = v_new[j]
                for c in range(6):
                    coef[c, k, j] = co[j][c]
                ratio[n % 2, k, j] = co[j][6]
            return link, ratios

        lax.fori_loop(0, LV, dynamics, (zeros_like_tiles(16, 2), zeros_like_tiles(16, 2)), unroll=4)

        @pl.loop(0, LV, unroll=4)
        def _(k):
            for f, buf in enumerate((h_buf, u_buf, v_buf)):
                for j in range(2):
                    if n < ITERS:
                        saved_f[n - 1, f, k, j] = keep_rows(n, lambda r: buf[k, j, r:r + 8, :])
                    else:
                        mid_f[f, k, j] = buf[k, j, 12:20, :]

        for s in range(2):
            for r0 in ((8, 16) if n < ITERS else (12,)):
                def down(k, before, s=s, r0=r0, src=src, slot=slot, base=r0 if n == 1 else r0 - 4):
                    co = [[coef[c, k, j, r0 - 8:r0, :] for j in range(2)] for c in range(6)]
                    read = lambda t, r: [src[s][t, k, j, r:r + 8, :] for j in range(2)]
                    now = forward(co, [(read(t, base), read(t, base - 1), read(t, base + 1)) for t in range(PER)], before)
                    for t in range(PER):
                        for j in range(2):
                            solved[slot][k, t, j] = now[t][j]
                    return now

                def upward(k, m, s=s, r0=r0, dst=dst, slot=slot, n=n):
                    r = [ratio[n % 2, k, j, r0 - 8:r0, :] for j in range(2)]
                    m = [[solved[slot][k, t, j] + r[j] * m[t][j] for j in range(2)] for t in range(PER)]
                    outs = react(table[s], m)
                    for t in range(PER):
                        for j in range(2):
                            if n < ITERS:
                                dst[s][t, k, j, r0 - 4:r0 + 4, :] = outs[t][j]
                            else:
                                mid[s * PER + t, k, j, 4:12, :] = outs[t][j]
                    return m

                sweep(down, pending)
                pending = upward
                slot = 1 - slot

    sweep(None, pending)


def halo_pack_kernel(y_s, y_n, own_f, r_own, l_own, halo, x_r, x_l):
    low = sub_iota() < 4
    place = lane_iota() & 31
    for i in range(2):
        rows = slice(8 * i, 8 * i + 8)
        x_r[LV, rows, :] = to_east(own_f[LV, rows, :], 4)
        x_l[LV, rows, :] = to_west(own_f[LV, rows, :], 4)

    @pl.loop(0, LV, unroll=4)
    def _(k):
        for i in range(2):
            rows = slice(8 * i, 8 * i + 8)
            x_r[k, rows, :] = jnp.where(place >= 16, to_east(own_f[k, rows, :], 4), r_own[k, rows, :])
            x_l[k, rows, :] = jnp.where(place >= 16, to_west(own_f[k, rows, :], 4), l_own[k, rows, :])

    def pair(index, j):
        ys, yn = y_s[index, j], y_n[index, j]
        return jnp.where(low, ys, pltpu.roll(yn, 4, 0)), jnp.where(low, pltpu.roll(ys, 4, 0), yn)

    @pl.loop(0, LV, unroll=2)
    def _(k):
        pairs = [[pair(t * LV + k, j) for j in range(2)] for t in range(PER)]
        hu = [pair(128 + k, j) for j in range(2)]
        vd = [pair(144 + k, j) for j in range(2)]
        groups = [[[pairs[4 * (g % 2) + q][j][g // 2] for j in range(2)] for q in range(4)] for g in range(4)]
        groups.append([[x[j][w] for j in range(2)] for x in (hu, vd) for w in range(2)])
        xr, xl = None, None
        for g in range(5):
            packed = pack_lanes(groups[g])
            halo[k, g] = packed
            here = place >= 4 * g
            xr = to_east(packed, g) if g == 0 else jnp.where(here, to_east(packed, g), xr)
            xl = to_west(packed, g) if g == 0 else jnp.where(here, to_west(packed, g), xl)
        x_r[k, 16:24, :] = xr
        x_l[k, 16:24, :] = xl

    packed = pack_lanes([[pair(160, j)[0] for j in range(2)]] * 4)
    for g in range(5):
        halo[LV, g] = packed
    x_r[LV, 16:24, :] = to_east(packed, 4)
    x_l[LV, 16:24, :] = to_west(packed, 4)


def edge_kernel(rows_total, scal, kept, one_a, one_b, two_a, two_b, three_a, three_b, saved_f, h_first, u_first, v_first, y_s, y_n, d_first, p_first, table, mid,
                out_c, out_f, *scratch):
    c_buf = [scratch[2 * (n % 2):2 * (n % 2) + 2] for n in range(ITERS)]
    f_buf, d_buf, p_buf, solved_a, solved_b, coef, ratio = scratch[4:]
    solved = (solved_a, solved_b)
    stages = (None, (one_a, one_b), (two_a, two_b), (three_a, three_b))
    sub = sub_iota()
    low, six = sub < 4, sub < 6
    high = jnp.logical_not(low)

    def put(ref, inside, ys, yn, half):
        south = ys if half == 0 else pltpu.roll(ys, 4, 0)
        north = yn if half == 1 else pltpu.roll(yn, 4, 0)
        ref[0:8, :] = jnp.where(low, south, inside)
        pltpu.store(ref.at[pl.ds(4, 8), :], north, mask=high)

    @pl.loop(0, LV, unroll=2)
    def _(k):
        for j in range(2):
            for t in range(PER):
                ys, yn = y_s[t * LV + k, j], y_n[t * LV + k, j]
                for half in range(2):
                    put(c_buf[0][half].at[t, k, j], kept[t + PER * half, k, j], ys, yn, half)
            for f, (buf, index, half) in enumerate(((h_first, 128, 0), (u_first, 128, 1), (v_first, 144, 0))):
                inside = keep_rows(0, lambda r: buf[k, j, r:r + 8, :])
                put(f_buf.at[0, f, k, j], inside, y_s[index + k, j], y_n[index + k, j], half)
            ys, yn = y_s[144 + k, j], y_n[144 + k, j]
            d_buf[k, j, 0:8, :] = ys
            d_buf[k, j, 8:16, :] = d_first[k, j, 8:16, :]
            d_buf[k, j, 16:24, :] = d_first[k, j, 16:24, :]
            d_buf[k, j, 24:32, :] = pltpu.roll(yn, 4, 0)

    for j in range(2):
        p_buf[j, 0:8, :] = y_s[160, j].astype(jnp.int32)
        p_buf[j, 8:24, :] = p_first[j, 8:24, :]
        p_buf[j, 24:32, :] = y_n[160, j].astype(jnp.int32)

    def gather(read, shift):
        return jnp.where(low, read(shift), read(shift + 2))

    pending, slot = None, 0
    for n in range(1, ITERS + 1):
        def at(buf, j, shift):
            return jnp.where(low, buf[j, 4 + n + shift:12 + n + shift, :], buf[j, 20 - n + shift:28 - n + shift, :])

        row = jnp.where(low, sub - 4 + n, sub + 12 - n) + scal[1]
        cor_c = coriolis_of(row, rows_total)
        cor_s = coriolis_of(row - 1, rows_total)
        d_c = [at(p_buf, j, 0) for j in range(2)]
        d_e = [jnp.minimum(a, b) for a, b in zip(d_c, from_east(d_c))]
        d_n = [jnp.minimum(d_c[j], at(p_buf, j, 1)) for j in range(2)]
        d_s = [jnp.minimum(d_c[j], at(p_buf, j, -1)) for j in range(2)]

        def dynamics(k, carry):
            up, prev = carry
            read = lambda f, shift: [gather(lambda r: f_buf[n - 1, f, k, j, r:r + 8, :], shift) for j in range(2)]
            link = [at(d_buf.at[k], j, 0) for j in range(2)]
            h_c = read(0, 1)

            def south(_):
                h_s, u_s, v_s = read(0, 0), read(1, 0), read(2, 0)
                return [jnp.where(k < d_s[j], v_s[j] - DT * (cor_s * u_s[j] + G * (h_c[j] - h_s[j])), 0.0)
                        * 0.5 * (h_s[j] + h_c[j]) for j in range(2)]

            h_new, u_new, v_new, co, ratios = level_step(
                k, h_c, read(0, 2), read(1, 1), read(2, 1), (d_c, d_e, d_n), cor_c, link, up, prev, south)
            for j in range(2):
                for f, x in enumerate((h_new[j], u_new[j], v_new[j])):
                    if n < ITERS:
                        f_buf[n, f, k, j, 0:8, :] = jnp.where(low, x, saved_f[n - 1, f, k, j])
                        pltpu.store(f_buf.at[n, f, k, j, pl.ds(4, 8), :], x, mask=jnp.logical_not(low))
                    else:
                        out_f[f, k, j] = x
                for c in range(6):
                    coef[c, k, j] = co[j][c]
                ratio[n % 2, k, j] = co[j][6]
            return link, ratios

        lax.fori_loop(0, LV, dynamics, (zeros_like_tiles(8, 2), zeros_like_tiles(8, 2)), unroll=8)

        for s in range(2):
            def down(k, before, s=s, n=n, slot=slot):
                co = [[coef[c, k, j] for j in range(2)] for c in range(6)]

                def read(t, shift):
                    return [gather(lambda r: c_buf[n - 1][s][t, k, j, r:r + 8, :], shift) for j in range(2)]

                now = forward(co, [(read(t, 1), read(t, 0), read(t, 2)) for t in range(PER)], before)
                for t in range(PER):
                    for j in range(2):
                        solved[slot][k, t, j] = now[t][j]
                return now

            def upward(k, m, s=s, n=n, slot=slot):
                r = [ratio[n % 2, k, j] for j in range(2)]
                m = [[solved[slot][k, t, j] + r[j] * m[t][j] for j in range(2)] for t in range(PER)]
                outs = react(table[s], m)
                for t in range(PER):
                    for j in range(2):
                        if n < ITERS:
                            inside = stages[n][s].at[t, k, j]
                            first = c_buf[n][s].at[t, k, j, pl.ds(0, 8), :]
                            pltpu.store(first, outs[t][j], mask=low)
                            pltpu.store(first, inside[n:n + 8, :], mask=high & six)
                            pltpu.store(first, inside[12 - n:20 - n, :], mask=jnp.logical_not(six))
                            pltpu.store(c_buf[n][s].at[t, k, j, pl.ds(4, 8), :], outs[t][j], mask=high)
                        else:
                            inside = mid.at[s * PER + t, k, j]
                            out_c[s * PER + t, k, j, 0:8, :] = jnp.where(low, outs[t][j], inside[0:8, :])
                            out_c[s * PER + t, k, j, 8:16, :] = jnp.where(low, inside[8:16, :], outs[t][j])
                return m

            sweep(down, pending)
            pending = upward
            slot = 1 - slot

    sweep(None, pending)


def strip_kernel(rows_total, scal, own, own_f, halo, x_w, x_e, table, mid_f, edge, edge_f, out, out_h, out_v,
                 c_buf, c_alt, h_buf, u_buf, v_buf, flux, d_buf, p_buf, solved, coef, mixed, out_c, o_h, o_v, sem):
    lane = lane_iota()
    place = lane & 31
    slot = lane >> 5
    low = sub_iota() < 4

    def whole(k, g, i, xg):
        rows = slice(8 * i, 8 * i + 8)
        a = pltpu.roll(x_w[k, rows, :], (-4 * xg) % 128, 1)
        b = pltpu.roll(x_e[k, rows, :], (28 - 4 * xg) % 128, 1)
        if i == 2:
            body = halo[k, g]
        elif g == 4:
            body = own_f[k, rows, :]
        else:
            body = own[k, g, rows, :]
        return jnp.where(place < 4, a, jnp.where(place >= 28, b, body))

    def put(ref, i, x):
        if i < 2:
            ref[12 + 8 * i:20 + 8 * i, :] = x
        else:
            pltpu.store(ref.at[pl.ds(8, 8), :], x, mask=low)
            pltpu.store(ref.at[pl.ds(24, 8), :], x, mask=jnp.logical_not(low))

    @pl.loop(0, LV, unroll=4)
    def _(k):
        for i in range(3):
            for g in range(4):
                put(c_buf.at[g, k], i, whole(k, g, i, g))
            x = whole(k, 4, i, 4)
            turned = [x] + [pltpu.roll(x, 32 * rho, 1) for rho in range(1, 4)]
            for f, buf in enumerate((h_buf, u_buf, v_buf, d_buf)):
                y = turned[(3 - f) % 4]
                for q in range(3):
                    y = jnp.where(slot == q, turned[(q - f) % 4], y)
                put(buf.at[k], i, y)

    for i in range(3):
        put(p_buf, i, whole(LV, 4, i, 4).astype(jnp.int32))

    rows = lax.broadcasted_iota(jnp.int32, (24, 128), 0) - 4 + scal[1]
    cor_c = coriolis_of(rows, rows_total)
    d_c = [p_buf[8:32, :]]
    d_e = [jnp.minimum(d_c[0], from_east(d_c)[0])]
    d_n = [jnp.minimum(d_c[0], p_buf[9:33, :])]

    def merge(body, strip, q, j):
        if j == 0:
            return jnp.where(lane < 4, pltpu.roll(strip, (-(32 * q + 4)) % 128, 1), body)
        return jnp.where(lane >= 124, pltpu.roll(strip, (100 - 32 * q) % 128, 1), body)

    def dynamics(k, carry, side):
        up, prev = carry
        read = lambda buf, r: [buf[k, r:r + 24, :]]
        link = read(d_buf, 8)

        def south(fluxes):
            flux[k, 8:32, :] = fluxes[0]
            return read(flux, 7)

        h_new, u_new, v_new, co, ratios = level_step(
            k, read(h_buf, 8), read(h_buf, 9), read(u_buf, 8), read(v_buf, 8), (d_c, d_e, d_n), cor_c, link, up, prev, south)
        h_buf[k, 8:32, :] = h_new[0]
        u_buf[k, 8:32, :] = u_new[0]
        v_buf[k, 8:32, :] = v_new[0]
        for c in range(7):
            coef[side, c, k] = co[0][c]
        return link, ratios

    fresh = (zeros_like_tiles(24, 1), zeros_like_tiles(24, 1))
    lax.fori_loop(0, LV, lambda k, carry: dynamics(k, carry, 1), fresh, unroll=8)
    leaving = []
    for n in range(1, ITERS + 1):
        src, dst = (c_buf, c_alt) if n % 2 else (c_alt, c_buf)
        starts = (8, 16, 24) if n < ITERS else (12, 20)
        tiles = len(starts)

        def down(k, carry):
            before, after = carry
            co = [[coef[n % 2, c, k, r0 - 8:r0, :] for r0 in starts] for c in range(6)]
            read = lambda t, shift: [src[t, k, r0 + shift:r0 + shift + 8, :] for r0 in starts]
            now = forward(co, [(read(t, 0), read(t, -1), read(t, 1)) for t in range(4)], before, joined=False)
            for t in range(4):
                for i in range(tiles):
                    solved[k, t, i] = now[t][i]
            if n < ITERS:
                after = dynamics(k, after, (n + 1) % 2)
            return now, after

        lax.fori_loop(0, LV, down, ([zeros_like_tiles(8, tiles) for _ in range(4)], fresh if n < ITERS else 0), unroll=4)

        if n == ITERS - 1:
            off = scal[0] * (LV // 2)

            @pl.loop(0, LV // 2, unroll=4)
            def _(k):
                for f, buf in enumerate((h_buf, u_buf, v_buf)):
                    for i in range(2):
                        strip = buf[k + off, 12 + 8 * i:20 + 8 * i, :]
                        for j in range(2):
                            turned = pltpu.roll(mid_f[f, k + off, j], 4, 0)
                            outer = edge_f[f, k + off, j]
                            body = jnp.where(low, outer, turned) if i == 0 else jnp.where(low, turned, outer)
                            place_at = (k, slice(8 * i, 8 * i + 8), slice(128 * j, 128 * j + 128))
                            if f == 0:
                                o_h[place_at] = merge(body, strip, 0, j)
                            else:
                                o_v[(f - 1,) + place_at] = merge(body, strip, 0, j)

            leaving += [pltpu.make_async_copy(o_h, out_h, sem.at[8]), pltpu.make_async_copy(o_v, out_v, sem.at[9])]
            for c in leaving:
                c.start()

        def upward(i, m):
            k = LV - 1 - i
            r = [coef[n % 2, 6, k, r0 - 8:r0, :] for r0 in starts]
            m = [[solved[k, t, i] + r[i] * m[t][i] for i in range(tiles)] for t in range(4)]
            for t in range(4):
                for i in range(tiles):
                    mixed[t // 2, pl.ds(pl.multiple_of(8 * tiles * k + 8 * i, 8), 8), 128 * (t % 2):128 * (t % 2) + 128] = m[t][i]
            return m

        lax.fori_loop(0, LV, upward, [zeros_like_tiles(8, tiles) for _ in range(4)], unroll=4)

        size = 8 * tiles * LV // 2
        for s in range(2):
            for half in range(2):
                x = mixed[s, size * half:size * half + size, :]
                high = x.astype(BF16)
                rest = (x - high.astype(F32)).astype(BF16)
                made = jnp.dot(jnp.concatenate([high, rest, high], axis=1), table[s], preferred_element_type=F32)
                for k in range(LV // 2):
                    for i, r0 in enumerate(starts):
                        at = 8 * (tiles * k + i)
                        for go in range(2):
                            dst[2 * s + go, LV // 2 * half + k, r0:r0 + 8, :] = made[at:at + 8, 128 * go:128 * go + 128]

    final = c_buf if ITERS % 2 == 0 else c_alt
    for part in range(8):
        @pl.loop(2 * part, 2 * part + 2, unroll=2)
        def _(k):
            for t in range(NT):
                for i in range(2):
                    strip = final[t // 4, k, 12 + 8 * i:20 + 8 * i, :]
                    for j in range(2):
                        out_c[t, k, 8 * i:8 * i + 8, 128 * j:128 * j + 128] = merge(
                            edge[t, k, j, 8 * i:8 * i + 8, :], strip, t % 4, j)
        levels = pl.ds(2 * part, 2)
        leaving.append(pltpu.make_async_copy(out_c.at[:, levels], out.at[:, levels], sem.at[part]))
        leaving[-1].start()

    for c in leaving:
        c.wait()


def room(mebibytes):
    return pltpu.CompilerParams(vmem_limit_bytes=mebibytes * 1024 * 1024)


def sds(*shape):
    return jax.ShapeDtypeStruct(shape, F32)


def body(tracers, thickness, velocity, diffusivity, reaction, land_mask, level_count):
    rows_local = thickness.shape[1]
    rows_total = rows_local * lax.axis_size("ty")
    set_index = lax.axis_index("set").astype(jnp.int32)
    row_start = lax.axis_index("ty").astype(jnp.int32) * rows_local
    scal = jnp.stack([set_index, row_start])
    swap = [(0, 1), (1, 0)]
    h_pair = lax.ppermute(thickness, "set", swap)
    v_pair = lax.ppermute(velocity, "set", swap)
    field = sds(LV, 2, 32, 128)
    y_shape = sds(161, 2, 8, 128)
    up_part, dn_part, own, r_own, l_own, c_first, kept, table, s_table = pl.pallas_call(
        tracer_pack_kernel,
        out_shape=[y_shape, y_shape, sds(LV, 4, 16, 128), sds(LV, 16, 128), sds(LV, 16, 128), sds(NT, LV, 2, 32, 128),
                   sds(NT, LV, 2, 8, 128), jax.ShapeDtypeStruct((2, 64, 256), BF16), jax.ShapeDtypeStruct((2, 768, 256), BF16)],
        in_specs=[ANY, SMEM], out_specs=[VMEM] * 9,
        scratch_shapes=[pltpu.SemaphoreType.DMA((4,))],
        compiler_params=room(4), name="tracer_pack")(tracers, reaction)
    h_pair, v_pair, up_part, dn_part = lax.optimization_barrier((h_pair, v_pair, up_part, dn_part))
    y_up, y_dn, own_f, h_first, u_first, v_first, d_first, p_first = pl.pallas_call(
        field_pack_kernel, out_shape=[y_shape, y_shape, sds(LV + 1, 16, 128)] + [field] * 4 + [jax.ShapeDtypeStruct((2, 32, 128), jnp.int32)],
        in_specs=[SMEM] + [ANY] * 9, out_specs=[ANY, ANY] + [VMEM] * 6,
        input_output_aliases={8: 0, 9: 1},
        scratch_shapes=[pltpu.VMEM((33, 2, 8, 128), F32), pltpu.VMEM((33, 2, 8, 128), F32),
                        pltpu.VMEM((2, 2, 16, 128), jnp.int32),
                        pltpu.SemaphoreType.DMA((18,)), pltpu.SemaphoreType.DMA((2,))],
        compiler_params=room(4), name="field_pack")(
            scal, thickness, h_pair, velocity, v_pair, diffusivity, land_mask, level_count, up_part, dn_part)
    ty = lax.axis_size("ty")
    north = [(i, i + 1) for i in range(ty - 1)]
    south = [(j, i) for i, j in north]
    y_s = lax.ppermute(y_up, "ty", north)
    y_n = lax.ppermute(y_dn, "ty", south)
    *stages, saved_f, mid, mid_f = pl.pallas_call(
        lambda *a: inner_kernel(rows_total, *a),
        out_shape=[sds(PER, LV, 2, 24, 128)] * (2 * ITERS - 2) + [sds(ITERS - 1, 3, LV, 2, 8, 128), sds(NT, LV, 2, 16, 128), sds(3, LV, 2, 8, 128)],
        in_specs=[SMEM] + [VMEM] * 7, out_specs=[VMEM] * (2 * ITERS + 1),
        scratch_shapes=[pltpu.VMEM((LV, 2, 32, 128), F32)] * 4 + [
            pltpu.VMEM((LV, PER, 2, 8, 128), F32),
            pltpu.VMEM((LV, PER, 2, 8, 128), F32),
            pltpu.VMEM((6, LV, 2, 16, 128), F32),
            pltpu.VMEM((2, LV, 2, 16, 128), F32)],
        compiler_params=room(8), name="inner")(scal, c_first, h_first, u_first, v_first, d_first, p_first, table)
    y_s, y_n, mid_f = lax.optimization_barrier((y_s, y_n, mid_f))
    halo, x_r, x_l = pl.pallas_call(
        halo_pack_kernel, out_shape=[sds(LV + 1, 5, 8, 128), sds(LV + 1, 24, 128), sds(LV + 1, 24, 128)],
        in_specs=[VMEM] * 5, out_specs=[VMEM] * 3,
        compiler_params=room(4), name="halo_pack")(y_s, y_n, own_f, r_own, l_own)
    tx = lax.axis_size("tx")
    east = [(i, (i + 1) % tx) for i in range(tx)]
    west = [(j, i) for i, j in east]
    x_w = lax.ppermute(x_r, "tx", east)
    x_e = lax.ppermute(x_l, "tx", west)
    edge, edge_f = pl.pallas_call(
        lambda *a: edge_kernel(rows_total, *a),
        out_shape=[sds(NT, LV, 2, 16, 128), sds(3, LV, 2, 8, 128)],
        in_specs=[SMEM] + [VMEM] * 17, out_specs=[VMEM] * 2,
        scratch_shapes=[pltpu.VMEM((PER, LV, 2, 16, 128), F32)] * 4 + [
            pltpu.VMEM((ITERS, 3, LV, 2, 16, 128), F32),
            pltpu.VMEM((LV, 2, 32, 128), F32),
            pltpu.VMEM((2, 32, 128), jnp.int32),
            pltpu.VMEM((LV, PER, 2, 8, 128), F32),
            pltpu.VMEM((LV, PER, 2, 8, 128), F32),
            pltpu.VMEM((6, LV, 2, 8, 128), F32),
            pltpu.VMEM((2, LV, 2, 8, 128), F32)],
        compiler_params=room(17), name="edge")(
            scal, kept, *stages, saved_f, h_first, u_first, v_first, y_s, y_n, d_first, p_first, table, mid)
    return pl.pallas_call(
        lambda *a: strip_kernel(rows_total, *a),
        out_shape=[sds(*tracers.shape), sds(*thickness.shape), sds(*velocity.shape)],
        in_specs=[SMEM] + [VMEM] * 9, out_specs=[ANY] * 3,
        scratch_shapes=[
            pltpu.VMEM((4, LV, 40, 128), F32),
            pltpu.VMEM((4, LV, 40, 128), F32),
            pltpu.VMEM((LV, 40, 128), F32),
            pltpu.VMEM((LV, 40, 128), F32),
            pltpu.VMEM((LV, 40, 128), F32),
            pltpu.VMEM((LV, 40, 128), F32),
            pltpu.VMEM((LV, 40, 128), F32),
            pltpu.VMEM((40, 128), jnp.int32),
            pltpu.VMEM((LV, 4, 3, 8, 128), F32),
            pltpu.VMEM((2, 7, LV, 24, 128), F32),
            pltpu.VMEM((2, 24 * LV, 256), F32),
            pltpu.VMEM((NT, LV, 16, 256), F32),
            pltpu.VMEM(thickness.shape, F32),
            pltpu.VMEM(velocity.shape, F32),
            pltpu.SemaphoreType.DMA((10,))],
        compiler_params=room(17), name="strips")(scal, own, own_f, halo, x_w, x_e, s_table, mid_f, edge, edge_f)


def solution(mesh):
    placed = (
        P("set", None, "ty", "tx"),
        P("set", "ty", "tx"),
        P(None, "set", "ty", "tx"),
        P(None, "ty", "tx"),
        P("set", None, None),
        P("ty", "tx"),
        P("ty", "tx"),
    )

    def whole(*args):
        return tuple(body(*args))

    return jax.shard_map(
        whole,
        mesh=mesh,
        in_specs=placed,
        out_specs=(P("set", None, "ty", "tx"), P("set", "ty", "tx"), P(None, "set", "ty", "tx")),
        check_vma=False,
    )
```

```python
import jax
import jax.numpy as jnp
from jax import lax
from jax.experimental import pallas as pl
from jax.experimental.pallas import tpu as pltpu
from jax.sharding import PartitionSpec as P

ITERS = 4
DT = 0.2
G = 1.0
ROTATION = 0.5
LV = 16
NT = 16
PER = 8
F32 = jnp.float32
BF16 = jnp.bfloat16
ANY = pl.BlockSpec(memory_space=pl.ANY)
SMEM = pl.BlockSpec(memory_space=pltpu.SMEM)
VMEM = pl.BlockSpec(memory_space=pltpu.VMEM)


def sub_iota(rows=8):
    return lax.broadcasted_iota(jnp.int32, (rows, 128), 0)


def lane_iota(rows=8):
    return lax.broadcasted_iota(jnp.int32, (rows, 128), 1)


def from_east(tiles, joined=True):
    rolled = [pltpu.roll(x, 127, 1) for x in tiles]
    lane = lane_iota(tiles[0].shape[0])
    last = len(tiles) - 1
    return [rolled[i] if i == last or not joined else jnp.where(lane == 127, rolled[i + 1], rolled[i]) for i in range(last + 1)]


def from_west(tiles, joined=True):
    rolled = [pltpu.roll(x, 1, 1) for x in tiles]
    lane = lane_iota(tiles[0].shape[0])
    return [rolled[i] if i == 0 or not joined else jnp.where(lane == 0, rolled[i - 1], rolled[i]) for i in range(len(tiles))]


def coriolis_of(row, rows_total):
    return ROTATION * (2.0 * (row.astype(F32) + 0.5) / rows_total - 1.0)


def level_step(k, h_c, h_n, u_c, v_c, deep, cor_c, link, up, prev, south):
    d_c, d_e, d_n = deep
    h_e = from_east(h_c)
    count = len(h_c)
    u_new, v_new, u_flux, v_flux = [], [], [], []
    for j in range(count):
        un = jnp.where(k < d_e[j], u_c[j] + DT * (cor_c * v_c[j] - G * (h_e[j] - h_c[j])), 0.0)
        vn = jnp.where(k < d_n[j], v_c[j] - DT * (cor_c * u_c[j] + G * (h_n[j] - h_c[j])), 0.0)
        u_new.append(un)
        v_new.append(vn)
        u_flux.append(un * 0.5 * (h_c[j] + h_e[j]))
        v_flux.append(vn * 0.5 * (h_c[j] + h_n[j]))
    w_flux = from_west(u_flux)
    s_flux = south(v_flux)
    h_new, coefs, ratios = [], [], []
    for j in range(count):
        fe, fw, fn, fs = u_flux[j], w_flux[j], v_flux[j], s_flux[j]
        hn = h_c[j] - DT * ((fe - fw) + (fn - fs))
        q = jnp.where(k < d_c[j], 1.0 / (hn + up[j] + link[j] - up[j] * prev[j]), 0.0)
        r = link[j] * q
        dq = DT * q
        ce = dq * jnp.maximum(-fe, 0.0)
        cw = dq * jnp.maximum(fw, 0.0)
        cn = dq * jnp.maximum(-fn, 0.0)
        cs = dq * jnp.maximum(fs, 0.0)
        out = (jnp.maximum(fe, 0.0) - jnp.minimum(fw, 0.0)) + (jnp.maximum(fn, 0.0) - jnp.minimum(fs, 0.0))
        ca = q * h_c[j] - dq * out
        h_new.append(hn)
        ratios.append(r)
        coefs.append((ca, ce, cw, cn, cs, up[j] * q, r))
    return h_new, u_new, v_new, coefs, ratios


def forward(coefs, cells, before, joined=True):
    result = []
    for t, (c, s, n) in enumerate(cells):
        e = from_east(c, joined)
        w = from_west(c, joined)
        result.append([
            ((coefs[0][j] * c[j] + coefs[1][j] * e[j]) + (coefs[2][j] * w[j] + coefs[3][j] * n[j]))
            + (coefs[4][j] * s[j] + coefs[5][j] * before[t][j])
            for j in range(len(c))
        ])
    return result


def react(weights, m):
    x = jnp.concatenate([jnp.concatenate([m[t][j] for t in range(PER)], axis=0) for j in range(2)], axis=1)
    high = x.astype(BF16)
    rest = (x - high.astype(F32)).astype(BF16)
    parts = jnp.concatenate([high, rest, high], axis=0)
    out = jnp.dot(weights[:, :192], parts, preferred_element_type=F32)
    return [[out[8 * t:8 * t + 8, 128 * j:128 * j + 128] for j in range(2)] for t in range(PER)]


def sweep(down, upward, unroll=8):
    def step(i, carry):
        before, m = carry
        if down is not None:
            before = down(i, before)
        if upward is not None:
            m = upward(LV - 1 - i, m)
        return before, m

    start = [zeros_like_tiles(8, 2) for _ in range(PER)]
    lax.fori_loop(0, LV, step, (start if down is not None else 0, start if upward is not None else 0), unroll=unroll)


def zeros_like_tiles(rows, count):
    return [jnp.zeros((rows, 128), F32) for _ in range(count)]


def pack_lanes(sources):
    lane = lane_iota()
    place, slot = lane & 31, lane >> 5
    acc = None
    for q, (left, right) in enumerate(sources):
        a = pltpu.roll(left, (4 + 32 * q) % 128, 1)
        b = pltpu.roll(right, (28 + 32 * q) % 128, 1)
        x = jnp.where(place < 16, a, b)
        acc = x if acc is None else jnp.where(slot == q, x, acc)
    return acc


def to_east(packed, g):
    return pltpu.roll(packed, (4 * g - 24) % 128, 1)


def to_west(packed, g):
    return pltpu.roll(packed, (4 * g - 4) % 128, 1)


def tracer_pack_kernel(tr, reaction, y_up, y_dn, own, x_r, x_l, c_buf, kept, table, s_table, sem):
    copies = [pltpu.make_async_copy(
        tr.at[pl.ds(8 * s, 8), :, :, pl.ds(128 * j, 128)],
        c_buf.at[pl.ds(8 * s, 8), :, j, pl.ds(8, 16), :], sem.at[2 * s + j]) for s in range(2) for j in range(2)]
    for c in copies:
        c.start()
    low = sub_iota() < 4
    place = lane_iota() & 31
    same = (lane_iota() & 7) == sub_iota()
    column = (lane_iota() >> 3) & 7
    for s in range(2):
        blocks = []
        for a in range(PER):
            v = jnp.zeros((8, 128), F32)
            for b in range(PER):
                w = DT * reaction[s, a, b] + (1.0 if a == b else 0.0)
                v = jnp.where(same & (column == b), jnp.full((8, 128), w, F32), v)
            blocks.append(v)
        v = jnp.concatenate(blocks, axis=0)
        high = v.astype(BF16)
        table[s, :, 0:128] = high
        table[s, :, 128:256] = (v - high.astype(F32)).astype(BF16)
    slot = lane_iota() >> 5
    for s in range(2):
        for b in range(PER):
            spread = []
            for go in range(2):
                v = jnp.zeros((8, 128), F32)
                for q in range(4):
                    a = 4 * go + q
                    w = DT * reaction[s, a, b] + (1.0 if a == b else 0.0)
                    v = jnp.where(slot == q, jnp.full((8, 128), w, F32), v)
                spread.append(v)
            for go in range(2):
                tiles = [jnp.where((lane_iota() & 31) == sub_iota() + 8 * r, spread[go], 0.0) for r in range(4)]
                v = jnp.concatenate(tiles, axis=0)
                high = v.astype(BF16)
                lanes = slice(128 * go, 128 * go + 128)
                s_table[s, 32 * b:32 * b + 32, lanes] = high
                s_table[s, 256 + 32 * b:288 + 32 * b, lanes] = high
                s_table[s, 512 + 32 * b:544 + 32 * b, lanes] = (v - high.astype(F32)).astype(BF16)
    for c in copies:
        c.wait()

    @pl.loop(0, LV, unroll=2)
    def _(k):
        for j in range(2):
            for t in range(PER):
                read = lambda b, r: c_buf[t + b, k, j, r:r + 8, :]
                y_up[t * LV + k, j] = jnp.where(low, read(0, 20), read(PER, 16))
                y_dn[t * LV + k, j] = jnp.where(low, read(0, 8), read(PER, 4))
            for t in range(NT):
                c_buf[t, k, j, 0:8, :] = jnp.zeros((8, 128), F32)
                c_buf[t, k, j, 24:32, :] = jnp.zeros((8, 128), F32)
                kept[t, k, j] = keep_rows(0, lambda r: c_buf[t, k, j, r:r + 8, :])
        for i in range(2):
            rows = slice(8 * i, 8 * i + 8)
            xr, xl = None, None
            for g in range(4):
                packed = pack_lanes([[c_buf[4 * g + q, k, j, 8 + 8 * i:16 + 8 * i, :] for j in range(2)] for q in range(4)])
                own[k, g, rows, :] = packed
                here = place >= 4 * g
                xr = to_east(packed, g) if g == 0 else jnp.where(here, to_east(packed, g), xr)
                xl = to_west(packed, g) if g == 0 else jnp.where(here, to_west(packed, g), xl)
            x_r[k, rows, :] = xr
            x_l[k, rows, :] = xl


def keep_rows(n, read):
    return jnp.where(sub_iota() < 6, read(4 + n), read(16 - n))


def field_pack_kernel(scal, ho, hp, vo, vp, df, land, level, up_in, dn_in, y_up, y_dn, own, h_buf, u_buf, v_buf, d_buf, p_buf,
                      f_up, f_dn, l_buf, sem, out_sem):
    off = scal[0] * (LV // 2)
    part = LV // 2
    rows = pl.ds(8, 16)
    copies = []
    for j in range(2):
        lanes = pl.ds(128 * j, 128)
        for i, (h, v, at) in enumerate(((ho, vo, off), (hp, vp, part - off))):
            levels = pl.ds(at, part)
            copies.append(pltpu.make_async_copy(h.at[:, :, lanes], h_buf.at[levels, j, rows, :], sem.at[6 * j + 3 * i]))
            copies.append(pltpu.make_async_copy(v.at[0, :, :, lanes], u_buf.at[levels, j, rows, :], sem.at[6 * j + 3 * i + 1]))
            copies.append(pltpu.make_async_copy(v.at[1, :, :, lanes], v_buf.at[levels, j, rows, :], sem.at[6 * j + 3 * i + 2]))
        copies.append(pltpu.make_async_copy(df.at[:, :, lanes], d_buf.at[:, j, rows, :], sem.at[12 + j]))
        copies.append(pltpu.make_async_copy(land.at[:, lanes], l_buf.at[0, j], sem.at[14 + j]))
        copies.append(pltpu.make_async_copy(level.at[:, lanes], l_buf.at[1, j], sem.at[16 + j]))
    for c in copies:
        c.start()
    low = sub_iota() < 4
    for c in copies:
        c.wait()

    for j in range(2):
        p_buf[j, 0:8, :] = jnp.zeros((8, 128), jnp.int32)
        p_buf[j, 8:24, :] = jnp.where(l_buf[0, j] == 1, l_buf[1, j], 0)
        p_buf[j, 24:32, :] = jnp.zeros((8, 128), jnp.int32)

    @pl.loop(0, LV, unroll=4)
    def _(k):
        for j in range(2):
            h_buf[k, j, 24:32, :] = jnp.zeros((8, 128), F32)
            d_buf[k, j, 8:24, :] = jnp.where(k + 1 < p_buf[j, 8:24, :], DT * d_buf[k, j, 8:24, :], 0.0)

    def put(index, j, first, second):
        f_up[index, j] = jnp.where(low, first(20), second(16))
        f_dn[index, j] = jnp.where(low, first(8), second(4))

    @pl.loop(0, LV, unroll=4)
    def _(k):
        for j in range(2):
            put(k, j, lambda r: h_buf[k, j, r:r + 8, :], lambda r: u_buf[k, j, r:r + 8, :])
            put(16 + k, j, lambda r: v_buf[k, j, r:r + 8, :], lambda r: d_buf[k, j, r:r + 8, :])

    for j in range(2):
        get = lambda r: p_buf[j, r:r + 8, :].astype(F32)
        put(32, j, get, get)
    leaving = [pltpu.make_async_copy(f, y.at[pl.ds(128, 33)], out_sem.at[i]) for i, (f, y) in enumerate(((f_up, y_up), (f_dn, y_dn)))]
    for c in leaving:
        c.start()

    @pl.loop(0, LV, unroll=4)
    def _(k):
        for i in range(2):
            own[k, 8 * i:8 * i + 8, :] = pack_lanes(
                [[buf[k, j, 8 + 8 * i:16 + 8 * i, :] for j in range(2)] for buf in (h_buf, u_buf, v_buf, d_buf)])

    for i in range(2):
        own[LV, 8 * i:8 * i + 8, :] = pack_lanes([[p_buf[j, 8 + 8 * i:16 + 8 * i, :].astype(F32) for j in range(2)]] * 4)
    for c in leaving:
        c.wait()


def inner_kernel(rows_total, scal, c_first, h_first, u_first, v_first, d_buf, p_buf, table, saved, saved_f, mid, mid_f,
                 h_buf, u_buf, v_buf, flux, one_a, one_b, two_a, two_b, solved_a, solved_b, coef, ratio):
    rows = lax.broadcasted_iota(jnp.int32, (16, 128), 0) + scal[1]
    cor_c = coriolis_of(rows, rows_total)
    d_c = [p_buf[j, 8:24, :] for j in range(2)]
    d_e = [jnp.minimum(a, b) for a, b in zip(d_c, from_east(d_c))]
    d_n = [jnp.minimum(d_c[j], p_buf[j, 9:25, :]) for j in range(2)]
    c_one, c_two = (one_a, one_b), (two_a, two_b)
    buffers = ((c_first.at[pl.ds(0, PER)], c_first.at[pl.ds(PER, PER)]), c_one, c_two, c_one, None)
    solved = (solved_a, solved_b)
    pending, keep, slot = None, None, 0
    for n in range(1, ITERS + 1):
        src, dst = buffers[n - 1], buffers[n]
        old = (h_first, u_first, v_first) if n == 1 else (h_buf, u_buf, v_buf)

        def dynamics(k, carry):
            up, prev = carry
            read = lambda buf, r: [buf[k, j, r:r + 16, :] for j in range(2)]
            link = read(d_buf, 8)

            def south(fluxes):
                for j in range(2):
                    if n == 1:
                        flux[k, j, 0:8, :] = jnp.zeros((8, 128), F32)
                        h_buf[k, j, 24:32, :] = jnp.zeros((8, 128), F32)
                    flux[k, j, 8:24, :] = fluxes[j]
                return read(flux, 7)

            h_new, u_new, v_new, co, ratios = level_step(
                k, read(old[0], 8), read(old[0], 9), read(old[1], 8), read(old[2], 8), (d_c, d_e, d_n), cor_c, link, up, prev, south)
            for j in range(2):
                h_buf[k, j, 8:24, :] = h_new[j]
                u_buf[k, j, 8:24, :] = u_new[j]
                v_buf[k, j, 8:24, :] = v_new[j]
                for c in range(6):
                    coef[c, k, j] = co[j][c]
                ratio[n % 2, k, j] = co[j][6]
            return link, ratios

        lax.fori_loop(0, LV, dynamics, (zeros_like_tiles(16, 2), zeros_like_tiles(16, 2)), unroll=4)

        @pl.loop(0, LV, unroll=4)
        def _(k):
            for f, buf in enumerate((h_buf, u_buf, v_buf)):
                for j in range(2):
                    if n < ITERS:
                        saved_f[n - 1, f, k, j] = keep_rows(n, lambda r: buf[k, j, r:r + 8, :])
                    else:
                        mid_f[f, k, j] = buf[k, j, 12:20, :]

        for s in range(2):
            for r0 in ((8, 16) if n < ITERS else (12,)):
                def down(k, before, s=s, r0=r0, src=src, slot=slot):
                    co = [[coef[c, k, j, r0 - 8:r0, :] for j in range(2)] for c in range(6)]
                    read = lambda t, r: [src[s][t, k, j, r:r + 8, :] for j in range(2)]
                    now = forward(co, [(read(t, r0), read(t, r0 - 1), read(t, r0 + 1)) for t in range(PER)], before)
                    for t in range(PER):
                        for j in range(2):
                            solved[slot][k, t, j] = now[t][j]
                    return now

                def upward(k, m, s=s, r0=r0, dst=dst, slot=slot, n=n):
                    r = [ratio[n % 2, k, j, r0 - 8:r0, :] for j in range(2)]
                    m = [[solved[slot][k, t, j] + r[j] * m[t][j] for j in range(2)] for t in range(PER)]
                    outs = react(table[s], m)
                    for t in range(PER):
                        for j in range(2):
                            if n < ITERS:
                                dst[s][t, k, j, r0:r0 + 8, :] = outs[t][j]
                                if n < 3:
                                    beyond = 0 if r0 == 8 else 24
                                    dst[s][t, k, j, beyond:beyond + 8, :] = jnp.zeros((8, 128), F32)
                            else:
                                mid[s * PER + t, k, j, 4:12, :] = outs[t][j]
                    return m

                sweep(down, pending)
                pending = upward
                slot = 1 - slot
                if keep is not None:
                    keep()
                    keep = None

        def keep(n=n, dst=dst):
            @pl.loop(0, LV, unroll=2)
            def _(k):
                for t in range(NT):
                    for j in range(2):
                        saved[n - 1, t, k, j] = keep_rows(n, lambda r: dst[t // PER][t % PER, k, j, r:r + 8, :])

    sweep(None, pending)


def halo_pack_kernel(y_s, y_n, own_f, r_own, l_own, halo, x_r, x_l):
    low = sub_iota() < 4
    place = lane_iota() & 31
    for i in range(2):
        rows = slice(8 * i, 8 * i + 8)
        x_r[LV, rows, :] = to_east(own_f[LV, rows, :], 4)
        x_l[LV, rows, :] = to_west(own_f[LV, rows, :], 4)

    @pl.loop(0, LV, unroll=4)
    def _(k):
        for i in range(2):
            rows = slice(8 * i, 8 * i + 8)
            x_r[k, rows, :] = jnp.where(place >= 16, to_east(own_f[k, rows, :], 4), r_own[k, rows, :])
            x_l[k, rows, :] = jnp.where(place >= 16, to_west(own_f[k, rows, :], 4), l_own[k, rows, :])

    def pair(index, j):
        ys, yn = y_s[index, j], y_n[index, j]
        return jnp.where(low, ys, pltpu.roll(yn, 4, 0)), jnp.where(low, pltpu.roll(ys, 4, 0), yn)

    @pl.loop(0, LV, unroll=2)
    def _(k):
        pairs = [[pair(t * LV + k, j) for j in range(2)] for t in range(PER)]
        hu = [pair(128 + k, j) for j in range(2)]
        vd = [pair(144 + k, j) for j in range(2)]
        groups = [[[pairs[4 * (g % 2) + q][j][g // 2] for j in range(2)] for q in range(4)] for g in range(4)]
        groups.append([[x[j][w] for j in range(2)] for x in (hu, vd) for w in range(2)])
        xr, xl = None, None
        for g in range(5):
            packed = pack_lanes(groups[g])
            halo[k, g] = packed
            here = place >= 4 * g
            xr = to_east(packed, g) if g == 0 else jnp.where(here, to_east(packed, g), xr)
            xl = to_west(packed, g) if g == 0 else jnp.where(here, to_west(packed, g), xl)
        x_r[k, 16:24, :] = xr
        x_l[k, 16:24, :] = xl

    packed = pack_lanes([[pair(160, j)[0] for j in range(2)]] * 4)
    for g in range(5):
        halo[LV, g] = packed
    x_r[LV, 16:24, :] = to_east(packed, 4)
    x_l[LV, 16:24, :] = to_west(packed, 4)


def edge_kernel(rows_total, scal, kept, saved, saved_f, h_first, u_first, v_first, y_s, y_n, d_first, p_first, table, mid,
                out_c, out_f, *scratch):
    c_buf = [scratch[2 * n:2 * n + 2] for n in range(ITERS)]
    f_buf, d_buf, p_buf, solved_a, solved_b, coef, ratio = scratch[2 * ITERS:]
    solved = (solved_a, solved_b)
    sub = sub_iota()
    low = sub < 4
    high = jnp.logical_not(low)

    def put(ref, inside, ys, yn, half):
        south = ys if half == 0 else pltpu.roll(ys, 4, 0)
        north = yn if half == 1 else pltpu.roll(yn, 4, 0)
        ref[0:8, :] = jnp.where(low, south, inside)
        pltpu.store(ref.at[pl.ds(4, 8), :], north, mask=high)

    @pl.loop(0, LV, unroll=2)
    def _(k):
        for j in range(2):
            for t in range(PER):
                ys, yn = y_s[t * LV + k, j], y_n[t * LV + k, j]
                for half in range(2):
                    put(c_buf[0][half].at[t, k, j], kept[t + PER * half, k, j], ys, yn, half)
            for f, (buf, index, half) in enumerate(((h_first, 128, 0), (u_first, 128, 1), (v_first, 144, 0))):
                inside = keep_rows(0, lambda r: buf[k, j, r:r + 8, :])
                put(f_buf.at[0, f, k, j], inside, y_s[index + k, j], y_n[index + k, j], half)
            ys, yn = y_s[144 + k, j], y_n[144 + k, j]
            d_buf[k, j, 0:8, :] = ys
            d_buf[k, j, 8:16, :] = d_first[k, j, 8:16, :]
            d_buf[k, j, 16:24, :] = d_first[k, j, 16:24, :]
            d_buf[k, j, 24:32, :] = pltpu.roll(yn, 4, 0)

    for j in range(2):
        p_buf[j, 0:8, :] = y_s[160, j].astype(jnp.int32)
        p_buf[j, 8:24, :] = p_first[j, 8:24, :]
        p_buf[j, 24:32, :] = y_n[160, j].astype(jnp.int32)

    def gather(read, shift):
        return jnp.where(low, read(shift), read(shift + 2))

    pending, slot = None, 0
    for n in range(1, ITERS + 1):
        def at(buf, j, shift):
            return jnp.where(low, buf[j, 4 + n + shift:12 + n + shift, :], buf[j, 20 - n + shift:28 - n + shift, :])

        row = jnp.where(low, sub - 4 + n, sub + 12 - n) + scal[1]
        cor_c = coriolis_of(row, rows_total)
        cor_s = coriolis_of(row - 1, rows_total)
        d_c = [at(p_buf, j, 0) for j in range(2)]
        d_e = [jnp.minimum(a, b) for a, b in zip(d_c, from_east(d_c))]
        d_n = [jnp.minimum(d_c[j], at(p_buf, j, 1)) for j in range(2)]
        d_s = [jnp.minimum(d_c[j], at(p_buf, j, -1)) for j in range(2)]

        def dynamics(k, carry):
            up, prev = carry
            read = lambda f, shift: [gather(lambda r: f_buf[n - 1, f, k, j, r:r + 8, :], shift) for j in range(2)]
            link = [at(d_buf.at[k], j, 0) for j in range(2)]
            h_c = read(0, 1)

            def south(_):
                h_s, u_s, v_s = read(0, 0), read(1, 0), read(2, 0)
                return [jnp.where(k < d_s[j], v_s[j] - DT * (cor_s * u_s[j] + G * (h_c[j] - h_s[j])), 0.0)
                        * 0.5 * (h_s[j] + h_c[j]) for j in range(2)]

            h_new, u_new, v_new, co, ratios = level_step(
                k, h_c, read(0, 2), read(1, 1), read(2, 1), (d_c, d_e, d_n), cor_c, link, up, prev, south)
            for j in range(2):
                for f, x in enumerate((h_new[j], u_new[j], v_new[j])):
                    if n < ITERS:
                        f_buf[n, f, k, j, 0:8, :] = jnp.where(low, x, saved_f[n - 1, f, k, j])
                        pltpu.store(f_buf.at[n, f, k, j, pl.ds(4, 8), :], x, mask=jnp.logical_not(low))
                    else:
                        out_f[f, k, j] = x
                for c in range(6):
                    coef[c, k, j] = co[j][c]
                ratio[n % 2, k, j] = co[j][6]
            return link, ratios

        lax.fori_loop(0, LV, dynamics, (zeros_like_tiles(8, 2), zeros_like_tiles(8, 2)), unroll=8)

        for s in range(2):
            def down(k, before, s=s, n=n, slot=slot):
                co = [[coef[c, k, j] for j in range(2)] for c in range(6)]

                def read(t, shift):
                    return [gather(lambda r: c_buf[n - 1][s][t, k, j, r:r + 8, :], shift) for j in range(2)]

                now = forward(co, [(read(t, 1), read(t, 0), read(t, 2)) for t in range(PER)], before)
                for t in range(PER):
                    for j in range(2):
                        solved[slot][k, t, j] = now[t][j]
                return now

            def upward(k, m, s=s, n=n, slot=slot):
                r = [ratio[n % 2, k, j] for j in range(2)]
                m = [[solved[slot][k, t, j] + r[j] * m[t][j] for j in range(2)] for t in range(PER)]
                outs = react(table[s], m)
                for t in range(PER):
                    for j in range(2):
                        if n < ITERS:
                            c_buf[n][s][t, k, j, 0:8, :] = jnp.where(low, outs[t][j], saved[n - 1, s * PER + t, k, j])
                            pltpu.store(c_buf[n][s].at[t, k, j, pl.ds(4, 8), :], outs[t][j], mask=high)
                        else:
                            inside = mid.at[s * PER + t, k, j]
                            out_c[s * PER + t, k, j, 0:8, :] = jnp.where(low, outs[t][j], inside[0:8, :])
                            out_c[s * PER + t, k, j, 8:16, :] = jnp.where(low, inside[8:16, :], outs[t][j])
                return m

            sweep(down, pending)
            pending = upward
            slot = 1 - slot

    sweep(None, pending)


def strip_kernel(rows_total, scal, own, own_f, halo, x_w, x_e, table, mid_f, edge, edge_f, out, out_h, out_v,
                 c_buf, c_alt, h_buf, u_buf, v_buf, flux, d_buf, p_buf, solved, coef, mixed, out_c, o_h, o_v, sem):
    lane = lane_iota()
    place = lane & 31
    slot = lane >> 5
    low = sub_iota() < 4

    def whole(k, g, i, xg):
        rows = slice(8 * i, 8 * i + 8)
        a = pltpu.roll(x_w[k, rows, :], (-4 * xg) % 128, 1)
        b = pltpu.roll(x_e[k, rows, :], (28 - 4 * xg) % 128, 1)
        if i == 2:
            body = halo[k, g]
        elif g == 4:
            body = own_f[k, rows, :]
        else:
            body = own[k, g, rows, :]
        return jnp.where(place < 4, a, jnp.where(place >= 28, b, body))

    def put(ref, i, x):
        if i < 2:
            ref[12 + 8 * i:20 + 8 * i, :] = x
        else:
            pltpu.store(ref.at[pl.ds(8, 8), :], x, mask=low)
            pltpu.store(ref.at[pl.ds(24, 8), :], x, mask=jnp.logical_not(low))

    @pl.loop(0, LV, unroll=4)
    def _(k):
        for i in range(3):
            for g in range(4):
                put(c_buf.at[g, k], i, whole(k, g, i, g))
            x = whole(k, 4, i, 4)
            turned = [x] + [pltpu.roll(x, 32 * rho, 1) for rho in range(1, 4)]
            for f, buf in enumerate((h_buf, u_buf, v_buf, d_buf)):
                y = turned[(3 - f) % 4]
                for q in range(3):
                    y = jnp.where(slot == q, turned[(q - f) % 4], y)
                put(buf.at[k], i, y)

        for buf in [c_buf.at[g] for g in range(4)] + [c_alt.at[g] for g in range(4)] + [h_buf, flux]:
            buf[k, 0:8, :] = jnp.zeros((8, 128), F32)
            buf[k, 32:40, :] = jnp.zeros((8, 128), F32)

    for i in range(3):
        put(p_buf, i, whole(LV, 4, i, 4).astype(jnp.int32))
    p_buf[32:40, :] = jnp.zeros((8, 128), jnp.int32)

    rows = lax.broadcasted_iota(jnp.int32, (24, 128), 0) - 4 + scal[1]
    cor_c = coriolis_of(rows, rows_total)
    d_c = [p_buf[8:32, :]]
    d_e = [jnp.minimum(d_c[0], from_east(d_c)[0])]
    d_n = [jnp.minimum(d_c[0], p_buf[9:33, :])]

    def merge(body, strip, q, j):
        if j == 0:
            return jnp.where(lane < 4, pltpu.roll(strip, (-(32 * q + 4)) % 128, 1), body)
        return jnp.where(lane >= 124, pltpu.roll(strip, (100 - 32 * q) % 128, 1), body)

    def dynamics(k, carry, side):
        up, prev = carry
        read = lambda buf, r: [buf[k, r:r + 24, :]]
        link = read(d_buf, 8)

        def south(fluxes):
            flux[k, 8:32, :] = fluxes[0]
            return read(flux, 7)

        h_new, u_new, v_new, co, ratios = level_step(
            k, read(h_buf, 8), read(h_buf, 9), read(u_buf, 8), read(v_buf, 8), (d_c, d_e, d_n), cor_c, link, up, prev, south)
        h_buf[k, 8:32, :] = h_new[0]
        u_buf[k, 8:32, :] = u_new[0]
        v_buf[k, 8:32, :] = v_new[0]
        for c in range(7):
            coef[side, c, k] = co[0][c]
        return link, ratios

    fresh = (zeros_like_tiles(24, 1), zeros_like_tiles(24, 1))
    lax.fori_loop(0, LV, lambda k, carry: dynamics(k, carry, 1), fresh, unroll=8)
    leaving = []
    for n in range(1, ITERS + 1):
        src, dst = (c_buf, c_alt) if n % 2 else (c_alt, c_buf)
        starts = (8, 16, 24) if n < ITERS else (12, 20)
        tiles = len(starts)

        def down(k, carry):
            before, after = carry
            co = [[coef[n % 2, c, k, r0 - 8:r0, :] for r0 in starts] for c in range(6)]
            read = lambda t, shift: [src[t, k, r0 + shift:r0 + shift + 8, :] for r0 in starts]
            now = forward(co, [(read(t, 0), read(t, -1), read(t, 1)) for t in range(4)], before, joined=False)
            for t in range(4):
                for i in range(tiles):
                    solved[k, t, i] = now[t][i]
            if n < ITERS:
                after = dynamics(k, after, (n + 1) % 2)
            return now, after

        lax.fori_loop(0, LV, down, ([zeros_like_tiles(8, tiles) for _ in range(4)], fresh if n < ITERS else 0), unroll=4)

        if n == ITERS - 1:
            off = scal[0] * (LV // 2)

            @pl.loop(0, LV // 2, unroll=4)
            def _(k):
                for f, buf in enumerate((h_buf, u_buf, v_buf)):
                    for i in range(2):
                        strip = buf[k + off, 12 + 8 * i:20 + 8 * i, :]
                        for j in range(2):
                            turned = pltpu.roll(mid_f[f, k + off, j], 4, 0)
                            outer = edge_f[f, k + off, j]
                            body = jnp.where(low, outer, turned) if i == 0 else jnp.where(low, turned, outer)
                            place_at = (k, slice(8 * i, 8 * i + 8), slice(128 * j, 128 * j + 128))
                            if f == 0:
                                o_h[place_at] = merge(body, strip, 0, j)
                            else:
                                o_v[(f - 1,) + place_at] = merge(body, strip, 0, j)

            leaving += [pltpu.make_async_copy(o_h, out_h, sem.at[8]), pltpu.make_async_copy(o_v, out_v, sem.at[9])]
            for c in leaving:
                c.start()

        def upward(i, m):
            k = LV - 1 - i
            r = [coef[n % 2, 6, k, r0 - 8:r0, :] for r0 in starts]
            m = [[solved[k, t, i] + r[i] * m[t][i] for i in range(tiles)] for t in range(4)]
            for t in range(4):
                for i in range(tiles):
                    mixed[t // 2, pl.ds(pl.multiple_of(8 * tiles * k + 8 * i, 8), 8), 128 * (t % 2):128 * (t % 2) + 128] = m[t][i]
            return m

        lax.fori_loop(0, LV, upward, [zeros_like_tiles(8, tiles) for _ in range(4)], unroll=4)

        size = 8 * tiles * LV // 2
        for s in range(2):
            for half in range(2):
                x = mixed[s, size * half:size * half + size, :]
                high = x.astype(BF16)
                rest = (x - high.astype(F32)).astype(BF16)
                made = jnp.dot(jnp.concatenate([high, rest, high], axis=1), table[s], preferred_element_type=F32)
                for k in range(LV // 2):
                    for i, r0 in enumerate(starts):
                        at = 8 * (tiles * k + i)
                        for go in range(2):
                            dst[2 * s + go, LV // 2 * half + k, r0:r0 + 8, :] = made[at:at + 8, 128 * go:128 * go + 128]

    final = c_buf if ITERS % 2 == 0 else c_alt
    for part in range(8):
        @pl.loop(2 * part, 2 * part + 2, unroll=2)
        def _(k):
            for t in range(NT):
                for i in range(2):
                    strip = final[t // 4, k, 12 + 8 * i:20 + 8 * i, :]
                    for j in range(2):
                        out_c[t, k, 8 * i:8 * i + 8, 128 * j:128 * j + 128] = merge(
                            edge[t, k, j, 8 * i:8 * i + 8, :], strip, t % 4, j)
        levels = pl.ds(2 * part, 2)
        leaving.append(pltpu.make_async_copy(out_c.at[:, levels], out.at[:, levels], sem.at[part]))
        leaving[-1].start()

    for c in leaving:
        c.wait()


def room(mebibytes):
    return pltpu.CompilerParams(vmem_limit_bytes=mebibytes * 1024 * 1024)


def sds(*shape):
    return jax.ShapeDtypeStruct(shape, F32)


def body(tracers, thickness, velocity, diffusivity, reaction, land_mask, level_count):
    rows_local = thickness.shape[1]
    rows_total = rows_local * lax.axis_size("ty")
    set_index = lax.axis_index("set").astype(jnp.int32)
    row_start = lax.axis_index("ty").astype(jnp.int32) * rows_local
    scal = jnp.stack([set_index, row_start])
    swap = [(0, 1), (1, 0)]
    h_pair = lax.ppermute(thickness, "set", swap)
    v_pair = lax.ppermute(velocity, "set", swap)
    field = sds(LV, 2, 32, 128)
    y_shape = sds(161, 2, 8, 128)
    up_part, dn_part, own, r_own, l_own, c_first, kept, table, s_table = pl.pallas_call(
        tracer_pack_kernel,
        out_shape=[y_shape, y_shape, sds(LV, 4, 16, 128), sds(LV, 16, 128), sds(LV, 16, 128), sds(NT, LV, 2, 32, 128),
                   sds(NT, LV, 2, 8, 128), jax.ShapeDtypeStruct((2, 64, 256), BF16), jax.ShapeDtypeStruct((2, 768, 256), BF16)],
        in_specs=[ANY, SMEM], out_specs=[VMEM] * 9,
        scratch_shapes=[pltpu.SemaphoreType.DMA((4,))],
        compiler_params=room(4), name="tracer_pack")(tracers, reaction)
    h_pair, v_pair, up_part, dn_part = lax.optimization_barrier((h_pair, v_pair, up_part, dn_part))
    y_up, y_dn, own_f, h_first, u_first, v_first, d_first, p_first = pl.pallas_call(
        field_pack_kernel, out_shape=[y_shape, y_shape, sds(LV + 1, 16, 128)] + [field] * 4 + [jax.ShapeDtypeStruct((2, 32, 128), jnp.int32)],
        in_specs=[SMEM] + [ANY] * 9, out_specs=[ANY, ANY] + [VMEM] * 6,
        input_output_aliases={8: 0, 9: 1},
        scratch_shapes=[pltpu.VMEM((33, 2, 8, 128), F32), pltpu.VMEM((33, 2, 8, 128), F32),
                        pltpu.VMEM((2, 2, 16, 128), jnp.int32),
                        pltpu.SemaphoreType.DMA((18,)), pltpu.SemaphoreType.DMA((2,))],
        compiler_params=room(4), name="field_pack")(
            scal, thickness, h_pair, velocity, v_pair, diffusivity, land_mask, level_count, up_part, dn_part)
    ty = lax.axis_size("ty")
    north = [(i, i + 1) for i in range(ty - 1)]
    south = [(j, i) for i, j in north]
    y_s = lax.ppermute(y_up, "ty", north)
    y_n = lax.ppermute(y_dn, "ty", south)
    saved, saved_f, mid, mid_f = pl.pallas_call(
        lambda *a: inner_kernel(rows_total, *a),
        out_shape=[sds(ITERS - 1, NT, LV, 2, 8, 128), sds(ITERS - 1, 3, LV, 2, 8, 128), sds(NT, LV, 2, 16, 128), sds(3, LV, 2, 8, 128)],
        in_specs=[SMEM] + [VMEM] * 7, out_specs=[VMEM] * 4,
        scratch_shapes=[pltpu.VMEM((LV, 2, 32, 128), F32)] * 4 + [
            pltpu.VMEM((PER, LV, 2, 32, 128), F32)] * 4 + [
            pltpu.VMEM((LV, PER, 2, 8, 128), F32),
            pltpu.VMEM((LV, PER, 2, 8, 128), F32),
            pltpu.VMEM((6, LV, 2, 16, 128), F32),
            pltpu.VMEM((2, LV, 2, 16, 128), F32)],
        compiler_params=room(26), name="inner")(scal, c_first, h_first, u_first, v_first, d_first, p_first, table)
    y_s, y_n, mid_f = lax.optimization_barrier((y_s, y_n, mid_f))
    halo, x_r, x_l = pl.pallas_call(
        halo_pack_kernel, out_shape=[sds(LV + 1, 5, 8, 128), sds(LV + 1, 24, 128), sds(LV + 1, 24, 128)],
        in_specs=[VMEM] * 5, out_specs=[VMEM] * 3,
        compiler_params=room(4), name="halo_pack")(y_s, y_n, own_f, r_own, l_own)
    tx = lax.axis_size("tx")
    east = [(i, (i + 1) % tx) for i in range(tx)]
    west = [(j, i) for i, j in east]
    x_w = lax.ppermute(x_r, "tx", east)
    x_e = lax.ppermute(x_l, "tx", west)
    edge, edge_f = pl.pallas_call(
        lambda *a: edge_kernel(rows_total, *a),
        out_shape=[sds(NT, LV, 2, 16, 128), sds(3, LV, 2, 8, 128)],
        in_specs=[SMEM] + [VMEM] * 12, out_specs=[VMEM] * 2,
        scratch_shapes=[pltpu.VMEM((PER, LV, 2, 16, 128), F32)] * (2 * ITERS) + [
            pltpu.VMEM((ITERS, 3, LV, 2, 16, 128), F32),
            pltpu.VMEM((LV, 2, 32, 128), F32),
            pltpu.VMEM((2, 32, 128), jnp.int32),
            pltpu.VMEM((LV, PER, 2, 8, 128), F32),
            pltpu.VMEM((LV, PER, 2, 8, 128), F32),
            pltpu.VMEM((6, LV, 2, 8, 128), F32),
            pltpu.VMEM((2, LV, 2, 8, 128), F32)],
        compiler_params=room(25), name="edge")(
            scal, kept, saved, saved_f, h_first, u_first, v_first, y_s, y_n, d_first, p_first, table, mid)
    return pl.pallas_call(
        lambda *a: strip_kernel(rows_total, *a),
        out_shape=[sds(*tracers.shape), sds(*thickness.shape), sds(*velocity.shape)],
        in_specs=[SMEM] + [VMEM] * 9, out_specs=[ANY] * 3,
        scratch_shapes=[
            pltpu.VMEM((4, LV, 40, 128), F32),
            pltpu.VMEM((4, LV, 40, 128), F32),
            pltpu.VMEM((LV, 40, 128), F32),
            pltpu.VMEM((LV, 40, 128), F32),
            pltpu.VMEM((LV, 40, 128), F32),
            pltpu.VMEM((LV, 40, 128), F32),
            pltpu.VMEM((LV, 40, 128), F32),
            pltpu.VMEM((40, 128), jnp.int32),
            pltpu.VMEM((LV, 4, 3, 8, 128), F32),
            pltpu.VMEM((2, 7, LV, 24, 128), F32),
            pltpu.VMEM((2, 24 * LV, 256), F32),
            pltpu.VMEM((NT, LV, 16, 256), F32),
            pltpu.VMEM(thickness.shape, F32),
            pltpu.VMEM(velocity.shape, F32),
            pltpu.SemaphoreType.DMA((10,))],
        compiler_params=room(17), name="strips")(scal, own, own_f, halo, x_w, x_e, s_table, mid_f, edge, edge_f)


def solution(mesh):
    placed = (
        P("set", None, "ty", "tx"),
        P("set", "ty", "tx"),
        P(None, "set", "ty", "tx"),
        P(None, "ty", "tx"),
        P("set", None, None),
        P("ty", "tx"),
        P("ty", "tx"),
    )

    def whole(*args):
        return tuple(body(*args))

    return jax.shard_map(
        whole,
        mesh=mesh,
        in_specs=placed,
        out_specs=(P("set", None, "ty", "tx"), P("set", "ty", "tx"), P(None, "set", "ty", "tx")),
        check_vma=False,
    )
```
